256 devices in a mesh: dp: 64 (over x_hi, y, z), tensor: 4 (over x_lo, core).
Axes of the slice: x: 4 (x_hi: 2, x_lo: 2; x = x_hi * 2 + x_lo), y: 4, z: 8, core: 2. Of those that a mesh axis runs over, the one named last changes fastest.
Arguments:
- queries: bfloat16 [32768, 4096], P('dp', 'tensor'), may hold values from -64 to 64
- key_proj: bfloat16 [32768, 512], P('dp', 'tensor'), may hold values from -6 to 6
- value_proj: bfloat16 [32768, 512], P('dp', 'tensor'), may hold values from -6 to 6
- out_weight: bfloat16 [4096, 5120], P(None, 'tensor'), may hold values from -0.375 to 0.375
- parents: int32 [128], replicated, may hold values from -1 to 126, as said below
Outputs:
- projected: bfloat16 [32768, 5120], P('dp', 'tensor')
The draws below stay inside these ranges and needn't reach their ends.
Inputs may be any that keep to these rules, and one draw needn't show every extreme that they name: `parents`: the segments form binary trees of depth at most 4; each tree's segments stand in depth-first preorder, so a segment follows its parent and a subtree's segments stand together; the first 5 segments of each tree form a path from its root to depth 4.
All inputs are finite; a program needn't handle non-finite values.
Results may differ from the reference program's by a relative error of at most 0.0053.
Values may be sent and summed in bfloat16 or wider, within the bound.
No kernel may reach another device: no remote copies, remote signals or barrier semaphores. Data moves between devices by JAX's collectives and lax.ppermute only.
A program may use at most 128 MiB of HBM per device.

```python
import jax
import jax.numpy as jnp
import numpy as np
from jax import lax

D = 5120
HEAD_DIM = 128
HEADS = 32
KV_HEADS = 4
SEG_LEN = 256
LEVELS = 4
SEGS = 128
TOKENS = 32768


def tree_table():
    preorder = []

    def visit(node_id):
        preorder.append(node_id)
        if node_id < 15:
            visit(2 * node_id + 1)
            visit(2 * node_id + 2)
    visit(0)
    position = {}
    for place, node_id in enumerate(preorder):
        position[node_id] = place
    parent_pos = np.zeros((31,), np.int32)
    for place, node_id in enumerate(preorder):
        if node_id > 0:
            parent_pos[place] = position[(node_id - 1) // 2]
    return (parent_pos, np.asarray(preorder, np.int32))


def draw_queries(key, part):
    key = jax.random.fold_in(key, 3)
    group_size = HEADS // KV_HEADS
    result = jnp.clip(2.0 * jax.random.normal(key, (TOKENS, KV_HEADS, group_size, HEAD_DIM), jnp.float32), -16.0, 16.0)
    return result.reshape(TOKENS, HEADS * HEAD_DIM).astype(jnp.bfloat16)


def draw_key_proj(key, part):
    key = jax.random.fold_in(key, 4)
    result = jnp.clip(jax.random.normal(key, (TOKENS, KV_HEADS, HEAD_DIM), jnp.float32), -6.0, 6.0)
    return result.reshape(TOKENS, KV_HEADS * HEAD_DIM).astype(jnp.bfloat16)


def draw_parents(key, part):
    key = jax.random.fold_in(key, 5)
    keep_key = jax.random.fold_in(key, 11)
    pick_key = jax.random.fold_in(key, 12)
    parent_np, preorder_np = tree_table()
    parent_table = jnp.asarray(parent_np, jnp.int32)
    preorder_ids = jnp.asarray(preorder_np, jnp.int32)
    keep_heap = jax.random.randint(keep_key, (SEGS, 31), 0, 4) != 0
    pick_side = jax.random.randint(pick_key, (SEGS, 15), 0, 2)
    left_keep = keep_heap[:, 1:31:2]
    right_keep = keep_heap[:, 2:31:2]
    neither = jnp.logical_not(left_keep) & jnp.logical_not(right_keep)
    left_keep = left_keep | neither & (pick_side == 0)
    right_keep = right_keep | neither & (pick_side == 1)
    children = jnp.stack([left_keep, right_keep], axis=-1).reshape(SEGS, 30)
    kept_heap = jnp.concatenate([jnp.ones((SEGS, 1), bool), children], axis=1)
    kept_mask = kept_heap[:, preorder_ids]
    for sweep_idx in range(4):
        kept_mask = kept_mask & kept_mask[:, parent_table]
    flat_kept = kept_mask.reshape(-1).astype(jnp.int32)
    ranks = jnp.cumsum(flat_kept) - 1
    order_ids = jnp.argsort(1 - flat_kept, stable=True)[:SEGS]
    node_ids = order_ids % 31
    tree_ids = order_ids // 31
    parent_flat = tree_ids * 31 + parent_table[node_ids]
    return jnp.where(node_ids == 0, -1, ranks[parent_flat]).astype(jnp.int32)


def level_of(key, extent, shards, smallest, largest):
    def one(axis_at, blocks):
        steps = jax.random.uniform(jax.random.fold_in(jax.random.fold_in(key, 6), axis_at), (blocks,), jnp.float32, smallest / len(shards), largest / len(shards))
        return jnp.repeat(jnp.exp(steps), extent[axis_at] // blocks).reshape((-1,) + (1,) * (len(extent) - axis_at - 1))

    level = one(*shards[0])
    for cut in shards[1:]:
        level = level * one(*cut)
    return level


def bell_draw(stream_key, shape, spread, limit, split=(), kind=jnp.bfloat16):
    values = spread * jax.random.normal(stream_key, shape, jnp.float32)
    if split:
        values = values * level_of(stream_key, shape, split, -0.22, 0.18)
    return jnp.clip(values, -limit, limit).astype(kind)


def setup_inputs(seed: int = 0) -> dict:
    streams_of = jax.random.split(jax.random.key(seed), 6)
    return {
        "queries": draw_queries(jax.random.fold_in(streams_of[5], 71), 0),
        "key_proj": draw_key_proj(jax.random.fold_in(streams_of[5], 71), 0),
        "value_proj": bell_draw(streams_of[2], (TOKENS, KV_HEADS * HEAD_DIM), 1.0, 6.0, ((0, 64), (1, 4))),
        "out_weight": bell_draw(streams_of[3], (HEADS * HEAD_DIM, D), (HEADS * HEAD_DIM // 16) ** -0.5, 0.375, ((1, 4),)),
        "parents": draw_parents(jax.random.fold_in(streams_of[5], 71), 0),
    }


def tree_levels(parents):
    seg_count = parents.shape[0]
    safe_parent = jnp.maximum(parents, 0)
    depths = jnp.zeros((seg_count,), jnp.int32)
    for sweep_idx in range(LEVELS + 1):
        depths = jnp.where(parents >= 0, depths[safe_parent] + 1, 0).astype(jnp.int32)
    current = jnp.arange(seg_count, dtype=jnp.int32)
    ancestor = jnp.zeros((seg_count, LEVELS), jnp.int32)
    level_ids = jnp.arange(LEVELS, dtype=jnp.int32)
    for sweep_idx in range(LEVELS):
        current = jnp.where(current >= 0, parents[jnp.maximum(current, 0)], -1).astype(jnp.int32)
        level_here = depths - 1 - sweep_idx
        matches = (level_here[:, None] == level_ids[None, :]) & (current[:, None] >= 0)
        ancestor = ancestor + jnp.where(matches, current[:, None], 0).astype(jnp.int32)
    return depths, ancestor


def attend(query_seg, key_block, value_block, seg_depth):
    row_count = query_seg.shape[0]
    key_count = key_block.shape[0]
    kv_count = key_block.shape[1] // HEAD_DIM
    group_size = query_seg.shape[1] // (kv_count * HEAD_DIM)
    query_heads = query_seg.reshape(row_count, kv_count, group_size, HEAD_DIM).astype(jnp.float32)
    key_heads = key_block.reshape(key_count, kv_count, HEAD_DIM).astype(jnp.float32)
    value_heads = value_block.reshape(key_count, kv_count, HEAD_DIM).astype(jnp.float32)
    scores = jnp.einsum("tjgd,kjd->jgtk", query_heads, key_heads) * (HEAD_DIM ** -0.5)
    key_ids = jnp.arange(key_count, dtype=jnp.int32)
    slot_ids = key_ids // row_count
    within = key_ids % row_count
    row_ids = jnp.arange(row_count, dtype=jnp.int32)
    allowed = jnp.where(slot_ids[None, :] < LEVELS, slot_ids[None, :] < seg_depth, within[None, :] <= row_ids[:, None])
    scores = jnp.where(allowed[None, None], scores, -jnp.inf)
    row_max = jnp.max(scores, axis=-1, keepdims=True)
    exponent = jnp.exp(scores - row_max)
    totals = jnp.sum(exponent, axis=-1)
    weights = exponent.astype(jnp.bfloat16)
    mixture = jnp.einsum("jgtk,kjd->tjgd", weights.astype(jnp.float32), value_heads)
    mixture = mixture / jnp.transpose(totals, (2, 0, 1))[..., None]
    return mixture.astype(jnp.bfloat16).reshape(row_count, -1)


def reference(queries, key_proj, value_proj, out_weight, parents):
    depths, ancestor = tree_levels(parents)
    key_segs = key_proj.reshape(SEGS, SEG_LEN, -1)
    value_segs = value_proj.reshape(SEGS, SEG_LEN, -1)
    query_segs = queries.reshape(SEGS, SEG_LEN, -1)
    key_width = key_segs.shape[2]

    def one_segment(seg_idx):
        chosen = ancestor[seg_idx]
        key_block = jnp.concatenate([key_segs[chosen].reshape(LEVELS * SEG_LEN, key_width), key_segs[seg_idx]], axis=0)
        value_block = jnp.concatenate([value_segs[chosen].reshape(LEVELS * SEG_LEN, key_width), value_segs[seg_idx]], axis=0)
        return attend(query_segs[seg_idx], key_block, value_block, depths[seg_idx])

    attended = lax.map(one_segment, jnp.arange(SEGS, dtype=jnp.int32))
    attended = attended.reshape(TOKENS, -1)
    return jnp.dot(attended, out_weight, preferred_element_type=jnp.float32).astype(jnp.bfloat16)
```

```python
import functools
import math

import jax
import jax.numpy as jnp
from jax import lax
from jax.experimental import pallas as pl
from jax.experimental.pallas import tpu as pltpu
from jax.sharding import PartitionSpec as P

HEAD_DIM = 128
SEG_LEN = 256
LEVELS = 4
PIECE = 8
MASKED = -1e30
EXP2_SCALE = math.log2(math.e) * HEAD_DIM ** (-0.5)
VMEM_LIMIT = 40 * 1024 * 1024


def path_of(parents_ref, seg):
    path = [parents_ref[seg]]
    for _ in range(LEVELS - 1):
        up = parents_ref[jnp.maximum(path[-1], 0)]
        path.append(jnp.where(path[-1] >= 0, up, -1))
    depth = sum((p >= 0).astype(jnp.int32) for p in path)
    return path, depth


def ancestry_kernel(first_ref, parents_ref, table_ref, limits_ref):
    targets = table_ref.shape[0] // LEVELS

    @pl.loop(0, targets)
    def _(target):
        path, depth = path_of(parents_ref, 2 * target)
        for level in range(LEVELS):
            found = jnp.int32(0)
            for up in range(LEVELS):
                found = jnp.where(depth - 1 - up == level, path[up], found)
            table_ref[target * LEVELS + level] = found

    first = first_ref[0]
    _, depth0 = path_of(parents_ref, first)
    _, depth1 = path_of(parents_ref, first + 1)
    limits_ref[0] = depth0
    limits_ref[1] = jnp.minimum(depth0, depth1)
    limits_ref[2] = (parents_ref[first + 1] == first).astype(jnp.int32)


def ancestry(first, parents, targets):
    smem = pl.BlockSpec(memory_space=pltpu.SMEM)
    return pl.pallas_call(
        ancestry_kernel,
        out_shape=(
            jax.ShapeDtypeStruct((targets * LEVELS,), jnp.int32),
            jax.ShapeDtypeStruct((3,), jnp.int32),
        ),
        in_specs=[smem, smem],
        out_specs=(smem, smem),
        cost_estimate=pl.CostEstimate(flops=8000, bytes_accessed=2000, transcendentals=0),
        name="ancestry",
    )(first, parents)


def pick_kernel(table_ref, pieces_ref, picked_ref):
    @pl.loop(0, picked_ref.shape[0], unroll=8)
    def _(slot):
        picked_ref[slot] = pieces_ref[table_ref[slot]]


def pick(table, pieces):
    slots = table.shape[0]
    vmem = pl.BlockSpec(memory_space=pltpu.VMEM)
    return pl.pallas_call(
        pick_kernel,
        out_shape=jax.ShapeDtypeStruct((slots,) + pieces.shape[1:], pieces.dtype),
        in_specs=[pl.BlockSpec(memory_space=pltpu.SMEM), vmem],
        out_specs=vmem,
        cost_estimate=pl.CostEstimate(flops=0, bytes_accessed=1 << 20, transcendentals=0),
        name="pick",
    )(table, pieces)


def attend_kernel(limits_ref, query_ref, path_key_ref, path_value_ref, key_ref, value_ref, out_ref):
    def scores_of(query, keys):
        return lax.dot_general(
            query, keys, (((1,), (1,)), ((), ())), preferred_element_type=jnp.float32
        )

    def with_ones(values):
        return jnp.concatenate([values, jnp.ones_like(values)], axis=1)

    path_keys, path_values = path_key_ref[...], with_ones(path_value_ref[...])
    level = (lax.broadcasted_iota(jnp.int32, (1, path_keys.shape[0]), 1) // PIECE) % LEVELS
    rows = lax.broadcasted_iota(jnp.int32, (SEG_LEN, SEG_LEN), 0)
    columns = lax.broadcasted_iota(jnp.int32, (SEG_LEN, SEG_LEN), 1)
    for seg in range(2):
        here = slice(seg * SEG_LEN, (seg + 1) * SEG_LEN)
        query = query_ref[here]
        path_scores = scores_of(query, path_keys)
        path_scores = path_scores + jnp.where(level < limits_ref[seg], 0.0, MASKED)
        own_scores = jnp.where(columns <= rows, scores_of(query, key_ref[here]), MASKED)
        blocks = [(path_scores, path_values), (own_scores, with_ones(value_ref[here]))]
        if seg == 1:
            before = scores_of(query, key_ref[:SEG_LEN])
            before = before + jnp.where(limits_ref[2] > 0, 0.0, MASKED)
            blocks.append((before, with_ones(value_ref[:SEG_LEN])))
        row_max = functools.reduce(
            jnp.maximum, [jnp.max(s, axis=1, keepdims=True) for s, _ in blocks]
        )
        total = None
        for scores, values in blocks:
            weights = jnp.exp2((scores - row_max) * EXP2_SCALE).astype(jnp.bfloat16)
            part = jnp.dot(weights, values, preferred_element_type=jnp.float32)
            total = part if total is None else total + part
        out_ref[here] = (total[:, :HEAD_DIM] / total[:, HEAD_DIM:]).astype(out_ref.dtype)


def attend(limits, queries, path_keys, path_values, keys, values, first_head, heads):
    rows = queries.shape[0]
    whole = lambda a: pl.BlockSpec(a.shape, lambda h, limits: (0, 0))
    key_count = path_keys.shape[0] + SEG_LEN + SEG_LEN // 2
    return pl.pallas_call(
        attend_kernel,
        grid_spec=pltpu.PrefetchScalarGridSpec(
            num_scalar_prefetch=1,
            grid=(heads,),
            in_specs=[
                pl.BlockSpec((rows, HEAD_DIM), lambda h, limits: (0, first_head + h)),
                whole(path_keys),
                whole(path_values),
                whole(keys),
                whole(values),
            ],
            out_specs=pl.BlockSpec((rows, HEAD_DIM), lambda h, limits: (0, h)),
        ),
        out_shape=jax.ShapeDtypeStruct((rows, heads * HEAD_DIM), jnp.bfloat16),
        compiler_params=pltpu.CompilerParams(vmem_limit_bytes=VMEM_LIMIT),
        cost_estimate=pl.CostEstimate(
            flops=heads * rows * key_count * HEAD_DIM * 6,
            bytes_accessed=heads * rows * HEAD_DIM * 4 + 4 * path_keys.size,
            transcendentals=heads * rows * key_count,
        ),
        name="attend",
    )(limits, queries, path_keys, path_values, keys, values)


def project_kernel(count, has_base, blocks_ref, *refs):
    parts, weight_ref, rest = refs[:count], refs[count], refs[count + 1 :]
    base_ref = rest[0] if has_base else None
    out_ref, total_ref = rest[-2:]
    step = pl.program_id(0)

    for i in range(count):

        @pl.when(step == i)
        def _(i=i):
            product = jnp.dot(parts[i][...], weight_ref[...], preferred_element_type=jnp.float32)
            if i == 0:
                before = base_ref[...] if has_base else None
            else:
                before = total_ref[...]
            total = product if before is None else before + product
            if i == count - 1:
                out_ref[...] = total.astype(out_ref.dtype)
            else:
                total_ref[...] = total


def project(parts, blocks, weight, base, dtype):
    rows, depth = parts[0].shape
    width = weight.shape[1]
    count = len(parts)
    whole = lambda shape: pl.BlockSpec(shape, lambda k, blocks: (0, 0))
    in_specs = [whole(p.shape) for p in parts]
    in_specs.append(pl.BlockSpec((depth, width), lambda k, blocks: (blocks[k], 0)))
    args = list(parts) + [weight]
    if base is not None:
        in_specs.append(whole(base.shape))
        args.append(base)
    return pl.pallas_call(
        functools.partial(project_kernel, count, base is not None),
        grid_spec=pltpu.PrefetchScalarGridSpec(
            num_scalar_prefetch=1,
            grid=(count,),
            in_specs=in_specs,
            out_specs=whole((rows, width)),
            scratch_shapes=[pltpu.VMEM((rows, width), jnp.float32)],
        ),
        out_shape=jax.ShapeDtypeStruct((rows, width), dtype),
        compiler_params=pltpu.CompilerParams(vmem_limit_bytes=VMEM_LIMIT),
        cost_estimate=pl.CostEstimate(
            flops=2 * count * rows * depth * width,
            bytes_accessed=2 * count * depth * (rows + width) + 4 * rows * width,
            transcendentals=0,
        ),
        name="project",
    )(blocks, *args)


def swap(part, bit):
    size = lax.axis_size("tensor")
    return lax.ppermute(part, "tensor", [(i, i ^ bit) for i in range(size)])


def per_device(queries, key_proj, value_proj, out_weight, parents):
    devices = lax.axis_size("dp")
    me = lax.axis_index("tensor")
    segs = queries.shape[0] // SEG_LEN
    first = (lax.axis_index("dp") * segs).astype(jnp.int32).reshape(1)
    table, limits = ancestry(first, parents, devices)

    half = devices // 2
    cut = lambda a: a.reshape(segs, half, PIECE, HEAD_DIM)
    pieces = jnp.concatenate([cut(key_proj), cut(value_proj)], axis=1).transpose(1, 0, 2, 3)
    pieces = lax.all_to_all(pieces, "dp", 0, 0, tiled=True)
    picked = pick(table, pieces.reshape(devices * segs, PIECE, HEAD_DIM))
    picked = picked.reshape(devices, LEVELS, PIECE, HEAD_DIM)
    picked = lax.all_to_all(picked, "dp", 0, 0, tiled=True)
    path = picked.reshape(2, half * LEVELS * PIECE, HEAD_DIM)

    heads = queries.shape[1] // HEAD_DIM
    chunk = 2
    chunks = heads // chunk
    own = [
        attend(limits, queries, path[0], path[1], key_proj, value_proj, c * chunk, chunk)
        for c in range(chunks)
    ]
    across = [swap(part, 2) for part in own]
    beside = [swap(part, 1) for part in own]
    corner = [swap(part, 1) for part in across]
    where = lambda bit: (me ^ bit) * chunks + jnp.arange(chunks, dtype=jnp.int32)
    near = project(
        own + beside, jnp.concatenate([where(0), where(1)]), out_weight, None, jnp.float32
    )
    far = jnp.stack([where(2), where(3)], axis=1).reshape(-1)
    far_parts = [part for pair in zip(across, corner) for part in pair]
    split = 2 * (chunks - 1)
    near = project(far_parts[:split], far[:split], out_weight, near, jnp.float32)
    return project(far_parts[split:], far[split:], out_weight, near, jnp.bfloat16)


def solution(mesh):
    placed = (P("dp", "tensor"), P("dp", "tensor"), P("dp", "tensor"), P(None, "tensor"), P())
    return jax.shard_map(
        per_device, mesh=mesh, in_specs=placed, out_specs=P("dp", "tensor"), check_vma=False
    )
```

```python
import functools
import math

import jax
import jax.numpy as jnp
from jax import lax
from jax.experimental import pallas as pl
from jax.experimental.pallas import tpu as pltpu
from jax.sharding import PartitionSpec as P

HEAD_DIM = 128
SEG_LEN = 256
LEVELS = 4
FAR = LEVELS - 1
ROW = 8
ROW_SEGS = 2 * ROW
PIECE = SEG_LEN // ROW
PATH = LEVELS * SEG_LEN
FAR_ROWS = FAR * PIECE
MASKED = -1e30
EXP2_SCALE = math.log2(math.e) * HEAD_DIM ** (-0.5)
ATTEND_VMEM = 20 * 1024 * 1024
PROJECT_VMEM = 28 * 1024 * 1024

VMEM = pl.BlockSpec(memory_space=pltpu.VMEM)
SMEM = pl.BlockSpec(memory_space=pltpu.SMEM)
ANY = pl.BlockSpec(memory_space=pl.ANY)


def path_of(parents_ref, seg):
    path = [parents_ref[seg]]
    for _ in range(LEVELS - 1):
        up = parents_ref[jnp.maximum(path[-1], 0)]
        path.append(jnp.where(path[-1] >= 0, up, -1))
    depth = sum((p >= 0).astype(jnp.int32) for p in path)
    return path, depth


def level_of(path, depth, level):
    found = jnp.int32(0)
    for up in range(LEVELS):
        found = jnp.where(depth - 1 - up == level, path[up], found)
    return found


def ancestry_kernel(first_ref, parents_ref, table_ref, carry_ref, limits_ref):
    first = first_ref[0]
    base = (first // ROW_SEGS) * ROW_SEGS
    place = (first - base) // 2

    for shift in range(ROW):
        target = lax.rem(place + shift, ROW)
        path, depth = path_of(parents_ref, base + 2 * target)
        for level in range(FAR):
            seg = level_of(path, depth, level)
            slot = jnp.where(seg >= base - ROW_SEGS, ROW_SEGS + level, ROW_SEGS + FAR)
            table_ref[shift * FAR + level] = jnp.where(seg >= base, seg - base, slot)

    last = parents_ref.shape[0] - 1
    path, depth = path_of(parents_ref, jnp.minimum(base + ROW_SEGS, last))
    for level in range(FAR):
        carry_ref[level] = jnp.clip(level_of(path, depth, level) - base, 0, ROW_SEGS - 1)
    path, depth = path_of(parents_ref, jnp.minimum(base + 2 * ROW_SEGS, last))
    carry_ref[FAR] = jnp.clip(level_of(path, depth, 0) - base, 0, ROW_SEGS - 1)
    carry_ref[FAR + 1] = place

    _, depth0 = path_of(parents_ref, first)
    _, depth1 = path_of(parents_ref, first + 1)
    limits_ref[0] = depth0
    limits_ref[1] = jnp.minimum(depth0, depth1)
    limits_ref[2] = (parents_ref[first + 1] == first).astype(jnp.int32)


def ancestry(first, parents):
    shape = lambda n: jax.ShapeDtypeStruct((n,), jnp.int32)
    return pl.pallas_call(
        ancestry_kernel,
        out_shape=(shape(ROW * FAR), shape(FAR + 2), shape(3)),
        in_specs=[SMEM, SMEM],
        out_specs=(SMEM, SMEM, SMEM),
        cost_estimate=pl.CostEstimate(flops=8000, bytes_accessed=2000, transcendentals=0),
        name="ancestry",
    )(first, parents)


def pack_kernel(first_ref, parents_ref, key_ref, value_ref, deep_ref, *piece_refs):
    place = lax.rem(first_ref[0] // 2, ROW)
    for shift, piece_ref in enumerate(piece_refs):
        piece = lax.rem(place + shift, ROW)
        for seg in range(2):
            rows = pl.ds(pl.multiple_of(seg * SEG_LEN + piece * PIECE, PIECE), PIECE)
            piece_ref[seg, :PIECE] = key_ref[rows]
            piece_ref[seg, PIECE:] = value_ref[rows]
    _, depth = path_of(parents_ref, first_ref[0] + 1)
    start = jnp.where(depth == FAR, SEG_LEN, 0)
    rows = pl.ds(pl.multiple_of(start, SEG_LEN), SEG_LEN)
    deep_ref[:SEG_LEN] = key_ref[rows]
    deep_ref[SEG_LEN:] = value_ref[rows]


def pack(first, parents, keys, values):
    shape = lambda *dims: jax.ShapeDtypeStruct(dims, keys.dtype)
    return pl.pallas_call(
        pack_kernel,
        out_shape=(shape(2 * SEG_LEN, HEAD_DIM),) + (shape(2, 2 * PIECE, HEAD_DIM),) * ROW,
        in_specs=[SMEM, SMEM, VMEM, VMEM],
        out_specs=(VMEM,) * (ROW + 1),
        cost_estimate=pl.CostEstimate(flops=0, bytes_accessed=1 << 19, transcendentals=0),
        name="pack",
    )(first, parents, keys, values)


def carry_kernel(carry_ref, *refs):
    pieces, (held_ref, next_ref, second_ref) = refs[:ROW], refs[ROW:]
    place = carry_ref[FAR + 1]
    for shift, piece in enumerate(pieces):
        source = lax.rem(place + ROW - shift, ROW)
        held_ref[pl.ds(2 * source, 2)] = piece[...]
    for level in range(FAR):
        next_ref[level] = held_ref[carry_ref[level]]
    second_ref[0] = held_ref[carry_ref[FAR]]


def carry_out(carry, pieces):
    shape = lambda n: jax.ShapeDtypeStruct((n,) + pieces[0].shape[1:], pieces[0].dtype)
    return pl.pallas_call(
        carry_kernel,
        out_shape=(shape(ROW_SEGS), shape(FAR), shape(1)),
        in_specs=[SMEM] + [VMEM] * ROW,
        out_specs=(VMEM, VMEM, VMEM),
        cost_estimate=pl.CostEstimate(flops=0, bytes_accessed=1 << 18, transcendentals=0),
        name="carry_out",
    )(carry, *pieces)


def pick_kernel(table_ref, pieces_ref, next_ref, second_ref, *refs):
    picked, held_ref = refs[:ROW], refs[ROW]
    held_ref[:ROW_SEGS] = pieces_ref[...]
    held_ref[ROW_SEGS : ROW_SEGS + FAR] = next_ref[...]
    held_ref[ROW_SEGS + FAR :] = second_ref[...]
    for shift, picked_ref in enumerate(picked):
        for level in range(FAR):
            picked_ref[level] = held_ref[table_ref[shift * FAR + level]]


def pick(table, held, carried, second):
    dims = held.shape[1:]
    return pl.pallas_call(
        pick_kernel,
        out_shape=(jax.ShapeDtypeStruct((FAR,) + dims, held.dtype),) * ROW,
        in_specs=[SMEM, VMEM, VMEM, VMEM],
        out_specs=(VMEM,) * ROW,
        scratch_shapes=[pltpu.VMEM((ROW_SEGS + FAR + 1,) + dims, held.dtype)],
        cost_estimate=pl.CostEstimate(flops=0, bytes_accessed=1 << 20, transcendentals=0),
        name="pick",
    )(table, held, carried, second)


def attend_kernel(first_head, heads, limits_ref, query_ref, key_ref, value_ref, deep_ref, *refs):
    pieces = refs[:ROW]
    out_ref, path_key_ref, path_value_ref = refs[-3:]

    def scores_of(query, keys):
        return lax.dot_general(
            query, keys, (((1,), (1,)), ((), ())), preferred_element_type=jnp.float32
        )

    def with_ones(values):
        return jnp.concatenate([values, jnp.ones_like(values)], axis=1)

    for at, piece in enumerate(pieces):
        for level in range(FAR):
            rows = pl.ds(at * FAR_ROWS + level * PIECE, PIECE)
            path_key_ref[rows, :HEAD_DIM] = piece[level, :PIECE]
            path_value_ref[rows, :HEAD_DIM] = piece[level, PIECE:]
    path_key_ref[FAR * SEG_LEN :, :HEAD_DIM] = deep_ref[:SEG_LEN]
    path_value_ref[FAR * SEG_LEN :, :HEAD_DIM] = deep_ref[SEG_LEN:]
    path_value_ref[:, HEAD_DIM:] = jnp.ones((PATH, HEAD_DIM), jnp.bfloat16)
    row = lax.broadcasted_iota(jnp.int32, (PATH, HEAD_DIM), 0)
    lane = lax.broadcasted_iota(jnp.int32, (PATH, HEAD_DIM), 1)
    level = jnp.where(row < FAR * SEG_LEN, lax.rem(row // PIECE, FAR), FAR)
    limit = jnp.where(lane == 0, limits_ref[0], jnp.where(lane == 1, limits_ref[1], LEVELS))
    path_key_ref[:, HEAD_DIM:] = jnp.where(level < limit, 0.0, MASKED).astype(jnp.bfloat16)
    path_keys, path_values = path_key_ref[...], path_value_ref[...]

    rows = lax.broadcasted_iota(jnp.int32, (2 * SEG_LEN, HEAD_DIM), 0)
    lanes = lax.broadcasted_iota(jnp.int32, (2 * SEG_LEN, HEAD_DIM), 1)
    marks = (lanes == rows // SEG_LEN).astype(jnp.float32).astype(jnp.bfloat16)
    causal = lax.broadcasted_iota(jnp.int32, (SEG_LEN, SEG_LEN), 1) <= lax.broadcasted_iota(
        jnp.int32, (SEG_LEN, SEG_LEN), 0
    )
    follows = jnp.where(limits_ref[2] > 0, 0.0, MASKED)
    halves = [slice(0, SEG_LEN), slice(SEG_LEN, 2 * SEG_LEN)]
    own_values = [with_ones(value_ref[half]) for half in halves]
    for head in range(heads):
        at = (first_head + head) * HEAD_DIM
        query = query_ref[:, at : at + HEAD_DIM]
        path_scores = scores_of(jnp.concatenate([query, marks], axis=1), path_keys)
        own = [
            [(jnp.where(causal, scores_of(query[half], key_ref[half]), MASKED), values)]
            for half, values in zip(halves, own_values)
        ]
        own[1].append((scores_of(query[halves[1]], key_ref[halves[0]]) + follows, own_values[0]))
        path_weights, own_parts = [], []
        for half, blocks in zip(halves, own):
            row_max = functools.reduce(
                jnp.maximum,
                [jnp.max(s, axis=1, keepdims=True) for s, _ in blocks]
                + [jnp.max(path_scores[half], axis=1, keepdims=True)],
            )
            weigh = lambda s: jnp.exp2((s - row_max) * EXP2_SCALE).astype(jnp.bfloat16)
            path_weights.append(weigh(path_scores[half]))
            own_parts.append(
                sum(
                    jnp.dot(weigh(s), values, preferred_element_type=jnp.float32)
                    for s, values in blocks
                )
            )
        total = jnp.dot(
            jnp.concatenate(path_weights, axis=0), path_values, preferred_element_type=jnp.float32
        ) + jnp.concatenate(own_parts, axis=0)
        mixture = total[:, :HEAD_DIM] / total[:, HEAD_DIM:]
        out_ref[:, head * HEAD_DIM : (head + 1) * HEAD_DIM] = mixture.astype(out_ref.dtype)


def attend(limits, queries, keys, values, deep, pieces, first_head, heads, after):
    rows = queries.shape[0]
    key_count = PATH + SEG_LEN + SEG_LEN // 2
    return pl.pallas_call(
        functools.partial(attend_kernel, first_head, heads),
        out_shape=jax.ShapeDtypeStruct((rows, heads * HEAD_DIM), jnp.bfloat16),
        in_specs=[SMEM] + [VMEM] * (4 + ROW) + [ANY] * len(after),
        out_specs=VMEM,
        scratch_shapes=[pltpu.VMEM((PATH, 2 * HEAD_DIM), jnp.bfloat16)] * 2,
        compiler_params=pltpu.CompilerParams(vmem_limit_bytes=ATTEND_VMEM),
        cost_estimate=pl.CostEstimate(
            flops=heads * rows * key_count * HEAD_DIM * 10,
            bytes_accessed=heads * rows * HEAD_DIM * 4 + 8 * PATH * HEAD_DIM,
            transcendentals=heads * rows * key_count,
        ),
        name="attend",
    )(limits, queries, keys, values, deep, *pieces, *after)


def project_kernel(groups, tile, has_base, starts_ref, weight_ref, *refs):
    count = sum(groups)
    parts, rest = refs[:count], refs[count:]
    out_ref, held_ref = rest[-2:]
    at = 0
    for part in parts:
        held_ref[:, at : at + part.shape[1]] = part[...]
        at += part.shape[1]

    for column in range(0, out_ref.shape[1], tile):
        columns = slice(column, column + tile)
        total = rest[0][:, columns] if has_base else None
        at, left = 0, parts
        for g, group in enumerate(groups):
            depth = sum(part.shape[1] for part in left[:group])
            left = left[group:]
            rows = pl.ds(pl.multiple_of(starts_ref[g], 2 * HEAD_DIM), depth)
            product = jnp.dot(
                held_ref[:, at : at + depth],
                weight_ref[rows, columns],
                preferred_element_type=jnp.float32,
            )
            total = product if total is None else total + product
            at += depth
        out_ref[:, columns] = total.astype(out_ref.dtype)


def project(groups, starts, weight, base, dtype):
    parts = [part for group in groups for part in group]
    rows = parts[0].shape[0]
    depth = sum(part.shape[1] for part in parts)
    width = weight.shape[1]
    bases = [] if base is None else [base]
    return pl.pallas_call(
        functools.partial(project_kernel, [len(g) for g in groups], 256, base is not None),
        out_shape=jax.ShapeDtypeStruct((rows, width), dtype),
        in_specs=[SMEM] + [VMEM] * (1 + len(parts) + len(bases)),
        out_specs=VMEM,
        scratch_shapes=[pltpu.VMEM((rows, depth), parts[0].dtype)],
        compiler_params=pltpu.CompilerParams(vmem_limit_bytes=PROJECT_VMEM),
        cost_estimate=pl.CostEstimate(
            flops=2 * rows * depth * width,
            bytes_accessed=2 * depth * (rows + width) + 4 * rows * width,
            transcendentals=0,
        ),
        name="project",
    )(starts, weight, *parts, *bases)


def swap(part, bit):
    size = lax.axis_size("tensor")
    return lax.ppermute(part, "tensor", [(i, i ^ bit) for i in range(size)])


def around(pieces):
    devices = lax.axis_size("dp")
    moved = [
        lax.ppermute(
            piece, "dp", [(i, i - i % ROW + (i + shift) % ROW) for i in range(devices)]
        )
        for shift, piece in enumerate(pieces)
        if shift
    ]
    return [pieces[0]] + moved


def onward(piece, step):
    devices = lax.axis_size("dp")
    return lax.ppermute(piece, "dp", [(i, i + step) for i in range(devices - step)])


def per_device(queries, key_proj, value_proj, out_weight, parents):
    me = lax.axis_index("tensor")
    first = (lax.axis_index("dp") * 2).astype(jnp.int32).reshape(1)
    deep, *pieces = pack(first, parents, key_proj, value_proj)
    pieces = around(pieces)
    deep = onward(deep, 1)
    table, carry, limits = ancestry(first, parents)
    held, to_next, to_second = carry_out(carry, pieces)
    picked = pick(table, held, onward(to_next, ROW), onward(to_second, 2 * ROW))
    picked = around(picked)

    width = queries.shape[1]
    chunk = 2
    chunks = width // HEAD_DIM // chunk
    own, across = [], []
    for c in range(chunks):
        after = across[c - 2 : c - 1] if c >= 2 else []
        own.append(
            attend(
                limits, queries, key_proj, value_proj, deep, picked, c * chunk, chunk, after
            )
        )
        across.append(swap(own[c], 2))
    beside = [swap(part, 1) for part in own]
    split = chunks - 1
    corner = [swap(part, 1) for part in across[:split]]
    starts = jnp.stack([me, me ^ 1, me ^ 2, me ^ 3]) * width
    near = project(
        [own, beside, across[:split], corner], starts, out_weight, None, jnp.float32
    )
    last, near = lax.optimization_barrier((across[split], near))
    return project(
        [[last], [swap(last, 1)]],
        starts[2:] + split * chunk * HEAD_DIM,
        out_weight,
        near,
        jnp.bfloat16,
    )


def solution(mesh):
    placed = (P("dp", "tensor"), P("dp", "tensor"), P("dp", "tensor"), P(None, "tensor"), P())
    return jax.shard_map(
        per_device, mesh=mesh, in_specs=placed, out_specs=P("dp", "tensor"), check_vma=False
    )
```

```python
import functools
import math

import jax
import jax.numpy as jnp
from jax import lax
from jax.experimental import pallas as pl
from jax.experimental.pallas import tpu as pltpu
from jax.sharding import PartitionSpec as P

HEAD_DIM = 128
SEG_LEN = 256
LEVELS = 4
ROW = 8
ROW_SEGS = 2 * ROW
PIECE = SEG_LEN // ROW
PATH = LEVELS * SEG_LEN
STACK = LEVELS * PIECE
MASKED = -1e30
EXP2_SCALE = math.log2(math.e) * HEAD_DIM ** (-0.5)
SMALL_VMEM = 6 * 1024 * 1024
ATTEND_VMEM = 20 * 1024 * 1024
PROJECT_VMEM = 28 * 1024 * 1024
LAST_VMEM = 16 * 1024 * 1024
TILE = 256

VMEM = pl.BlockSpec(memory_space=pltpu.VMEM)
SMEM = pl.BlockSpec(memory_space=pltpu.SMEM)
ANY = pl.BlockSpec(memory_space=pl.ANY)
HBM = pl.BlockSpec(memory_space=pltpu.HBM)
FLAG_ROWS = 16


def in_hbm(array):
    return pltpu.with_memory_space_constraint(array, pltpu.HBM)


def path_of(parents_ref, seg):
    path = [parents_ref[seg]]
    for _ in range(LEVELS - 1):
        up = parents_ref[jnp.maximum(path[-1], 0)]
        path.append(jnp.where(path[-1] >= 0, up, -1))
    depth = sum((p >= 0).astype(jnp.int32) for p in path)
    return path, depth


def level_of(path, depth, level):
    found = jnp.int32(0)
    for up in range(LEVELS):
        found = jnp.where(depth - 1 - up == level, path[up], found)
    return found


def pack_kernel(key_ref, value_ref, piece_ref, held_ref, sem):
    copies = [
        pltpu.make_async_copy(source, held_ref.at[i], sem.at[i])
        for i, source in enumerate([key_ref, value_ref])
    ]
    for copy in copies:
        copy.start()
    for i, copy in enumerate(copies):
        copy.wait()
        for piece in range(ROW):
            for seg in range(2):
                rows = pl.ds(seg * SEG_LEN + piece * PIECE, PIECE)
                piece_ref[piece, seg, i * PIECE : (i + 1) * PIECE] = held_ref[i, rows]


def pack(keys, values):
    return pl.pallas_call(
        pack_kernel,
        out_shape=jax.ShapeDtypeStruct((ROW, 2, 2 * PIECE, HEAD_DIM), keys.dtype),
        in_specs=[HBM, HBM],
        out_specs=VMEM,
        scratch_shapes=[pltpu.VMEM((2,) + keys.shape, keys.dtype), pltpu.SemaphoreType.DMA((2,))],
        compiler_params=pltpu.CompilerParams(vmem_limit_bytes=SMALL_VMEM),
        cost_estimate=pl.CostEstimate(flops=0, bytes_accessed=1 << 19, transcendentals=0),
        name="pack",
    )(in_hbm(keys), in_hbm(values))


def row_start(first_ref):
    return (first_ref[0] // ROW_SEGS) * ROW_SEGS


def carry_kernel(first_ref, parents_ref, pieces_ref, next_ref, second_ref):
    base = row_start(first_ref)
    last = parents_ref.shape[0] - 1

    def held(path, depth, level):
        return pieces_ref[jnp.clip(level_of(path, depth, level) - base, 0, ROW_SEGS - 1)]

    path, depth = path_of(parents_ref, jnp.minimum(base + ROW_SEGS, last))
    for level in range(LEVELS):
        next_ref[level] = held(path, depth, level)
    path, depth = path_of(parents_ref, jnp.minimum(base + 2 * ROW_SEGS, last))
    second_ref[0] = held(path, depth, 0)


def carry_out(first, parents, pieces):
    shape = lambda n: jax.ShapeDtypeStruct((n,) + pieces.shape[1:], pieces.dtype)
    return pl.pallas_call(
        carry_kernel,
        out_shape=(shape(LEVELS), shape(1)),
        in_specs=[SMEM, SMEM, VMEM],
        out_specs=(VMEM, VMEM),
        compiler_params=pltpu.CompilerParams(vmem_limit_bytes=SMALL_VMEM),
        cost_estimate=pl.CostEstimate(flops=0, bytes_accessed=1 << 18, transcendentals=0),
        name="carry_out",
    )(first, parents, pieces)


def pick_kernel(first_ref, parents_ref, pieces_ref, inside_ref, next_ref, second_ref):
    base = row_start(first_ref)
    ones = lambda on: jnp.full((FLAG_ROWS, HEAD_DIM), on, jnp.float32).astype(jnp.bfloat16)
    for target in range(ROW):
        path, depth = path_of(parents_ref, base + 2 * target)
        for level in range(LEVELS):
            seg = level_of(path, depth, level)
            within = seg >= base
            piece = pieces_ref[jnp.maximum(seg - base, 0)]
            inside_ref[target, level] = jnp.where(within, piece, jnp.zeros_like(piece))
            before = jnp.logical_and(seg < base, seg >= base - ROW_SEGS)
            next_ref[target, level] = ones(jnp.where(before, 1.0, 0.0))
            if level == 0:
                second_ref[target] = ones(jnp.where(seg < base - ROW_SEGS, 1.0, 0.0))


def pick(first, parents, pieces):
    shape = lambda *dims: jax.ShapeDtypeStruct(dims, pieces.dtype)
    return pl.pallas_call(
        pick_kernel,
        out_shape=(
            shape(ROW, LEVELS, *pieces.shape[1:]),
            shape(ROW, LEVELS, FLAG_ROWS, HEAD_DIM),
            shape(ROW, FLAG_ROWS, HEAD_DIM),
        ),
        in_specs=[SMEM, SMEM, VMEM],
        out_specs=(VMEM, VMEM, VMEM),
        compiler_params=pltpu.CompilerParams(vmem_limit_bytes=SMALL_VMEM),
        cost_estimate=pl.CostEstimate(flops=0, bytes_accessed=1 << 20, transcendentals=0),
        name="pick",
    )(first, parents, pieces)


def merge_kernel(inside_ref, on_next_ref, on_second_ref, next_ref, second_ref, picked_ref):
    for level in range(LEVELS):
        for at in range(0, 2 * PIECE, FLAG_ROWS):
            rows = pl.ds(at, FLAG_ROWS)
            carried = next_ref[level, rows]
            older = second_ref[0, rows]
            for target in range(ROW):
                total = inside_ref[target, level, rows] + carried * on_next_ref[target, level]
                if level == 0:
                    total = total + older * on_second_ref[target]
                picked_ref[target, level, rows] = total


def merge(inside, on_next, on_second, carried, second):
    return pl.pallas_call(
        merge_kernel,
        out_shape=jax.ShapeDtypeStruct(inside.shape, inside.dtype),
        in_specs=[VMEM] * 5,
        out_specs=VMEM,
        compiler_params=pltpu.CompilerParams(vmem_limit_bytes=SMALL_VMEM),
        cost_estimate=pl.CostEstimate(flops=0, bytes_accessed=1 << 20, transcendentals=0),
        name="merge",
    )(inside, on_next, on_second, carried, second)


def attend_kernel(
    first_head, heads, first_ref, parents_ref, query_ref, key_ref, value_ref, far_ref, *refs
):
    out_ref, path_key_ref, path_value_ref = refs[-3:]
    first = first_ref[0]
    _, depth0 = path_of(parents_ref, first)
    _, depth1 = path_of(parents_ref, first + 1)
    follows = jnp.where(parents_ref[first + 1] == first, 0.0, MASKED)

    def scores_of(query, keys):
        return lax.dot_general(
            query, keys, (((1,), (1,)), ((), ())), preferred_element_type=jnp.float32
        )

    def with_ones(values):
        return jnp.concatenate([values, jnp.ones_like(values)], axis=1)

    for piece in range(ROW):
        for level in range(LEVELS):
            rows = pl.ds(piece * STACK + level * PIECE, PIECE)
            path_key_ref[rows, :HEAD_DIM] = far_ref[piece, level, :PIECE]
            path_value_ref[rows, :HEAD_DIM] = far_ref[piece, level, PIECE:]
    path_value_ref[:, HEAD_DIM:] = jnp.ones((PATH, HEAD_DIM), jnp.bfloat16)
    row = lax.broadcasted_iota(jnp.int32, (PATH, HEAD_DIM), 0)
    lane = lax.broadcasted_iota(jnp.int32, (PATH, HEAD_DIM), 1)
    level = lax.rem(row // PIECE, LEVELS)
    limit = jnp.where(lane == 0, depth0, jnp.where(lane == 1, jnp.minimum(depth0, depth1), LEVELS))
    path_key_ref[:, HEAD_DIM:] = jnp.where(level < limit, 0.0, MASKED).astype(jnp.bfloat16)
    path_keys, path_values = path_key_ref[...], path_value_ref[...]

    rows = lax.broadcasted_iota(jnp.int32, (2 * SEG_LEN, HEAD_DIM), 0)
    lanes = lax.broadcasted_iota(jnp.int32, (2 * SEG_LEN, HEAD_DIM), 1)
    marks = (lanes == rows // SEG_LEN).astype(jnp.float32).astype(jnp.bfloat16)
    causal = lax.broadcasted_iota(jnp.int32, (SEG_LEN, SEG_LEN), 1) <= lax.broadcasted_iota(
        jnp.int32, (SEG_LEN, SEG_LEN), 0
    )
    halves = [slice(0, SEG_LEN), slice(SEG_LEN, 2 * SEG_LEN)]
    own_values = [with_ones(value_ref[half]) for half in halves]
    for head in range(heads):
        at = (first_head + head) * HEAD_DIM
        query = query_ref[:, at : at + HEAD_DIM]
        path_scores = scores_of(jnp.concatenate([query, marks], axis=1), path_keys)
        own = [
            [(jnp.where(causal, scores_of(query[half], key_ref[half]), MASKED), values)]
            for half, values in zip(halves, own_values)
        ]
        own[1].append((scores_of(query[halves[1]], key_ref[halves[0]]) + follows, own_values[0]))
        path_weights, own_parts = [], []
        for half, blocks in zip(halves, own):
            row_max = functools.reduce(
                jnp.maximum,
                [jnp.max(s, axis=1, keepdims=True) for s, _ in blocks]
                + [jnp.max(path_scores[half], axis=1, keepdims=True)],
            )
            weigh = lambda s: jnp.exp2((s - row_max) * EXP2_SCALE).astype(jnp.bfloat16)
            path_weights.append(weigh(path_scores[half]))
            own_parts.append(
                sum(
                    jnp.dot(weigh(s), values, preferred_element_type=jnp.float32)
                    for s, values in blocks
                )
            )
        total = jnp.dot(
            jnp.concatenate(path_weights, axis=0), path_values, preferred_element_type=jnp.float32
        ) + jnp.concatenate(own_parts, axis=0)
        mixture = total[:, :HEAD_DIM] / total[:, HEAD_DIM:]
        out_ref[:, head * HEAD_DIM : (head + 1) * HEAD_DIM] = mixture.astype(out_ref.dtype)


def attend(first, parents, queries, keys, values, far, first_head, heads, after):
    rows = queries.shape[0]
    key_count = PATH + SEG_LEN + SEG_LEN // 2
    return pl.pallas_call(
        functools.partial(attend_kernel, first_head, heads),
        out_shape=jax.ShapeDtypeStruct((rows, heads * HEAD_DIM), jnp.bfloat16),
        in_specs=[SMEM, SMEM] + [VMEM] * 4 + [ANY] * len(after),
        out_specs=VMEM,
        scratch_shapes=[pltpu.VMEM((PATH, 2 * HEAD_DIM), jnp.bfloat16)] * 2,
        compiler_params=pltpu.CompilerParams(vmem_limit_bytes=ATTEND_VMEM),
        cost_estimate=pl.CostEstimate(
            flops=heads * rows * key_count * HEAD_DIM * 10,
            bytes_accessed=heads * rows * HEAD_DIM * 4 + 8 * PATH * HEAD_DIM,
            transcendentals=heads * rows * key_count,
        ),
        name="attend",
    )(first, parents, queries, keys, values, far, *after)


def near_kernel(
    depths, counts, starts_ref, weight_ref, *refs
):
    count = sum(counts)
    parts = refs[:count]
    out_ref, last_ref, held_ref, tile_ref, sem, last_sem = refs[count:]
    width = out_ref.shape[1]
    tiles = width // TILE

    def fetch(n, g):
        columns = pl.ds(n * TILE, TILE)
        rows = pl.ds(pl.multiple_of(starts_ref[g], 2 * HEAD_DIM), depths[g])
        at = sum(depths[:g])
        return pltpu.make_async_copy(
            weight_ref.at[rows, columns], tile_ref.at[n, pl.ds(at, depths[g])], sem.at[n, g]
        )

    def fetch_last(i):
        depth = last_ref.shape[0] // 2
        at = starts_ref[2 + i] + depths[2]
        rows = pl.ds(pl.multiple_of(at, HEAD_DIM), depth)
        return pltpu.make_async_copy(
            weight_ref.at[rows], last_ref.at[pl.ds(i * depth, depth)], last_sem.at[i]
        )

    groups = range(len(depths))
    for n in range(tiles):
        for g in groups:
            fetch(n, g).start()
    for i in range(2):
        fetch_last(i).start()
    at = 0
    for part in parts:
        held_ref[:, at : at + part.shape[1]] = part[...]
        at += part.shape[1]
    for n in range(tiles):
        for g in groups:
            fetch(n, g).wait()
        out_ref[:, n * TILE : (n + 1) * TILE] = jnp.dot(
            held_ref[...], tile_ref[n], preferred_element_type=jnp.float32
        )
    for i in range(2):
        fetch_last(i).wait()


def near_project(groups, starts, weight):
    parts = [part for group in groups for part in group]
    rows = parts[0].shape[0]
    depths = [sum(part.shape[1] for part in group) for group in groups]
    depth = sum(depths)
    full, width = weight.shape
    left = 2 * (depths[0] - depths[2])
    return pl.pallas_call(
        functools.partial(near_kernel, depths, [len(group) for group in groups]),
        out_shape=(
            jax.ShapeDtypeStruct((rows, width), jnp.float32),
            jax.ShapeDtypeStruct((left, width), weight.dtype),
        ),
        in_specs=[SMEM, HBM] + [VMEM] * len(parts),
        out_specs=(VMEM, VMEM),
        scratch_shapes=[
            pltpu.VMEM((rows, depth), weight.dtype),
            pltpu.VMEM((width // TILE, depth, TILE), weight.dtype),
            pltpu.SemaphoreType.DMA((width // TILE, len(groups))),
            pltpu.SemaphoreType.DMA((2,)),
        ],
        compiler_params=pltpu.CompilerParams(vmem_limit_bytes=PROJECT_VMEM),
        cost_estimate=pl.CostEstimate(
            flops=2 * rows * depth * width,
            bytes_accessed=2 * (depth + left) * width + 2 * rows * depth + 4 * rows * width,
            transcendentals=0,
        ),
        name="near_project",
    )(starts, in_hbm(weight), *parts)


def last_kernel(across_ref, corner_ref, weight_ref, base_ref, out_ref):
    depth = across_ref.shape[1]
    for column in range(0, out_ref.shape[1], TILE):
        columns = slice(column, column + TILE)
        total = base_ref[:, columns]
        for i, part_ref in enumerate([across_ref, corner_ref]):
            total = total + jnp.dot(
                part_ref[...],
                weight_ref[i * depth : (i + 1) * depth, columns],
                preferred_element_type=jnp.float32,
            )
        out_ref[:, columns] = total.astype(out_ref.dtype)


def last_project(across, corner, weight, base):
    rows, depth = across.shape
    width = weight.shape[1]
    return pl.pallas_call(
        last_kernel,
        out_shape=jax.ShapeDtypeStruct((rows, width), jnp.bfloat16),
        in_specs=[VMEM] * 4,
        out_specs=VMEM,
        compiler_params=pltpu.CompilerParams(vmem_limit_bytes=LAST_VMEM),
        cost_estimate=pl.CostEstimate(
            flops=4 * rows * depth * width,
            bytes_accessed=4 * depth * (rows + width) + 6 * rows * width,
            transcendentals=0,
        ),
        name="last_project",
    )(across, corner, weight, base)


def swap(part, bit):
    size = lax.axis_size("tensor")
    return lax.ppermute(part, "tensor", [(i, i ^ bit) for i in range(size)])


def trade(pieces):
    devices = lax.axis_size("dp")
    rows = [list(range(at, at + ROW)) for at in range(0, devices, ROW)]
    return lax.all_to_all(pieces, "dp", 0, 0, tiled=True, axis_index_groups=rows)


def onward(piece, step):
    devices = lax.axis_size("dp")
    return lax.ppermute(piece, "dp", [(i, (i + step) % devices) for i in range(devices)])


def per_device(queries, key_proj, value_proj, out_weight, parents):
    me = lax.axis_index("tensor")
    first = (lax.axis_index("dp") * 2).astype(jnp.int32).reshape(1)
    pieces = trade(pack(key_proj, value_proj)).reshape(ROW_SEGS, 2 * PIECE, HEAD_DIM)
    to_next, to_second = carry_out(first, parents, pieces)
    inside = pick(first, parents, pieces)
    far = trade(merge(*inside, onward(to_next, ROW), onward(to_second, 2 * ROW)))

    sizes = [1, 2, 2, 3]
    own, across, head = [], [], 0
    for c, size in enumerate(sizes):
        after = [across[c - 2]] if c >= 2 else []
        own.append(
            attend(first, parents, queries, key_proj, value_proj, far, head, size, after)
        )
        across.append(swap(own[c], 2))
        head += size
    beside = [swap(part, 1) for part in own]
    corner = [swap(part, 1) for part in across[:-1]]
    starts = jnp.stack([me, me ^ 1, me ^ 2, me ^ 3]) * queries.shape[1]
    near, weight = near_project([own, beside, across[:-1], corner], starts, out_weight)
    last, near = lax.optimization_barrier((across[-1], near))
    return last_project(last, swap(last, 1), weight, near)


def solution(mesh):
    placed = (P("dp", "tensor"), P("dp", "tensor"), P("dp", "tensor"), P(None, "tensor"), P())
    return jax.shard_map(
        per_device, mesh=mesh, in_specs=placed, out_specs=P("dp", "tensor"), check_vma=False
    )
```

```python
import functools
import math

import jax
import jax.numpy as jnp
from jax import lax
from jax.experimental import pallas as pl
from jax.experimental.pallas import tpu as pltpu
from jax.sharding import PartitionSpec as P

HEAD_DIM = 128
SEG_LEN = 256
LEVELS = 4
ROW = 8
ROW_SEGS = 2 * ROW
PIECE = SEG_LEN // ROW
PATH = LEVELS * SEG_LEN
STACK = LEVELS * PIECE
MASKED = -1e30
EXP2_SCALE = math.log2(math.e) * HEAD_DIM ** (-0.5)
SMALL_VMEM = 6 * 1024 * 1024
ATTEND_VMEM = 18 * 1024 * 1024
PROJECT_VMEM = 14 * 1024 * 1024
LAST_VMEM = 10 * 1024 * 1024
HOLD_VMEM = 14 * 1024 * 1024
TILE = 256

VMEM = pl.BlockSpec(memory_space=pltpu.VMEM)
SMEM = pl.BlockSpec(memory_space=pltpu.SMEM)
ANY = pl.BlockSpec(memory_space=pl.ANY)
HBM = pl.BlockSpec(memory_space=pltpu.HBM)
FLAG_ROWS = 16


def in_hbm(array):
    return pltpu.with_memory_space_constraint(array, pltpu.HBM)


def in_vmem(array):
    return pltpu.with_memory_space_constraint(array, pltpu.VMEM)


def path_of(parents_ref, seg):
    path = [parents_ref[seg]]
    for _ in range(LEVELS - 1):
        up = parents_ref[jnp.maximum(path[-1], 0)]
        path.append(jnp.where(path[-1] >= 0, up, -1))
    depth = sum((p >= 0).astype(jnp.int32) for p in path)
    return path, depth


def level_of(path, depth, level):
    found = jnp.int32(0)
    for up in range(LEVELS):
        found = jnp.where(depth - 1 - up == level, path[up], found)
    return found


def pack_kernel(key_ref, value_ref, piece_ref, held_ref, sem):
    copies = [
        pltpu.make_async_copy(source, held_ref.at[i], sem.at[i])
        for i, source in enumerate([key_ref, value_ref])
    ]
    for copy in copies:
        copy.start()
    for i, copy in enumerate(copies):
        copy.wait()
        for piece in range(ROW):
            for seg in range(2):
                rows = pl.ds(seg * SEG_LEN + piece * PIECE, PIECE)
                piece_ref[piece, seg, i * PIECE : (i + 1) * PIECE] = held_ref[i, rows]


def pack(keys, values):
    return pl.pallas_call(
        pack_kernel,
        out_shape=jax.ShapeDtypeStruct((ROW, 2, 2 * PIECE, HEAD_DIM), keys.dtype),
        in_specs=[HBM, HBM],
        out_specs=VMEM,
        scratch_shapes=[pltpu.VMEM((2,) + keys.shape, keys.dtype), pltpu.SemaphoreType.DMA((2,))],
        compiler_params=pltpu.CompilerParams(vmem_limit_bytes=SMALL_VMEM),
        cost_estimate=pl.CostEstimate(flops=0, bytes_accessed=1 << 19, transcendentals=0),
        name="pack",
    )(in_hbm(keys), in_hbm(values))


def row_start(first_ref):
    return (first_ref[0] // ROW_SEGS) * ROW_SEGS


def carry_kernel(first_ref, parents_ref, pieces_ref, _, next_ref, second_ref):
    base = row_start(first_ref)
    last = parents_ref.shape[0] - 1

    def held(path, depth, level):
        return pieces_ref[jnp.clip(level_of(path, depth, level) - base, 0, ROW_SEGS - 1)]

    path, depth = path_of(parents_ref, jnp.minimum(base + ROW_SEGS, last))
    for level in range(LEVELS):
        next_ref[level] = held(path, depth, level)
    path, depth = path_of(parents_ref, jnp.minimum(base + 2 * ROW_SEGS, last))
    second_ref[0] = held(path, depth, 0)


def carry_out(first, parents, pieces, after):
    shape = lambda n: jax.ShapeDtypeStruct((n,) + pieces.shape[1:], pieces.dtype)
    return pl.pallas_call(
        carry_kernel,
        out_shape=(shape(LEVELS), shape(1)),
        in_specs=[SMEM, SMEM, VMEM, ANY],
        out_specs=(VMEM, VMEM),
        compiler_params=pltpu.CompilerParams(vmem_limit_bytes=SMALL_VMEM),
        cost_estimate=pl.CostEstimate(flops=0, bytes_accessed=1 << 18, transcendentals=0),
        name="carry_out",
    )(first, parents, pieces, after)


def pick_kernel(first_ref, parents_ref, pieces_ref, inside_ref, next_ref, second_ref):
    base = row_start(first_ref)
    ones = lambda on: jnp.full((FLAG_ROWS, HEAD_DIM), on, jnp.float32).astype(jnp.bfloat16)
    for target in range(ROW):
        path, depth = path_of(parents_ref, base + 2 * target)
        for level in range(LEVELS):
            seg = level_of(path, depth, level)
            within = seg >= base
            piece = pieces_ref[jnp.maximum(seg - base, 0)]
            inside_ref[target, level] = jnp.where(within, piece, jnp.zeros_like(piece))
            before = jnp.logical_and(seg < base, seg >= base - ROW_SEGS)
            next_ref[target, level] = ones(jnp.where(before, 1.0, 0.0))
            if level == 0:
                second_ref[target] = ones(jnp.where(seg < base - ROW_SEGS, 1.0, 0.0))


def pick(first, parents, pieces):
    shape = lambda *dims: jax.ShapeDtypeStruct(dims, pieces.dtype)
    return pl.pallas_call(
        pick_kernel,
        out_shape=(
            shape(ROW, LEVELS, *pieces.shape[1:]),
            shape(ROW, LEVELS, FLAG_ROWS, HEAD_DIM),
            shape(ROW, FLAG_ROWS, HEAD_DIM),
        ),
        in_specs=[SMEM, SMEM, VMEM],
        out_specs=(VMEM, VMEM, VMEM),
        compiler_params=pltpu.CompilerParams(vmem_limit_bytes=SMALL_VMEM),
        cost_estimate=pl.CostEstimate(flops=0, bytes_accessed=1 << 20, transcendentals=0),
        name="pick",
    )(first, parents, pieces)


def merge_kernel(inside_ref, on_next_ref, on_second_ref, next_ref, second_ref, picked_ref):
    for level in range(LEVELS):
        for at in range(0, 2 * PIECE, FLAG_ROWS):
            rows = pl.ds(at, FLAG_ROWS)
            carried = next_ref[level, rows]
            older = second_ref[0, rows]
            for target in range(ROW):
                total = inside_ref[target, level, rows] + carried * on_next_ref[target, level]
                if level == 0:
                    total = total + older * on_second_ref[target]
                picked_ref[target, level, rows] = total


def merge(inside, on_next, on_second, carried, second):
    return pl.pallas_call(
        merge_kernel,
        out_shape=jax.ShapeDtypeStruct(inside.shape, inside.dtype),
        in_specs=[VMEM] * 5,
        out_specs=VMEM,
        compiler_params=pltpu.CompilerParams(vmem_limit_bytes=SMALL_VMEM),
        cost_estimate=pl.CostEstimate(flops=0, bytes_accessed=1 << 20, transcendentals=0),
        name="merge",
    )(inside, on_next, on_second, carried, second)


def attend_kernel(
    first_head, heads, first_ref, parents_ref, query_ref, key_ref, value_ref, far_ref, *refs
):
    out_ref, path_key_ref, path_value_ref = refs[-3:]
    first = first_ref[0]
    _, depth0 = path_of(parents_ref, first)
    _, depth1 = path_of(parents_ref, first + 1)
    follows = jnp.where(parents_ref[first + 1] == first, 0.0, MASKED)

    def scores_of(query, keys):
        return lax.dot_general(
            query, keys, (((1,), (1,)), ((), ())), preferred_element_type=jnp.float32
        )

    def with_ones(values):
        return jnp.concatenate([values, jnp.ones_like(values)], axis=1)

    for piece in range(ROW):
        for level in range(LEVELS):
            rows = pl.ds(piece * STACK + level * PIECE, PIECE)
            path_key_ref[rows, :HEAD_DIM] = far_ref[piece, level, :PIECE]
            path_value_ref[rows, :HEAD_DIM] = far_ref[piece, level, PIECE:]
    path_value_ref[:, HEAD_DIM:] = jnp.ones((PATH, HEAD_DIM), jnp.bfloat16)
    row = lax.broadcasted_iota(jnp.int32, (PATH, HEAD_DIM), 0)
    lane = lax.broadcasted_iota(jnp.int32, (PATH, HEAD_DIM), 1)
    level = lax.rem(row // PIECE, LEVELS)
    limit = jnp.where(lane == 0, depth0, jnp.where(lane == 1, jnp.minimum(depth0, depth1), LEVELS))
    path_key_ref[:, HEAD_DIM:] = jnp.where(level < limit, 0.0, MASKED).astype(jnp.bfloat16)
    path_keys, path_values = path_key_ref[...], path_value_ref[...]

    rows = lax.broadcasted_iota(jnp.int32, (2 * SEG_LEN, HEAD_DIM), 0)
    lanes = lax.broadcasted_iota(jnp.int32, (2 * SEG_LEN, HEAD_DIM), 1)
    marks = (lanes == rows // SEG_LEN).astype(jnp.float32).astype(jnp.bfloat16)
    causal = lax.broadcasted_iota(jnp.int32, (SEG_LEN, SEG_LEN), 1) <= lax.broadcasted_iota(
        jnp.int32, (SEG_LEN, SEG_LEN), 0
    )
    halves = [slice(0, SEG_LEN), slice(SEG_LEN, 2 * SEG_LEN)]
    own_values = [with_ones(value_ref[half]) for half in halves]
    for head in range(heads):
        at = (first_head + head) * HEAD_DIM
        query = query_ref[:, at : at + HEAD_DIM]
        path_scores = scores_of(jnp.concatenate([query, marks], axis=1), path_keys)
        own = [
            [(jnp.where(causal, scores_of(query[half], key_ref[half]), MASKED), values)]
            for half, values in zip(halves, own_values)
        ]
        own[1].append((scores_of(query[halves[1]], key_ref[halves[0]]) + follows, own_values[0]))
        path_weights, own_parts = [], []
        for half, blocks in zip(halves, own):
            row_max = functools.reduce(
                jnp.maximum,
                [jnp.max(s, axis=1, keepdims=True) for s, _ in blocks]
                + [jnp.max(path_scores[half], axis=1, keepdims=True)],
            )
            weigh = lambda s: jnp.exp2((s - row_max) * EXP2_SCALE).astype(jnp.bfloat16)
            path_weights.append(weigh(path_scores[half]))
            own_parts.append(
                sum(
                    jnp.dot(weigh(s), values, preferred_element_type=jnp.float32)
                    for s, values in blocks
                )
            )
        total = jnp.dot(
            jnp.concatenate(path_weights, axis=0), path_values, preferred_element_type=jnp.float32
        ) + jnp.concatenate(own_parts, axis=0)
        mixture = total[:, :HEAD_DIM] / total[:, HEAD_DIM:]
        out_ref[:, head * HEAD_DIM : (head + 1) * HEAD_DIM] = mixture.astype(out_ref.dtype)


def attend(first, parents, queries, keys, values, far, first_head, heads, after):
    rows = queries.shape[0]
    key_count = PATH + SEG_LEN + SEG_LEN // 2
    return pl.pallas_call(
        functools.partial(attend_kernel, first_head, heads),
        out_shape=jax.ShapeDtypeStruct((rows, heads * HEAD_DIM), jnp.bfloat16),
        in_specs=[SMEM, SMEM] + [VMEM] * 4 + [ANY] * len(after),
        out_specs=VMEM,
        scratch_shapes=[pltpu.VMEM((PATH, 2 * HEAD_DIM), jnp.bfloat16)] * 2,
        compiler_params=pltpu.CompilerParams(vmem_limit_bytes=ATTEND_VMEM),
        cost_estimate=pl.CostEstimate(
            flops=heads * rows * key_count * HEAD_DIM * 10,
            bytes_accessed=heads * rows * HEAD_DIM * 4 + 8 * PATH * HEAD_DIM,
            transcendentals=heads * rows * key_count,
        ),
        name="attend",
    )(first, parents, queries, keys, values, far, *after)


def hold_kernel(me_ref, weight_ref, held_ref, sem):
    block = weight_ref.shape[0] // 4
    copies = []
    for bit in range(4):
        rows = pl.ds(pl.multiple_of((me_ref[0] ^ bit) * block, block), block)
        copies.append(
            pltpu.make_async_copy(
                weight_ref.at[rows], held_ref.at[pl.ds(bit * block, block)], sem.at[bit]
            )
        )
    for copy in copies:
        copy.start()
    for copy in copies:
        copy.wait()


def hold(me, weight):
    return pl.pallas_call(
        hold_kernel,
        out_shape=pltpu.VMEM(weight.shape, weight.dtype),
        in_specs=[SMEM, HBM],
        out_specs=VMEM,
        scratch_shapes=[pltpu.SemaphoreType.DMA((4,))],
        compiler_params=pltpu.CompilerParams(vmem_limit_bytes=HOLD_VMEM),
        cost_estimate=pl.CostEstimate(flops=0, bytes_accessed=4 * weight.size, transcendentals=0),
        name="hold",
    )(me, in_hbm(weight))


def near_kernel(counts, weight_ref, *refs):
    count = sum(counts)
    parts, (out_ref, held_ref) = refs[:count], refs[count:]
    block = weight_ref.shape[0] // 4
    at = 0
    for part in parts:
        held_ref[:, at : at + part.shape[1]] = part[...]
        at += part.shape[1]
    split = sum(part.shape[1] for part in parts[: -counts[-1]])
    for column in range(0, out_ref.shape[1], TILE):
        columns = slice(column, column + TILE)
        out_ref[:, columns] = jnp.dot(
            held_ref[:, :split], weight_ref[:split, columns], preferred_element_type=jnp.float32
        ) + jnp.dot(
            held_ref[:, split:],
            weight_ref[3 * block : 3 * block + at - split, columns],
            preferred_element_type=jnp.float32,
        )


def near_project(groups, weight):
    parts = [part for group in groups for part in group]
    rows = parts[0].shape[0]
    depth = sum(part.shape[1] for part in parts)
    width = weight.shape[1]
    return pl.pallas_call(
        functools.partial(near_kernel, [len(group) for group in groups]),
        out_shape=jax.ShapeDtypeStruct((rows, width), jnp.float32),
        in_specs=[VMEM] * (1 + len(parts)),
        out_specs=VMEM,
        scratch_shapes=[pltpu.VMEM((rows, depth), weight.dtype)],
        compiler_params=pltpu.CompilerParams(vmem_limit_bytes=PROJECT_VMEM),
        cost_estimate=pl.CostEstimate(
            flops=rows * depth * width // 4,
            bytes_accessed=2 * depth * rows,
            transcendentals=0,
        ),
        name="near_project",
    )(in_vmem(weight), *parts)


def last_kernel(across_ref, corner_ref, weight_ref, base_ref, out_ref):
    depth = across_ref.shape[1]
    block = weight_ref.shape[0] // 4
    for column in range(0, out_ref.shape[1], TILE):
        columns = slice(column, column + TILE)
        total = base_ref[:, columns]
        for end, part_ref in [(3 * block, across_ref), (4 * block, corner_ref)]:
            total = total + jnp.dot(
                part_ref[...],
                weight_ref[end - depth : end, columns],
                preferred_element_type=jnp.float32,
            )
        out_ref[:, columns] = total.astype(out_ref.dtype)


def last_project(across, corner, weight, base):
    rows, depth = across.shape
    width = weight.shape[1]
    return pl.pallas_call(
        last_kernel,
        out_shape=jax.ShapeDtypeStruct((rows, width), jnp.bfloat16),
        in_specs=[VMEM] * 4,
        out_specs=VMEM,
        compiler_params=pltpu.CompilerParams(vmem_limit_bytes=LAST_VMEM),
        cost_estimate=pl.CostEstimate(
            flops=4 * rows * depth * width,
            bytes_accessed=4 * depth * (rows + width) + 6 * rows * width,
            transcendentals=0,
        ),
        name="last_project",
    )(across, corner, in_vmem(weight), base)


def swap(part, bit):
    size = lax.axis_size("tensor")
    return lax.ppermute(part, "tensor", [(i, i ^ bit) for i in range(size)])


def trade(pieces):
    devices = lax.axis_size("dp")
    rows = [list(range(at, at + ROW)) for at in range(0, devices, ROW)]
    return lax.all_to_all(pieces, "dp", 0, 0, tiled=True, axis_index_groups=rows)


def onward(piece, step):
    devices = lax.axis_size("dp")
    return lax.ppermute(piece, "dp", [(i, (i + step) % devices) for i in range(devices)])


def per_device(queries, key_proj, value_proj, out_weight, parents):
    me = lax.axis_index("tensor")
    first = (lax.axis_index("dp") * 2).astype(jnp.int32).reshape(1)
    pieces = trade(pack(key_proj, value_proj)).reshape(ROW_SEGS, 2 * PIECE, HEAD_DIM)
    weight = hold(me.astype(jnp.int32).reshape(1), out_weight)
    to_next, to_second = carry_out(first, parents, pieces, weight)
    inside = pick(first, parents, pieces)
    far = trade(merge(*inside, onward(to_next, ROW), onward(to_second, 2 * ROW)))

    sizes = [1, 2, 2, 3]
    own, across, head = [], [], 0
    for c, size in enumerate(sizes):
        after = [across[c - 2]] if c >= 2 else []
        own.append(
            attend(first, parents, queries, key_proj, value_proj, far, head, size, after)
        )
        across.append(swap(own[c], 2))
        head += size
    beside = [swap(part, 1) for part in own]
    corner = [swap(part, 1) for part in across[:-1]]
    near = near_project([own, beside, across[:-1], corner], weight)
    last, near = lax.optimization_barrier((across[-1], near))
    return last_project(last, swap(last, 1), weight, near)


def solution(mesh):
    placed = (P("dp", "tensor"), P("dp", "tensor"), P("dp", "tensor"), P(None, "tensor"), P())
    return jax.shard_map(
        per_device, mesh=mesh, in_specs=placed, out_specs=P("dp", "tensor"), check_vma=False
    )
```

```python
import functools
import math

import jax
import jax.numpy as jnp
from jax import lax
from jax.experimental import pallas as pl
from jax.experimental.pallas import tpu as pltpu
from jax.sharding import PartitionSpec as P

HEAD_DIM = 128
SEG_LEN = 256
LEVELS = 4
ROW = 8
ROW_SEGS = 2 * ROW
PIECE = SEG_LEN // ROW
PATH = LEVELS * SEG_LEN
STACK = LEVELS * PIECE
MASKED = -1e30
EXP2_SCALE = math.log2(math.e) * HEAD_DIM ** (-0.5)
SMALL_VMEM = 6 * 1024 * 1024
ATTEND_VMEM = 18 * 1024 * 1024
PROJECT_VMEM = 14 * 1024 * 1024
TILE = 256
TOGETHER = 2

VMEM = pl.BlockSpec(memory_space=pltpu.VMEM)
SMEM = pl.BlockSpec(memory_space=pltpu.SMEM)
HBM = pl.BlockSpec(memory_space=pltpu.HBM)
FLAG_ROWS = 16


def in_hbm(array):
    return pltpu.with_memory_space_constraint(array, pltpu.HBM)


def in_vmem(array):
    return pltpu.with_memory_space_constraint(array, pltpu.VMEM)


def path_of(parents_ref, seg):
    path = [parents_ref[seg]]
    for _ in range(LEVELS - 1):
        up = parents_ref[jnp.maximum(path[-1], 0)]
        path.append(jnp.where(path[-1] >= 0, up, -1))
    depth = sum((p >= 0).astype(jnp.int32) for p in path)
    return path, depth


def level_of(path, depth, level):
    found = jnp.int32(0)
    for up in range(LEVELS):
        found = jnp.where(depth - 1 - up == level, path[up], found)
    return found


def pack_kernel(key_ref, value_ref, piece_ref, held_ref, sem):
    copies = [
        pltpu.make_async_copy(source, held_ref.at[i], sem.at[i])
        for i, source in enumerate([key_ref, value_ref])
    ]
    for copy in copies:
        copy.start()
    for i, copy in enumerate(copies):
        copy.wait()
        for piece in range(ROW):
            for seg in range(2):
                rows = pl.ds(seg * SEG_LEN + piece * PIECE, PIECE)
                piece_ref[piece, seg, i * PIECE : (i + 1) * PIECE] = held_ref[i, rows]


def pack(keys, values):
    return pl.pallas_call(
        pack_kernel,
        out_shape=(
            jax.ShapeDtypeStruct((ROW, 2, 2 * PIECE, HEAD_DIM), keys.dtype),
            jax.ShapeDtypeStruct((2,) + keys.shape, keys.dtype),
        ),
        in_specs=[HBM, HBM],
        out_specs=(VMEM, VMEM),
        scratch_shapes=[pltpu.SemaphoreType.DMA((2,))],
        compiler_params=pltpu.CompilerParams(vmem_limit_bytes=SMALL_VMEM),
        cost_estimate=pl.CostEstimate(flops=0, bytes_accessed=1 << 19, transcendentals=0),
        name="pack",
    )(in_hbm(keys), in_hbm(values))


def row_start(first_ref):
    return (first_ref[0] // ROW_SEGS) * ROW_SEGS


def carry_kernel(first_ref, parents_ref, pieces_ref, next_ref, second_ref):
    base = row_start(first_ref)
    last = parents_ref.shape[0] - 1

    def held(path, depth, level):
        return pieces_ref[jnp.clip(level_of(path, depth, level) - base, 0, ROW_SEGS - 1)]

    path, depth = path_of(parents_ref, jnp.minimum(base + ROW_SEGS, last))
    for level in range(LEVELS):
        next_ref[level] = held(path, depth, level)
    path, depth = path_of(parents_ref, jnp.minimum(base + 2 * ROW_SEGS, last))
    second_ref[0] = held(path, depth, 0)


def carry_out(first, parents, pieces):
    shape = lambda n: jax.ShapeDtypeStruct((n,) + pieces.shape[1:], pieces.dtype)
    return pl.pallas_call(
        carry_kernel,
        out_shape=(shape(LEVELS), shape(1)),
        in_specs=[SMEM, SMEM, VMEM],
        out_specs=(VMEM, VMEM),
        compiler_params=pltpu.CompilerParams(vmem_limit_bytes=SMALL_VMEM),
        cost_estimate=pl.CostEstimate(flops=0, bytes_accessed=1 << 18, transcendentals=0),
        name="carry_out",
    )(first, parents, pieces)


def pick_kernel(first_ref, parents_ref, pieces_ref, inside_ref, next_ref, second_ref):
    base = row_start(first_ref)
    ones = lambda on: jnp.full((FLAG_ROWS, HEAD_DIM), on, jnp.float32).astype(jnp.bfloat16)
    for target in range(ROW):
        path, depth = path_of(parents_ref, base + 2 * target)
        for level in range(LEVELS):
            seg = level_of(path, depth, level)
            within = seg >= base
            piece = pieces_ref[jnp.maximum(seg - base, 0)]
            inside_ref[target, level] = jnp.where(within, piece, jnp.zeros_like(piece))
            before = jnp.logical_and(seg < base, seg >= base - ROW_SEGS)
            next_ref[target, level] = ones(jnp.where(before, 1.0, 0.0))
            if level == 0:
                second_ref[target] = ones(jnp.where(seg < base - ROW_SEGS, 1.0, 0.0))


def pick(first, parents, pieces):
    shape = lambda *dims: jax.ShapeDtypeStruct(dims, pieces.dtype)
    return pl.pallas_call(
        pick_kernel,
        out_shape=(
            shape(ROW, LEVELS, *pieces.shape[1:]),
            shape(ROW, LEVELS, FLAG_ROWS, HEAD_DIM),
            shape(ROW, FLAG_ROWS, HEAD_DIM),
        ),
        in_specs=[SMEM, SMEM, VMEM],
        out_specs=(VMEM, VMEM, VMEM),
        compiler_params=pltpu.CompilerParams(vmem_limit_bytes=SMALL_VMEM),
        cost_estimate=pl.CostEstimate(flops=0, bytes_accessed=1 << 20, transcendentals=0),
        name="pick",
    )(first, parents, pieces)


def merge_kernel(inside_ref, on_next_ref, on_second_ref, next_ref, second_ref, picked_ref):
    for level in range(LEVELS):
        for at in range(0, 2 * PIECE, FLAG_ROWS):
            rows = pl.ds(at, FLAG_ROWS)
            carried = next_ref[level, rows]
            older = second_ref[0, rows]
            for target in range(ROW):
                total = inside_ref[target, level, rows] + carried * on_next_ref[target, level]
                if level == 0:
                    total = total + older * on_second_ref[target]
                picked_ref[target, level, rows] = total


def merge(inside, on_next, on_second, carried, second):
    return pl.pallas_call(
        merge_kernel,
        out_shape=jax.ShapeDtypeStruct(inside.shape, inside.dtype),
        in_specs=[VMEM] * 5,
        out_specs=VMEM,
        compiler_params=pltpu.CompilerParams(vmem_limit_bytes=SMALL_VMEM),
        cost_estimate=pl.CostEstimate(flops=0, bytes_accessed=1 << 20, transcendentals=0),
        name="merge",
    )(inside, on_next, on_second, carried, second)


def attend_kernel(first_ref, parents_ref, query_ref, pair_ref, far_ref, *refs):
    key_ref, value_ref = pair_ref.at[0], pair_ref.at[1]
    bring = len(refs) > 3
    if bring:
        me_ref, weight_ref, out_ref, held_ref, path_key_ref, path_value_ref, near_ref, sem = refs
        ready = pltpu.make_async_copy(query_ref, near_ref, sem.at[4])
        copies = weight_copies(me_ref, weight_ref, held_ref, sem)
        for copy in [ready] + copies:
            copy.start()
        query_ref = near_ref
    else:
        out_ref, path_key_ref, path_value_ref = refs
    first = first_ref[0]
    _, depth0 = path_of(parents_ref, first)
    _, depth1 = path_of(parents_ref, first + 1)
    follows = jnp.where(parents_ref[first + 1] == first, 0.0, MASKED)

    def scores_of(query, keys):
        return lax.dot_general(
            query, keys, (((1,), (1,)), ((), ())), preferred_element_type=jnp.float32
        )

    def with_ones(values):
        return jnp.concatenate([values, jnp.ones_like(values)], axis=1)

    for piece in range(ROW):
        for level in range(LEVELS):
            rows = pl.ds(piece * STACK + level * PIECE, PIECE)
            path_key_ref[rows, :HEAD_DIM] = far_ref[piece, level, :PIECE]
            path_value_ref[rows, :HEAD_DIM] = far_ref[piece, level, PIECE:]
    path_value_ref[:, HEAD_DIM:] = jnp.ones((PATH, HEAD_DIM), jnp.bfloat16)
    row = lax.broadcasted_iota(jnp.int32, (PATH, HEAD_DIM), 0)
    lane = lax.broadcasted_iota(jnp.int32, (PATH, HEAD_DIM), 1)
    level = lax.rem(row // PIECE, LEVELS)
    limit = jnp.where(lane == 0, depth0, jnp.where(lane == 1, jnp.minimum(depth0, depth1), LEVELS))
    path_key_ref[:, HEAD_DIM:] = jnp.where(level < limit, 0.0, MASKED).astype(jnp.bfloat16)

    rows = lax.broadcasted_iota(jnp.int32, (2 * SEG_LEN, HEAD_DIM), 0)
    lanes = lax.broadcasted_iota(jnp.int32, (2 * SEG_LEN, HEAD_DIM), 1)
    marks = (lanes == rows // SEG_LEN).astype(jnp.float32).astype(jnp.bfloat16)
    causal = lax.broadcasted_iota(jnp.int32, (SEG_LEN, SEG_LEN), 1) <= lax.broadcasted_iota(
        jnp.int32, (SEG_LEN, SEG_LEN), 0
    )
    halves = [slice(0, SEG_LEN), slice(SEG_LEN, 2 * SEG_LEN)]

    def attend_head(query):
        path_scores = scores_of(jnp.concatenate([query, marks], axis=1), path_key_ref[...])
        own_values = [with_ones(value_ref[half]) for half in halves]
        own = [
            [(jnp.where(causal, scores_of(query[half], key_ref[half]), MASKED), values)]
            for half, values in zip(halves, own_values)
        ]
        own[1].append((scores_of(query[halves[1]], key_ref[halves[0]]) + follows, own_values[0]))
        path_weights, own_parts = [], []
        for half, blocks in zip(halves, own):
            row_max = functools.reduce(
                jnp.maximum,
                [jnp.max(s, axis=1, keepdims=True) for s, _ in blocks]
                + [jnp.max(path_scores[half], axis=1, keepdims=True)],
            )
            weigh = lambda s: jnp.exp2((s - row_max) * EXP2_SCALE).astype(jnp.bfloat16)
            path_weights.append(weigh(path_scores[half]))
            own_parts.append(
                sum(
                    jnp.dot(weigh(s), values, preferred_element_type=jnp.float32)
                    for s, values in blocks
                )
            )
        total = jnp.dot(
            jnp.concatenate(path_weights, axis=0),
            path_value_ref[...],
            preferred_element_type=jnp.float32,
        ) + jnp.concatenate(own_parts, axis=0)
        return (total[:, :HEAD_DIM] / total[:, HEAD_DIM:]).astype(out_ref.dtype)

    if bring:
        ready.wait()

    @pl.loop(0, query_ref.shape[1] // (TOGETHER * HEAD_DIM))
    def _(turn):
        for head in range(TOGETHER):
            at = pl.multiple_of((turn * TOGETHER + head) * HEAD_DIM, HEAD_DIM)
            out_ref[:, pl.ds(at, HEAD_DIM)] = attend_head(query_ref[:, pl.ds(at, HEAD_DIM)])

    if bring:
        for copy in copies:
            copy.wait()


def weight_copies(me_ref, weight_ref, held_ref, sem):
    block = weight_ref.shape[0] // 4
    copies = []
    for bit in range(4):
        rows = pl.ds(pl.multiple_of((me_ref[0] ^ bit) * block, block), block)
        copies.append(
            pltpu.make_async_copy(
                weight_ref.at[rows], held_ref.at[pl.ds(bit * block, block)], sem.at[bit]
            )
        )
    return copies


def attend(first, parents, queries, pair, far, bring):
    rows, width = queries.shape
    out_shape = [jax.ShapeDtypeStruct((rows, width), jnp.bfloat16)]
    in_specs = [SMEM, SMEM, HBM if bring else VMEM, VMEM, VMEM]
    scratch = [pltpu.VMEM((PATH, 2 * HEAD_DIM), jnp.bfloat16)] * 2
    if bring:
        weight = bring[1]
        bring = [bring[0], in_hbm(weight)]
        queries = in_hbm(queries)
        in_specs += [SMEM, HBM]
        out_shape.append(pltpu.VMEM(weight.shape, weight.dtype))
        scratch.append(pltpu.VMEM(queries.shape, queries.dtype))
        scratch.append(pltpu.SemaphoreType.DMA((5,)))
    pairs = rows * (PATH + SEG_LEN + SEG_LEN // 2) * width // HEAD_DIM
    return pl.pallas_call(
        attend_kernel,
        out_shape=out_shape,
        in_specs=in_specs,
        out_specs=[VMEM] * len(out_shape),
        scratch_shapes=scratch,
        compiler_params=pltpu.CompilerParams(vmem_limit_bytes=ATTEND_VMEM),
        cost_estimate=pl.CostEstimate(
            flops=pairs * HEAD_DIM * 10,
            bytes_accessed=rows * width * 4 + 8 * PATH * HEAD_DIM,
            transcendentals=pairs,
        ),
        name="attend",
    )(first, parents, queries, pair, far, *bring)


def project_kernel(spans, has_base, weight_ref, *refs):
    parts, out_ref = refs[: len(spans)], refs[-1]
    for column in range(0, out_ref.shape[1], TILE):
        columns = slice(column, column + TILE)
        total = refs[len(spans)][:, columns] if has_base else None
        for start, part_ref in zip(spans, parts):
            product = jnp.dot(
                part_ref[...],
                weight_ref[start : start + part_ref.shape[1], columns],
                preferred_element_type=jnp.float32,
            )
            total = product if total is None else total + product
        out_ref[:, columns] = total.astype(out_ref.dtype)


def project(parts, spans, weight, base, dtype):
    rows = parts[0].shape[0]
    depth = sum(part.shape[1] for part in parts)
    width = weight.shape[1]
    bases = [] if base is None else [base]
    return pl.pallas_call(
        functools.partial(project_kernel, spans, base is not None),
        out_shape=jax.ShapeDtypeStruct((rows, width), dtype),
        in_specs=[VMEM] * (1 + len(parts) + len(bases)),
        out_specs=VMEM,
        compiler_params=pltpu.CompilerParams(vmem_limit_bytes=PROJECT_VMEM),
        cost_estimate=pl.CostEstimate(
            flops=2 * rows * depth * width,
            bytes_accessed=2 * depth * rows,
            transcendentals=0,
        ),
        name="project",
    )(in_vmem(weight), *parts, *bases)


def swap(part, bit):
    size = lax.axis_size("tensor")
    return lax.ppermute(part, "tensor", [(i, i ^ bit) for i in range(size)])


def trade(pieces):
    devices = lax.axis_size("dp")
    rows = [list(range(at, at + ROW)) for at in range(0, devices, ROW)]
    return lax.all_to_all(pieces, "dp", 0, 0, tiled=True, axis_index_groups=rows)


def onward(piece, step):
    devices = lax.axis_size("dp")
    return lax.ppermute(piece, "dp", [(i, (i + step) % devices) for i in range(devices)])


def per_device(queries, key_proj, value_proj, out_weight, parents):
    me = lax.axis_index("tensor").astype(jnp.int32).reshape(1)
    first = (lax.axis_index("dp") * 2).astype(jnp.int32).reshape(1)
    packed, pair = pack(key_proj, value_proj)
    other_pair = swap(pair, 2)
    pieces = trade(packed).reshape(ROW_SEGS, 2 * PIECE, HEAD_DIM)
    pieces, other_pair = lax.optimization_barrier((pieces, other_pair))
    to_next, to_second = carry_out(first, parents, pieces)
    other_queries = swap(queries, 2)
    inside = pick(first, parents, pieces)
    far = trade(merge(*inside, onward(to_next, ROW), onward(to_second, 2 * ROW)))
    far, other_queries = lax.optimization_barrier((far, other_queries))

    other_far = swap(far, 2)
    own, weight = attend(first, parents, queries, pair, far, [me, out_weight])
    beside = swap(own, 1)
    width = queries.shape[1]
    total = project([own], [0], weight, None, jnp.float32)
    other_far, total = lax.optimization_barrier((other_far, total))
    [across] = attend(first, parents, other_queries, other_pair, other_far, [])
    corner = swap(across, 1)
    total = project([beside, across], [width, 2 * width], weight, total, jnp.float32)
    return project([corner], [3 * width], weight, total, jnp.bfloat16)


def solution(mesh):
    placed = (P("dp", "tensor"), P("dp", "tensor"), P("dp", "tensor"), P(None, "tensor"), P())
    return jax.shard_map(
        per_device, mesh=mesh, in_specs=placed, out_specs=P("dp", "tensor"), check_vma=False
    )
```

```python
import functools
import math

import jax
import jax.numpy as jnp
from jax import lax
from jax.experimental import pallas as pl
from jax.experimental.pallas import tpu as pltpu
from jax.sharding import PartitionSpec as P

HEAD_DIM = 128
SEG_LEN = 256
LEVELS = 4
ROW = 8
ROW_SEGS = 2 * ROW
PIECE = SEG_LEN // ROW
PATH = LEVELS * SEG_LEN
STACK = LEVELS * PIECE
MASKED = -1e30
EXP2_SCALE = math.log2(math.e) * HEAD_DIM ** (-0.5)
SMALL_VMEM = 6 * 1024 * 1024
ATTEND_VMEM = 18 * 1024 * 1024
PROJECT_VMEM = 14 * 1024 * 1024
TILE = 256

VMEM = pl.BlockSpec(memory_space=pltpu.VMEM)
SMEM = pl.BlockSpec(memory_space=pltpu.SMEM)
ANY = pl.BlockSpec(memory_space=pl.ANY)
HBM = pl.BlockSpec(memory_space=pltpu.HBM)
FLAG_ROWS = 16


def in_hbm(array):
    return pltpu.with_memory_space_constraint(array, pltpu.HBM)


def in_vmem(array):
    return pltpu.with_memory_space_constraint(array, pltpu.VMEM)


def path_of(parents_ref, seg):
    path = [parents_ref[seg]]
    for _ in range(LEVELS - 1):
        up = parents_ref[jnp.maximum(path[-1], 0)]
        path.append(jnp.where(path[-1] >= 0, up, -1))
    depth = sum((p >= 0).astype(jnp.int32) for p in path)
    return path, depth


def level_of(path, depth, level):
    found = jnp.int32(0)
    for up in range(LEVELS):
        found = jnp.where(depth - 1 - up == level, path[up], found)
    return found


def pack_kernel(key_ref, value_ref, piece_ref, held_ref, sem):
    copies = [
        pltpu.make_async_copy(source, held_ref.at[i], sem.at[i])
        for i, source in enumerate([key_ref, value_ref])
    ]
    for copy in copies:
        copy.start()
    for i, copy in enumerate(copies):
        copy.wait()
        for piece in range(ROW):
            for seg in range(2):
                rows = pl.ds(seg * SEG_LEN + piece * PIECE, PIECE)
                piece_ref[piece, seg, i * PIECE : (i + 1) * PIECE] = held_ref[i, rows]


def pack(keys, values):
    return pl.pallas_call(
        pack_kernel,
        out_shape=jax.ShapeDtypeStruct((ROW, 2, 2 * PIECE, HEAD_DIM), keys.dtype),
        in_specs=[HBM, HBM],
        out_specs=VMEM,
        scratch_shapes=[pltpu.VMEM((2,) + keys.shape, keys.dtype), pltpu.SemaphoreType.DMA((2,))],
        compiler_params=pltpu.CompilerParams(vmem_limit_bytes=SMALL_VMEM),
        cost_estimate=pl.CostEstimate(flops=0, bytes_accessed=1 << 19, transcendentals=0),
        name="pack",
    )(in_hbm(keys), in_hbm(values))


def row_start(first_ref):
    return (first_ref[0] // ROW_SEGS) * ROW_SEGS


def slot_of(seg):
    return seg ^ (ROW_SEGS - 2)


def bring_parents(source_ref, parents_ref, sem):
    copy = pltpu.make_async_copy(source_ref, parents_ref, sem)
    copy.start()
    copy.wait()


def carry_kernel(first_ref, source_ref, pieces_ref, next_ref, second_ref, parents_ref, sem):
    bring_parents(source_ref, parents_ref, sem)
    base = row_start(first_ref)
    last = parents_ref.shape[0] - 1

    def held(path, depth, level):
        return pieces_ref[slot_of(jnp.clip(level_of(path, depth, level) - base, 0, ROW_SEGS - 1))]

    path, depth = path_of(parents_ref, jnp.minimum(base + ROW_SEGS, last))
    for level in range(LEVELS):
        next_ref[level] = held(path, depth, level)
    path, depth = path_of(parents_ref, jnp.minimum(base + 2 * ROW_SEGS, last))
    second_ref[0] = held(path, depth, 0)


def carry_out(first, parents, pieces):
    shape = lambda n: jax.ShapeDtypeStruct((n,) + pieces.shape[1:], pieces.dtype)
    return pl.pallas_call(
        carry_kernel,
        out_shape=(shape(LEVELS), shape(1)),
        in_specs=[SMEM, HBM, VMEM],
        out_specs=(VMEM, VMEM),
        scratch_shapes=[pltpu.SMEM(parents.shape, parents.dtype), pltpu.SemaphoreType.DMA],
        compiler_params=pltpu.CompilerParams(vmem_limit_bytes=SMALL_VMEM),
        cost_estimate=pl.CostEstimate(flops=0, bytes_accessed=1 << 18, transcendentals=0),
        name="carry_out",
    )(first, in_hbm(parents), pieces)


def pick_kernel(
    first_ref, source_ref, pieces_ref, inside_ref, next_ref, second_ref, parents_ref, sem
):
    bring_parents(source_ref, parents_ref, sem)
    base = row_start(first_ref)
    ones = lambda on: jnp.full((FLAG_ROWS, HEAD_DIM), on, jnp.float32).astype(jnp.bfloat16)
    for target in range(ROW):
        path, depth = path_of(parents_ref, base + 2 * (ROW - 1 - target))
        for level in range(LEVELS):
            seg = level_of(path, depth, level)
            within = seg >= base
            piece = pieces_ref[slot_of(jnp.maximum(seg - base, 0))]
            inside_ref[target, level] = jnp.where(within, piece, jnp.zeros_like(piece))
            before = jnp.logical_and(seg < base, seg >= base - ROW_SEGS)
            next_ref[target, level] = ones(jnp.where(before, 1.0, 0.0))
            if level == 0:
                second_ref[target] = ones(jnp.where(seg < base - ROW_SEGS, 1.0, 0.0))


def pick(first, parents, pieces):
    shape = lambda *dims: jax.ShapeDtypeStruct(dims, pieces.dtype)
    return pl.pallas_call(
        pick_kernel,
        out_shape=(
            shape(ROW, LEVELS, *pieces.shape[1:]),
            shape(ROW, LEVELS, FLAG_ROWS, HEAD_DIM),
            shape(ROW, FLAG_ROWS, HEAD_DIM),
        ),
        in_specs=[SMEM, HBM, VMEM],
        out_specs=(VMEM, VMEM, VMEM),
        scratch_shapes=[pltpu.SMEM(parents.shape, parents.dtype), pltpu.SemaphoreType.DMA],
        compiler_params=pltpu.CompilerParams(vmem_limit_bytes=SMALL_VMEM),
        cost_estimate=pl.CostEstimate(flops=0, bytes_accessed=1 << 20, transcendentals=0),
        name="pick",
    )(first, in_hbm(parents), pieces)


def merge_kernel(inside_ref, on_next_ref, on_second_ref, next_ref, second_ref, picked_ref):
    for level in range(LEVELS):
        for at in range(0, 2 * PIECE, FLAG_ROWS):
            rows = pl.ds(at, FLAG_ROWS)
            carried = next_ref[level, rows]
            older = second_ref[0, rows]
            for target in range(ROW):
                total = inside_ref[target, level, rows] + carried * on_next_ref[target, level]
                if level == 0:
                    total = total + older * on_second_ref[target]
                picked_ref[target, level, rows] = total


def merge(inside, on_next, on_second, carried, second):
    return pl.pallas_call(
        merge_kernel,
        out_shape=jax.ShapeDtypeStruct(inside.shape, inside.dtype),
        in_specs=[VMEM] * 5,
        out_specs=VMEM,
        compiler_params=pltpu.CompilerParams(vmem_limit_bytes=SMALL_VMEM),
        cost_estimate=pl.CostEstimate(flops=0, bytes_accessed=1 << 20, transcendentals=0),
        name="merge",
    )(inside, on_next, on_second, carried, second)


def attend_kernel(first_head, bring, first_ref, *refs):
    sources, (far_ref, *refs) = refs[:4], refs[4:]
    if bring:
        me_ref, weight_ref = refs[:2]
        weight_sem = refs.pop()
        held_ref = refs.pop(-8)
    out_ref, path_key_ref, path_value_ref, parents_ref, query_ref, key_ref, value_ref, sem = refs[-8:]
    heads = query_ref.shape[1] // HEAD_DIM
    columns = pl.ds(first_head * HEAD_DIM, query_ref.shape[1])
    views = [sources[0], sources[1].at[:, columns], sources[2], sources[3]]
    fetches = [
        pltpu.make_async_copy(view, target, sem.at[i])
        for i, (view, target) in enumerate(zip(views, [parents_ref, query_ref, key_ref, value_ref]))
    ]
    copies = weight_copies(me_ref, weight_ref, held_ref, weight_sem) if bring else []
    for copy in fetches + copies:
        copy.start()

    def scores_of(query, keys):
        return lax.dot_general(
            query, keys, (((1,), (1,)), ((), ())), preferred_element_type=jnp.float32
        )

    def with_ones(values):
        return jnp.concatenate([values, jnp.ones_like(values)], axis=1)

    for piece in range(ROW):
        for level in range(LEVELS):
            rows = pl.ds(piece * STACK + level * PIECE, PIECE)
            path_key_ref[rows, :HEAD_DIM] = far_ref[piece, level, :PIECE]
            path_value_ref[rows, :HEAD_DIM] = far_ref[piece, level, PIECE:]
    path_value_ref[:, HEAD_DIM:] = jnp.ones((PATH, HEAD_DIM), jnp.bfloat16)
    for copy in fetches:
        copy.wait()
    first = first_ref[0]
    _, depth0 = path_of(parents_ref, first)
    _, depth1 = path_of(parents_ref, first + 1)
    follows = jnp.where(parents_ref[first + 1] == first, 0.0, MASKED)
    row = lax.broadcasted_iota(jnp.int32, (PATH, HEAD_DIM), 0)
    lane = lax.broadcasted_iota(jnp.int32, (PATH, HEAD_DIM), 1)
    level = lax.rem(row // PIECE, LEVELS)
    limit = jnp.where(lane == 0, depth0, jnp.where(lane == 1, jnp.minimum(depth0, depth1), LEVELS))
    path_key_ref[:, HEAD_DIM:] = jnp.where(level < limit, 0.0, MASKED).astype(jnp.bfloat16)
    path_keys, path_values = path_key_ref[...], path_value_ref[...]

    rows = lax.broadcasted_iota(jnp.int32, (2 * SEG_LEN, HEAD_DIM), 0)
    lanes = lax.broadcasted_iota(jnp.int32, (2 * SEG_LEN, HEAD_DIM), 1)
    marks = (lanes == rows // SEG_LEN).astype(jnp.float32).astype(jnp.bfloat16)
    causal = lax.broadcasted_iota(jnp.int32, (SEG_LEN, SEG_LEN), 1) <= lax.broadcasted_iota(
        jnp.int32, (SEG_LEN, SEG_LEN), 0
    )
    halves = [slice(0, SEG_LEN), slice(SEG_LEN, 2 * SEG_LEN)]
    own_values = [with_ones(value_ref[half]) for half in halves]
    for head in range(heads):
        query = query_ref[:, head * HEAD_DIM : (head + 1) * HEAD_DIM]
        path_scores = scores_of(jnp.concatenate([query, marks], axis=1), path_keys)
        own = [
            [(jnp.where(causal, scores_of(query[half], key_ref[half]), MASKED), values)]
            for half, values in zip(halves, own_values)
        ]
        own[1].append((scores_of(query[halves[1]], key_ref[halves[0]]) + follows, own_values[0]))
        path_weights, own_parts = [], []
        for half, blocks in zip(halves, own):
            row_max = functools.reduce(
                jnp.maximum,
                [jnp.max(s, axis=1, keepdims=True) for s, _ in blocks]
                + [jnp.max(path_scores[half], axis=1, keepdims=True)],
            )
            weigh = lambda s: jnp.exp2((s - row_max) * EXP2_SCALE).astype(jnp.bfloat16)
            path_weights.append(weigh(path_scores[half]))
            own_parts.append(
                sum(
                    jnp.dot(weigh(s), values, preferred_element_type=jnp.float32)
                    for s, values in blocks
                )
            )
        total = jnp.dot(
            jnp.concatenate(path_weights, axis=0), path_values, preferred_element_type=jnp.float32
        ) + jnp.concatenate(own_parts, axis=0)
        mixture = total[:, :HEAD_DIM] / total[:, HEAD_DIM:]
        out_ref[:, head * HEAD_DIM : (head + 1) * HEAD_DIM] = mixture.astype(out_ref.dtype)
    for copy in copies:
        copy.wait()


def weight_copies(me_ref, weight_ref, held_ref, sem):
    block = weight_ref.shape[0] // 4
    copies = []
    for bit in range(4):
        rows = pl.ds(pl.multiple_of((me_ref[0] ^ bit) * block, block), block)
        copies.append(
            pltpu.make_async_copy(
                weight_ref.at[rows], held_ref.at[pl.ds(bit * block, block)], sem.at[bit]
            )
        )
    return copies


def attend(first, parents, queries, keys, values, far, first_head, heads, bring, after):
    rows = queries.shape[0]
    pairs = heads * rows * (PATH + SEG_LEN + SEG_LEN // 2)
    out_shape = [jax.ShapeDtypeStruct((rows, heads * HEAD_DIM), jnp.bfloat16)]
    in_specs = [SMEM] + [HBM] * 4 + [VMEM]
    scratch = [pltpu.VMEM((PATH, 2 * HEAD_DIM), jnp.bfloat16)] * 2 + [
        pltpu.SMEM(parents.shape, parents.dtype),
        pltpu.VMEM((rows, heads * HEAD_DIM), queries.dtype),
        pltpu.VMEM(keys.shape, keys.dtype),
        pltpu.VMEM(values.shape, values.dtype),
        pltpu.SemaphoreType.DMA((4,)),
    ]
    if bring:
        weight = bring[1]
        bring = [bring[0], in_hbm(weight)]
        in_specs += [SMEM, HBM]
        out_shape.append(pltpu.VMEM(weight.shape, weight.dtype))
        scratch.append(pltpu.SemaphoreType.DMA((4,)))
    return pl.pallas_call(
        functools.partial(attend_kernel, first_head, bool(bring)),
        out_shape=out_shape,
        in_specs=in_specs + [ANY] * len(after),
        out_specs=[VMEM] * len(out_shape),
        scratch_shapes=scratch,
        compiler_params=pltpu.CompilerParams(vmem_limit_bytes=ATTEND_VMEM),
        cost_estimate=pl.CostEstimate(
            flops=pairs * HEAD_DIM * 10,
            bytes_accessed=heads * rows * HEAD_DIM * 4 + 8 * PATH * HEAD_DIM,
            transcendentals=pairs,
        ),
        name="attend",
    )(
        first,
        in_hbm(parents),
        in_hbm(queries),
        in_hbm(keys),
        in_hbm(values),
        far,
        *bring,
        *after,
    )


def project_kernel(counts, spans, has_base, weight_ref, *refs):
    parts = refs[: sum(counts)]
    out_ref, held_ref = refs[-2:]
    at, ends = 0, [0]
    for count in counts:
        for part in parts[:count]:
            held_ref[:, at : at + part.shape[1]] = part[...]
            at += part.shape[1]
        parts = parts[count:]
        ends.append(at)
    for column in range(0, out_ref.shape[1], TILE):
        columns = slice(column, column + TILE)
        total = refs[sum(counts)][:, columns] if has_base else None
        for start, begin, end in zip(spans, ends, ends[1:]):
            product = jnp.dot(
                held_ref[:, begin:end],
                weight_ref[start : start + end - begin, columns],
                preferred_element_type=jnp.float32,
            )
            total = product if total is None else total + product
        out_ref[:, columns] = total.astype(out_ref.dtype)


def project(groups, spans, weight, base, dtype):
    parts = [part for group in groups for part in group]
    rows = parts[0].shape[0]
    depth = sum(part.shape[1] for part in parts)
    width = weight.shape[1]
    bases = [] if base is None else [base]
    return pl.pallas_call(
        functools.partial(project_kernel, [len(g) for g in groups], spans, base is not None),
        out_shape=jax.ShapeDtypeStruct((rows, width), dtype),
        in_specs=[VMEM] * (1 + len(parts) + len(bases)),
        out_specs=VMEM,
        scratch_shapes=[pltpu.VMEM((rows, depth), weight.dtype)],
        compiler_params=pltpu.CompilerParams(vmem_limit_bytes=PROJECT_VMEM),
        cost_estimate=pl.CostEstimate(
            flops=rows * width,
            bytes_accessed=rows * width,
            transcendentals=0,
        ),
        name="project",
    )(in_vmem(weight), *parts, *bases)


def swap(part, bit):
    size = lax.axis_size("tensor")
    return lax.ppermute(part, "tensor", [(i, i ^ bit) for i in range(size)])


def trade(pieces):
    devices = lax.axis_size("dp")
    rows = [list(range(at, at + ROW))[::-1] for at in range(0, devices, ROW)]
    return lax.all_to_all(pieces, "dp", 0, 0, tiled=True, axis_index_groups=rows)


def onward(piece, step):
    devices = lax.axis_size("dp")
    return lax.ppermute(piece, "dp", [(i, (i + step) % devices) for i in range(devices)])


def per_device(queries, key_proj, value_proj, out_weight, parents):
    me = lax.axis_index("tensor")
    first = (lax.axis_index("dp") * 2).astype(jnp.int32).reshape(1)
    pieces = trade(pack(key_proj, value_proj)).reshape(ROW_SEGS, 2 * PIECE, HEAD_DIM)
    to_next, to_second = carry_out(first, parents, pieces)
    inside = pick(first, parents, pieces)
    far = trade(merge(*inside, onward(to_next, ROW), onward(to_second, 2 * ROW)))

    width = queries.shape[1]
    size = 2
    chunks = width // (size * HEAD_DIM)
    own, across, weight = [], [], None
    for c in range(chunks):
        after = [across[c - 2]] if c >= 2 else []
        bring = [me.astype(jnp.int32).reshape(1), out_weight] if c == 2 else []
        part, *brought = attend(
            first, parents, queries, key_proj, value_proj, far, c * size, size, bring, after
        )
        weight = brought[0] if brought else weight
        own.append(part)
        across.append(swap(part, 2))
    beside = [swap(part, 1) for part in own]
    early = chunks - 1
    corner = [swap(part, 1) for part in across[:-1]]
    near = project(
        [own + beside + across[:early], corner[:early]], [0, 3 * width], weight, None, jnp.float32
    )
    across[-1], near = lax.optimization_barrier((across[-1], near))
    corner.append(swap(across[-1], 1))
    done = early * size * HEAD_DIM
    return project(
        [across[early:], corner[early:]],
        [2 * width + done, 3 * width + done],
        weight,
        near,
        jnp.bfloat16,
    )


def solution(mesh):
    placed = (P("dp", "tensor"), P("dp", "tensor"), P("dp", "tensor"), P(None, "tensor"), P())
    return jax.shard_map(
        per_device, mesh=mesh, in_specs=placed, out_specs=P("dp", "tensor"), check_vma=False
    )
```

```python
import functools
import math

import jax
import jax.numpy as jnp
from jax import lax
from jax.experimental import pallas as pl
from jax.experimental.pallas import tpu as pltpu
from jax.sharding import PartitionSpec as P

HEAD_DIM = 128
SEG_LEN = 256
LEVELS = 4
ROW = 8
ROW_SEGS = 2 * ROW
LISTED = (7, 3, 6, 2, 5, 1, 4, 0)
PIECE = SEG_LEN // ROW
PATH = LEVELS * SEG_LEN
STACK = LEVELS * PIECE
MASKED = -1e30
EXP2_SCALE = math.log2(math.e) * HEAD_DIM ** (-0.5)
SMALL_VMEM = 6 * 1024 * 1024
ATTEND_VMEM = 18 * 1024 * 1024
PROJECT_VMEM = 14 * 1024 * 1024
TILE = 256

VMEM = pl.BlockSpec(memory_space=pltpu.VMEM)
SMEM = pl.BlockSpec(memory_space=pltpu.SMEM)
ANY = pl.BlockSpec(memory_space=pl.ANY)
HBM = pl.BlockSpec(memory_space=pltpu.HBM)
FLAG_ROWS = 16


def in_hbm(array):
    return pltpu.with_memory_space_constraint(array, pltpu.HBM)


def in_vmem(array):
    return pltpu.with_memory_space_constraint(array, pltpu.VMEM)


def path_of(parents_ref, seg):
    path = [parents_ref[seg]]
    for _ in range(LEVELS - 1):
        up = parents_ref[jnp.maximum(path[-1], 0)]
        path.append(jnp.where(path[-1] >= 0, up, -1))
    depth = sum((p >= 0).astype(jnp.int32) for p in path)
    return path, depth


def level_of(path, depth, level):
    found = jnp.int32(0)
    for up in range(LEVELS):
        found = jnp.where(depth - 1 - up == level, path[up], found)
    return found


def pack_kernel(key_ref, value_ref, piece_ref, held_ref, sem):
    copies = [
        pltpu.make_async_copy(source, held_ref.at[i], sem.at[i])
        for i, source in enumerate([key_ref, value_ref])
    ]
    for copy in copies:
        copy.start()
    for i, copy in enumerate(copies):
        copy.wait()
        for piece in range(ROW):
            for seg in range(2):
                rows = pl.ds(seg * SEG_LEN + piece * PIECE, PIECE)
                piece_ref[piece, seg, i * PIECE : (i + 1) * PIECE] = held_ref[i, rows]


def pack(keys, values):
    return pl.pallas_call(
        pack_kernel,
        out_shape=jax.ShapeDtypeStruct((ROW, 2, 2 * PIECE, HEAD_DIM), keys.dtype),
        in_specs=[HBM, HBM],
        out_specs=VMEM,
        scratch_shapes=[pltpu.VMEM((2,) + keys.shape, keys.dtype), pltpu.SemaphoreType.DMA((2,))],
        compiler_params=pltpu.CompilerParams(vmem_limit_bytes=SMALL_VMEM),
        cost_estimate=pl.CostEstimate(flops=0, bytes_accessed=1 << 19, transcendentals=0),
        name="pack",
    )(in_hbm(keys), in_hbm(values))


def row_start(first_ref):
    return (first_ref[0] // ROW_SEGS) * ROW_SEGS


def slot_of(seg):
    place = seg // 2
    member = 2 * (ROW // 2 - 1 - place % (ROW // 2)) + 1 - place // (ROW // 2)
    return 2 * member + seg % 2


def bring_parents(source_ref, parents_ref, sem):
    copy = pltpu.make_async_copy(source_ref, parents_ref, sem)
    copy.start()
    copy.wait()


def carry_kernel(first_ref, source_ref, pieces_ref, next_ref, second_ref, parents_ref, sem):
    bring_parents(source_ref, parents_ref, sem)
    base = row_start(first_ref)
    last = parents_ref.shape[0] - 1

    def held(path, depth, level):
        return pieces_ref[slot_of(jnp.clip(level_of(path, depth, level) - base, 0, ROW_SEGS - 1))]

    path, depth = path_of(parents_ref, jnp.minimum(base + ROW_SEGS, last))
    for level in range(LEVELS):
        next_ref[level] = held(path, depth, level)
    path, depth = path_of(parents_ref, jnp.minimum(base + 2 * ROW_SEGS, last))
    second_ref[0] = held(path, depth, 0)


def carry_out(first, parents, pieces):
    shape = lambda n: jax.ShapeDtypeStruct((n,) + pieces.shape[1:], pieces.dtype)
    return pl.pallas_call(
        carry_kernel,
        out_shape=(shape(LEVELS), shape(1)),
        in_specs=[SMEM, HBM, VMEM],
        out_specs=(VMEM, VMEM),
        scratch_shapes=[pltpu.SMEM(parents.shape, parents.dtype), pltpu.SemaphoreType.DMA],
        compiler_params=pltpu.CompilerParams(vmem_limit_bytes=SMALL_VMEM),
        cost_estimate=pl.CostEstimate(flops=0, bytes_accessed=1 << 18, transcendentals=0),
        name="carry_out",
    )(first, in_hbm(parents), pieces)


def pick_kernel(
    first_ref, source_ref, pieces_ref, inside_ref, next_ref, second_ref, parents_ref, sem
):
    bring_parents(source_ref, parents_ref, sem)
    base = row_start(first_ref)
    ones = lambda on: jnp.full((FLAG_ROWS, HEAD_DIM), on, jnp.float32).astype(jnp.bfloat16)
    for target, place in enumerate(LISTED):
        path, depth = path_of(parents_ref, base + 2 * place)
        for level in range(LEVELS):
            seg = level_of(path, depth, level)
            within = seg >= base
            piece = pieces_ref[slot_of(jnp.maximum(seg - base, 0))]
            inside_ref[target, level] = jnp.where(within, piece, jnp.zeros_like(piece))
            before = jnp.logical_and(seg < base, seg >= base - ROW_SEGS)
            next_ref[target, level] = ones(jnp.where(before, 1.0, 0.0))
            if level == 0:
                second_ref[target] = ones(jnp.where(seg < base - ROW_SEGS, 1.0, 0.0))


def pick(first, parents, pieces):
    shape = lambda *dims: jax.ShapeDtypeStruct(dims, pieces.dtype)
    return pl.pallas_call(
        pick_kernel,
        out_shape=(
            shape(ROW, LEVELS, *pieces.shape[1:]),
            shape(ROW, LEVELS, FLAG_ROWS, HEAD_DIM),
            shape(ROW, FLAG_ROWS, HEAD_DIM),
        ),
        in_specs=[SMEM, HBM, VMEM],
        out_specs=(VMEM, VMEM, VMEM),
        scratch_shapes=[pltpu.SMEM(parents.shape, parents.dtype), pltpu.SemaphoreType.DMA],
        compiler_params=pltpu.CompilerParams(vmem_limit_bytes=SMALL_VMEM),
        cost_estimate=pl.CostEstimate(flops=0, bytes_accessed=1 << 20, transcendentals=0),
        name="pick",
    )(first, in_hbm(parents), pieces)


def merge_kernel(inside_ref, on_next_ref, on_second_ref, next_ref, second_ref, picked_ref):
    for level in range(LEVELS):
        for at in range(0, 2 * PIECE, FLAG_ROWS):
            rows = pl.ds(at, FLAG_ROWS)
            carried = next_ref[level, rows]
            older = second_ref[0, rows]
            for target in range(ROW):
                total = inside_ref[target, level, rows] + carried * on_next_ref[target, level]
                if level == 0:
                    total = total + older * on_second_ref[target]
                picked_ref[target, level, rows] = total


def merge(inside, on_next, on_second, carried, second):
    return pl.pallas_call(
        merge_kernel,
        out_shape=jax.ShapeDtypeStruct(inside.shape, inside.dtype),
        in_specs=[VMEM] * 5,
        out_specs=VMEM,
        compiler_params=pltpu.CompilerParams(vmem_limit_bytes=SMALL_VMEM),
        cost_estimate=pl.CostEstimate(flops=0, bytes_accessed=1 << 20, transcendentals=0),
        name="merge",
    )(inside, on_next, on_second, carried, second)


def attend_kernel(first_head, blocks, first_ref, *refs):
    sources, (far_ref, *refs) = refs[:4], refs[4:]
    if blocks:
        me_ref, weight_ref = refs[:2]
        weight_sem = refs.pop()
        held_ref = refs.pop(-8)
    out_ref, path_key_ref, path_value_ref, parents_ref, query_ref, key_ref, value_ref, sem = refs[-8:]
    heads = query_ref.shape[1] // HEAD_DIM
    columns = pl.ds(first_head * HEAD_DIM, query_ref.shape[1])
    views = [sources[0], sources[1].at[:, columns], sources[2], sources[3]]
    fetches = [
        pltpu.make_async_copy(view, target, sem.at[i])
        for i, (view, target) in enumerate(zip(views, [parents_ref, query_ref, key_ref, value_ref]))
    ]
    copies = weight_copies(blocks, me_ref, weight_ref, held_ref, weight_sem) if blocks else []
    for copy in fetches + copies:
        copy.start()

    def scores_of(query, keys):
        return lax.dot_general(
            query, keys, (((1,), (1,)), ((), ())), preferred_element_type=jnp.float32
        )

    def with_ones(values):
        return jnp.concatenate([values, jnp.ones_like(values)], axis=1)

    for piece in range(ROW):
        for level in range(LEVELS):
            rows = pl.ds(piece * STACK + level * PIECE, PIECE)
            path_key_ref[rows, :HEAD_DIM] = far_ref[piece, level, :PIECE]
            path_value_ref[rows, :HEAD_DIM] = far_ref[piece, level, PIECE:]
    path_value_ref[:, HEAD_DIM:] = jnp.ones((PATH, HEAD_DIM), jnp.bfloat16)
    for copy in fetches:
        copy.wait()
    first = first_ref[0]
    _, depth0 = path_of(parents_ref, first)
    _, depth1 = path_of(parents_ref, first + 1)
    follows = jnp.where(parents_ref[first + 1] == first, 0.0, MASKED)
    row = lax.broadcasted_iota(jnp.int32, (PATH, HEAD_DIM), 0)
    lane = lax.broadcasted_iota(jnp.int32, (PATH, HEAD_DIM), 1)
    level = lax.rem(row // PIECE, LEVELS)
    limit = jnp.where(lane == 0, depth0, jnp.where(lane == 1, jnp.minimum(depth0, depth1), LEVELS))
    path_key_ref[:, HEAD_DIM:] = jnp.where(level < limit, 0.0, MASKED).astype(jnp.bfloat16)
    path_keys, path_values = path_key_ref[...], path_value_ref[...]

    rows = lax.broadcasted_iota(jnp.int32, (2 * SEG_LEN, HEAD_DIM), 0)
    lanes = lax.broadcasted_iota(jnp.int32, (2 * SEG_LEN, HEAD_DIM), 1)
    marks = (lanes == rows // SEG_LEN).astype(jnp.float32).astype(jnp.bfloat16)
    causal = lax.broadcasted_iota(jnp.int32, (SEG_LEN, SEG_LEN), 1) <= lax.broadcasted_iota(
        jnp.int32, (SEG_LEN, SEG_LEN), 0
    )
    halves = [slice(0, SEG_LEN), slice(SEG_LEN, 2 * SEG_LEN)]
    own_values = [with_ones(value_ref[half]) for half in halves]
    for head in range(heads):
        query = query_ref[:, head * HEAD_DIM : (head + 1) * HEAD_DIM]
        path_scores = scores_of(jnp.concatenate([query, marks], axis=1), path_keys)
        own = [
            [(jnp.where(causal, scores_of(query[half], key_ref[half]), MASKED), values)]
            for half, values in zip(halves, own_values)
        ]
        own[1].append((scores_of(query[halves[1]], key_ref[halves[0]]) + follows, own_values[0]))
        path_weights, own_parts = [], []
        for half, blocks in zip(halves, own):
            row_max = functools.reduce(
                jnp.maximum,
                [jnp.max(s, axis=1, keepdims=True) for s, _ in blocks]
                + [jnp.max(path_scores[half], axis=1, keepdims=True)],
            )
            weigh = lambda s: jnp.exp2((s - row_max) * EXP2_SCALE).astype(jnp.bfloat16)
            path_weights.append(weigh(path_scores[half]))
            own_parts.append(
                sum(
                    jnp.dot(weigh(s), values, preferred_element_type=jnp.float32)
                    for s, values in blocks
                )
            )
        total = jnp.dot(
            jnp.concatenate(path_weights, axis=0), path_values, preferred_element_type=jnp.float32
        ) + jnp.concatenate(own_parts, axis=0)
        mixture = total[:, :HEAD_DIM] / total[:, HEAD_DIM:]
        out_ref[:, head * HEAD_DIM : (head + 1) * HEAD_DIM] = mixture.astype(out_ref.dtype)
    for copy in copies:
        copy.wait()


def weight_copies(blocks, me_ref, weight_ref, held_ref, sem):
    block = weight_ref.shape[0] // 4
    copies = []
    for i, bit in enumerate(blocks):
        rows = pl.ds(pl.multiple_of((me_ref[0] ^ bit) * block, block), block)
        copies.append(
            pltpu.make_async_copy(
                weight_ref.at[rows], held_ref.at[pl.ds(i * block, block)], sem.at[i]
            )
        )
    return copies


def attend(first, parents, queries, keys, values, far, first_head, heads, blocks, bring, after):
    rows = queries.shape[0]
    pairs = heads * rows * (PATH + SEG_LEN + SEG_LEN // 2)
    out_shape = [jax.ShapeDtypeStruct((rows, heads * HEAD_DIM), jnp.bfloat16)]
    in_specs = [SMEM] + [HBM] * 4 + [VMEM]
    scratch = [pltpu.VMEM((PATH, 2 * HEAD_DIM), jnp.bfloat16)] * 2 + [
        pltpu.SMEM(parents.shape, parents.dtype),
        pltpu.VMEM((rows, heads * HEAD_DIM), queries.dtype),
        pltpu.VMEM(keys.shape, keys.dtype),
        pltpu.VMEM(values.shape, values.dtype),
        pltpu.SemaphoreType.DMA((4,)),
    ]
    if blocks:
        me, weight = bring
        bring = [me, in_hbm(weight)]
        in_specs += [SMEM, HBM]
        shape = (len(blocks) * weight.shape[0] // 4, weight.shape[1])
        out_shape.append(pltpu.VMEM(shape, weight.dtype))
        scratch.append(pltpu.SemaphoreType.DMA((len(blocks),)))
    else:
        bring = []
    return pl.pallas_call(
        functools.partial(attend_kernel, first_head, blocks),
        out_shape=out_shape,
        in_specs=in_specs + [ANY] * len(after),
        out_specs=[VMEM] * len(out_shape),
        scratch_shapes=scratch,
        compiler_params=pltpu.CompilerParams(vmem_limit_bytes=ATTEND_VMEM),
        cost_estimate=pl.CostEstimate(
            flops=pairs * HEAD_DIM * 10,
            bytes_accessed=heads * rows * HEAD_DIM * 4 + 8 * PATH * HEAD_DIM,
            transcendentals=pairs,
        ),
        name="attend",
    )(
        first,
        in_hbm(parents),
        in_hbm(queries),
        in_hbm(keys),
        in_hbm(values),
        far,
        *bring,
        *after,
    )


def project_kernel(counts, spans, has_base, near_ref, far_ref, *refs):
    parts = refs[: sum(counts)]
    out_ref, held_ref = refs[-2:]
    at, ends = 0, [0]
    for count in counts:
        for part in parts[:count]:
            held_ref[:, at : at + part.shape[1]] = part[...]
            at += part.shape[1]
        parts = parts[count:]
        ends.append(at)
    for column in range(0, out_ref.shape[1], TILE):
        columns = slice(column, column + TILE)
        total = refs[sum(counts)][:, columns] if has_base else None
        for (half, start), begin, end in zip(spans, ends, ends[1:]):
            product = jnp.dot(
                held_ref[:, begin:end],
                (near_ref, far_ref)[half][start : start + end - begin, columns],
                preferred_element_type=jnp.float32,
            )
            total = product if total is None else total + product
        out_ref[:, columns] = total.astype(out_ref.dtype)


def project(groups, spans, weights, base, dtype):
    parts = [part for group in groups for part in group]
    rows = parts[0].shape[0]
    depth = sum(part.shape[1] for part in parts)
    width = weights[0].shape[1]
    bases = [] if base is None else [base]
    return pl.pallas_call(
        functools.partial(project_kernel, [len(g) for g in groups], spans, base is not None),
        out_shape=jax.ShapeDtypeStruct((rows, width), dtype),
        in_specs=[VMEM] * (2 + len(parts) + len(bases)),
        out_specs=VMEM,
        scratch_shapes=[pltpu.VMEM((rows, depth), parts[0].dtype)],
        compiler_params=pltpu.CompilerParams(vmem_limit_bytes=PROJECT_VMEM),
        cost_estimate=pl.CostEstimate(
            flops=rows * width,
            bytes_accessed=rows * width,
            transcendentals=0,
        ),
        name="project",
    )(*[in_vmem(weight) for weight in weights], *parts, *bases)


def swap(part, bit):
    size = lax.axis_size("tensor")
    return lax.ppermute(part, "tensor", [(i, i ^ bit) for i in range(size)])


def trade(pieces):
    devices = lax.axis_size("dp")
    rows = [[at + place for place in LISTED] for at in range(0, devices, ROW)]
    return lax.all_to_all(pieces, "dp", 0, 0, tiled=True, axis_index_groups=rows)


def onward(piece, step):
    devices = lax.axis_size("dp")
    return lax.ppermute(piece, "dp", [(i, (i + step) % devices) for i in range(devices)])


def per_device(queries, key_proj, value_proj, out_weight, parents):
    me = lax.axis_index("tensor")
    first = (lax.axis_index("dp") * 2).astype(jnp.int32).reshape(1)
    pieces = trade(pack(key_proj, value_proj)).reshape(ROW_SEGS, 2 * PIECE, HEAD_DIM)
    to_next, to_second = carry_out(first, parents, pieces)
    inside = pick(first, parents, pieces)
    far = trade(merge(*inside, onward(to_next, ROW), onward(to_second, 2 * ROW)))

    width = queries.shape[1]
    bring = (me.astype(jnp.int32).reshape(1), out_weight)
    own, across, weights, head = [], [], [], 0
    for c, (size, blocks) in enumerate([(2, ()), (3, (0, 1)), (3, (2, 3))]):
        after = [across[c - 2]] if c >= 2 else []
        part, *brought = attend(
            first, parents, queries, key_proj, value_proj, far, head, size, blocks, bring, after
        )
        weights += brought
        own.append(part)
        across.append(swap(part, 2))
        head += size
    beside = [swap(part, 1) for part in own]
    corner = [swap(part, 1) for part in across[:-1]]
    near = project(
        [own + beside, across[:-1], corner[:-1]], [(0, 0), (1, 0), (1, width)], weights, None, jnp.float32
    )
    last, near = lax.optimization_barrier((across[-1], near))
    corner.append(swap(last, 1))
    done = width - last.shape[1]
    turned = sum(part.shape[1] for part in corner[:-2])
    return project(
        [[last], corner[-2:]], [(1, done), (1, width + turned)], weights, near, jnp.bfloat16
    )


def solution(mesh):
    placed = (P("dp", "tensor"), P("dp", "tensor"), P("dp", "tensor"), P(None, "tensor"), P())
    return jax.shard_map(
        per_device, mesh=mesh, in_specs=placed, out_specs=P("dp", "tensor"), check_vma=False
    )
```

```python
import functools
import math

import jax
import jax.numpy as jnp
from jax import lax
from jax.experimental import pallas as pl
from jax.experimental.pallas import tpu as pltpu
from jax.sharding import PartitionSpec as P

HEAD_DIM = 128
SEG_LEN = 256
LEVELS = 4
ROW = 8
ROW_SEGS = 2 * ROW
LISTED = (7, 3, 6, 2, 5, 1, 4, 0)
PIECE = SEG_LEN // ROW
PATH = LEVELS * SEG_LEN
FAR = LEVELS - 1
STACK = FAR * PIECE
MASKED = -1e30
EXP2_SCALE = math.log2(math.e) * HEAD_DIM ** (-0.5)
SMALL_VMEM = 6 * 1024 * 1024
ATTEND_VMEM = 18 * 1024 * 1024
PROJECT_VMEM = 14 * 1024 * 1024
TILE = 256

VMEM = pl.BlockSpec(memory_space=pltpu.VMEM)
SMEM = pl.BlockSpec(memory_space=pltpu.SMEM)
ANY = pl.BlockSpec(memory_space=pl.ANY)
HBM = pl.BlockSpec(memory_space=pltpu.HBM)
FLAG_ROWS = 16


def in_hbm(array):
    return pltpu.with_memory_space_constraint(array, pltpu.HBM)


def in_vmem(array):
    return pltpu.with_memory_space_constraint(array, pltpu.VMEM)


def path_of(parents_ref, seg):
    path = [parents_ref[seg]]
    for _ in range(LEVELS - 1):
        up = parents_ref[jnp.maximum(path[-1], 0)]
        path.append(jnp.where(path[-1] >= 0, up, -1))
    depth = sum((p >= 0).astype(jnp.int32) for p in path)
    return path, depth


def level_of(path, depth, level):
    found = jnp.int32(0)
    for up in range(LEVELS):
        found = jnp.where(depth - 1 - up == level, path[up], found)
    return found


def pack_kernel(key_ref, value_ref, piece_ref, held_ref, sem):
    copies = [
        pltpu.make_async_copy(source, held_ref.at[i], sem.at[i])
        for i, source in enumerate([key_ref, value_ref])
    ]
    for copy in copies:
        copy.start()
    for i, copy in enumerate(copies):
        copy.wait()
        for piece in range(ROW):
            for seg in range(2):
                rows = pl.ds(seg * SEG_LEN + piece * PIECE, PIECE)
                piece_ref[piece, seg, i * PIECE : (i + 1) * PIECE] = held_ref[i, rows]


def pack(keys, values):
    return pl.pallas_call(
        pack_kernel,
        out_shape=jax.ShapeDtypeStruct((ROW, 2, 2 * PIECE, HEAD_DIM), keys.dtype),
        in_specs=[HBM, HBM],
        out_specs=VMEM,
        scratch_shapes=[pltpu.VMEM((2,) + keys.shape, keys.dtype), pltpu.SemaphoreType.DMA((2,))],
        compiler_params=pltpu.CompilerParams(vmem_limit_bytes=SMALL_VMEM),
        cost_estimate=pl.CostEstimate(flops=0, bytes_accessed=1 << 19, transcendentals=0),
        name="pack",
    )(in_hbm(keys), in_hbm(values))


def row_start(first_ref):
    return (first_ref[0] // ROW_SEGS) * ROW_SEGS


def slot_of(seg):
    place = seg // 2
    member = 2 * (ROW // 2 - 1 - place % (ROW // 2)) + 1 - place // (ROW // 2)
    return 2 * member + seg % 2


def bring_parents(source_ref, parents_ref, sem):
    copy = pltpu.make_async_copy(source_ref, parents_ref, sem)
    copy.start()
    copy.wait()


def carry_kernel(first_ref, source_ref, pieces_ref, next_ref, second_ref, parents_ref, sem):
    bring_parents(source_ref, parents_ref, sem)
    base = row_start(first_ref)
    last = parents_ref.shape[0] - 1

    def held(path, depth, level):
        return pieces_ref[slot_of(jnp.clip(level_of(path, depth, level) - base, 0, ROW_SEGS - 1))]

    path, depth = path_of(parents_ref, jnp.minimum(base + ROW_SEGS, last))
    for level in range(FAR):
        next_ref[level] = held(path, depth, level)
    path, depth = path_of(parents_ref, jnp.minimum(base + 2 * ROW_SEGS, last))
    second_ref[0] = held(path, depth, 0)


def carry_out(first, parents, pieces):
    shape = lambda n: jax.ShapeDtypeStruct((n,) + pieces.shape[1:], pieces.dtype)
    return pl.pallas_call(
        carry_kernel,
        out_shape=(shape(FAR), shape(1)),
        in_specs=[SMEM, HBM, VMEM],
        out_specs=(VMEM, VMEM),
        scratch_shapes=[pltpu.SMEM(parents.shape, parents.dtype), pltpu.SemaphoreType.DMA],
        compiler_params=pltpu.CompilerParams(vmem_limit_bytes=SMALL_VMEM),
        cost_estimate=pl.CostEstimate(flops=0, bytes_accessed=1 << 18, transcendentals=0),
        name="carry_out",
    )(first, in_hbm(parents), pieces)


def pick_kernel(
    first_ref,
    source_ref,
    key_ref,
    value_ref,
    pieces_ref,
    inside_ref,
    next_ref,
    second_ref,
    deep_ref,
    parents_ref,
    pair_ref,
    sem,
    pair_sem,
):
    copies = [
        pltpu.make_async_copy(source, pair_ref.at[i], pair_sem.at[i])
        for i, source in enumerate([key_ref, value_ref])
    ]
    for copy in copies:
        copy.start()
    bring_parents(source_ref, parents_ref, sem)
    base = row_start(first_ref)
    ones = lambda on: jnp.full((FLAG_ROWS, HEAD_DIM), on, jnp.float32).astype(jnp.bfloat16)
    for target, place in enumerate(LISTED):
        path, depth = path_of(parents_ref, base + 2 * place)
        for level in range(FAR):
            seg = level_of(path, depth, level)
            within = seg >= base
            piece = pieces_ref[slot_of(jnp.maximum(seg - base, 0))]
            inside_ref[target, level] = jnp.where(within, piece, jnp.zeros_like(piece))
            before = jnp.logical_and(seg < base, seg >= base - ROW_SEGS)
            next_ref[target, level] = ones(jnp.where(before, 1.0, 0.0))
            if level == 0:
                second_ref[target] = ones(jnp.where(seg < base - ROW_SEGS, 1.0, 0.0))
    _, depth = path_of(parents_ref, first_ref[0] + 1)
    start = jnp.where(depth == FAR, SEG_LEN, 0)
    rows = pl.ds(pl.multiple_of(start, SEG_LEN), SEG_LEN)
    for i, copy in enumerate(copies):
        copy.wait()
        deep_ref[i] = pair_ref[i, rows]


def pick(first, parents, keys, values, pieces):
    shape = lambda *dims: jax.ShapeDtypeStruct(dims, pieces.dtype)
    return pl.pallas_call(
        pick_kernel,
        out_shape=(
            shape(ROW, FAR, *pieces.shape[1:]),
            shape(ROW, FAR, FLAG_ROWS, HEAD_DIM),
            shape(ROW, FLAG_ROWS, HEAD_DIM),
            shape(2, SEG_LEN, HEAD_DIM),
        ),
        in_specs=[SMEM, HBM, HBM, HBM, VMEM],
        out_specs=(VMEM,) * 4,
        scratch_shapes=[
            pltpu.SMEM(parents.shape, parents.dtype),
            pltpu.VMEM((2,) + keys.shape, keys.dtype),
            pltpu.SemaphoreType.DMA,
            pltpu.SemaphoreType.DMA((2,)),
        ],
        compiler_params=pltpu.CompilerParams(vmem_limit_bytes=SMALL_VMEM),
        cost_estimate=pl.CostEstimate(flops=0, bytes_accessed=1 << 20, transcendentals=0),
        name="pick",
    )(first, in_hbm(parents), in_hbm(keys), in_hbm(values), pieces)


def merge_kernel(inside_ref, on_next_ref, on_second_ref, next_ref, second_ref, picked_ref):
    for level in range(FAR):
        for at in range(0, 2 * PIECE, FLAG_ROWS):
            rows = pl.ds(at, FLAG_ROWS)
            carried = next_ref[level, rows]
            older = second_ref[0, rows]
            for target in range(ROW):
                total = inside_ref[target, level, rows] + carried * on_next_ref[target, level]
                if level == 0:
                    total = total + older * on_second_ref[target]
                picked_ref[target, level, rows] = total


def merge(inside, on_next, on_second, carried, second):
    return pl.pallas_call(
        merge_kernel,
        out_shape=jax.ShapeDtypeStruct(inside.shape, inside.dtype),
        in_specs=[VMEM] * 5,
        out_specs=VMEM,
        compiler_params=pltpu.CompilerParams(vmem_limit_bytes=SMALL_VMEM),
        cost_estimate=pl.CostEstimate(flops=0, bytes_accessed=1 << 20, transcendentals=0),
        name="merge",
    )(inside, on_next, on_second, carried, second)


def attend_kernel(first_head, blocks, first_ref, *refs):
    sources, (far_ref, deep_ref, *refs) = refs[:4], refs[4:]
    if blocks:
        me_ref, weight_ref = refs[:2]
        weight_sem = refs.pop()
        held_ref = refs.pop(-8)
    out_ref, path_key_ref, path_value_ref, parents_ref, query_ref, key_ref, value_ref, sem = refs[-8:]
    heads = query_ref.shape[1] // HEAD_DIM
    columns = pl.ds(first_head * HEAD_DIM, query_ref.shape[1])
    views = [sources[0], sources[1].at[:, columns], sources[2], sources[3]]
    fetches = [
        pltpu.make_async_copy(view, target, sem.at[i])
        for i, (view, target) in enumerate(zip(views, [parents_ref, query_ref, key_ref, value_ref]))
    ]
    copies = weight_copies(blocks, me_ref, weight_ref, held_ref, weight_sem) if blocks else []
    for copy in fetches + copies:
        copy.start()

    def scores_of(query, keys):
        return lax.dot_general(
            query, keys, (((1,), (1,)), ((), ())), preferred_element_type=jnp.float32
        )

    def with_ones(values):
        return jnp.concatenate([values, jnp.ones_like(values)], axis=1)

    for piece in range(ROW):
        for level in range(FAR):
            rows = pl.ds(piece * STACK + level * PIECE, PIECE)
            path_key_ref[rows, :HEAD_DIM] = far_ref[piece, level, :PIECE]
            path_value_ref[rows, :HEAD_DIM] = far_ref[piece, level, PIECE:]
    path_key_ref[FAR * SEG_LEN :, :HEAD_DIM] = deep_ref[0]
    path_value_ref[FAR * SEG_LEN :, :HEAD_DIM] = deep_ref[1]
    path_value_ref[:, HEAD_DIM:] = jnp.ones((PATH, HEAD_DIM), jnp.bfloat16)
    for copy in fetches:
        copy.wait()
    first = first_ref[0]
    _, depth0 = path_of(parents_ref, first)
    _, depth1 = path_of(parents_ref, first + 1)
    follows = jnp.where(parents_ref[first + 1] == first, 0.0, MASKED)
    row = lax.broadcasted_iota(jnp.int32, (PATH, HEAD_DIM), 0)
    lane = lax.broadcasted_iota(jnp.int32, (PATH, HEAD_DIM), 1)
    level = jnp.where(row < FAR * SEG_LEN, lax.rem(row // PIECE, FAR), FAR)
    limit = jnp.where(lane == 0, depth0, jnp.where(lane == 1, jnp.minimum(depth0, depth1), LEVELS))
    path_key_ref[:, HEAD_DIM:] = jnp.where(level < limit, 0.0, MASKED).astype(jnp.bfloat16)
    path_keys, path_values = path_key_ref[...], path_value_ref[...]

    rows = lax.broadcasted_iota(jnp.int32, (2 * SEG_LEN, HEAD_DIM), 0)
    lanes = lax.broadcasted_iota(jnp.int32, (2 * SEG_LEN, HEAD_DIM), 1)
    marks = (lanes == rows // SEG_LEN).astype(jnp.float32).astype(jnp.bfloat16)
    causal = lax.broadcasted_iota(jnp.int32, (SEG_LEN, SEG_LEN), 1) <= lax.broadcasted_iota(
        jnp.int32, (SEG_LEN, SEG_LEN), 0
    )
    halves = [slice(0, SEG_LEN), slice(SEG_LEN, 2 * SEG_LEN)]
    own_values = [with_ones(value_ref[half]) for half in halves]
    for head in range(heads):
        query = query_ref[:, head * HEAD_DIM : (head + 1) * HEAD_DIM]
        path_scores = scores_of(jnp.concatenate([query, marks], axis=1), path_keys)
        own = [
            [(jnp.where(causal, scores_of(query[half], key_ref[half]), MASKED), values)]
            for half, values in zip(halves, own_values)
        ]
        own[1].append((scores_of(query[halves[1]], key_ref[halves[0]]) + follows, own_values[0]))
        path_weights, own_parts = [], []
        for half, blocks in zip(halves, own):
            row_max = functools.reduce(
                jnp.maximum,
                [jnp.max(s, axis=1, keepdims=True) for s, _ in blocks]
                + [jnp.max(path_scores[half], axis=1, keepdims=True)],
            )
            weigh = lambda s: jnp.exp2((s - row_max) * EXP2_SCALE).astype(jnp.bfloat16)
            path_weights.append(weigh(path_scores[half]))
            own_parts.append(
                sum(
                    jnp.dot(weigh(s), values, preferred_element_type=jnp.float32)
                    for s, values in blocks
                )
            )
        total = jnp.dot(
            jnp.concatenate(path_weights, axis=0), path_values, preferred_element_type=jnp.float32
        ) + jnp.concatenate(own_parts, axis=0)
        mixture = total[:, :HEAD_DIM] / total[:, HEAD_DIM:]
        out_ref[:, head * HEAD_DIM : (head + 1) * HEAD_DIM] = mixture.astype(out_ref.dtype)
    for copy in copies:
        copy.wait()


def weight_copies(blocks, me_ref, weight_ref, held_ref, sem):
    block = weight_ref.shape[0] // 4
    copies = []
    for i, bit in enumerate(blocks):
        rows = pl.ds(pl.multiple_of((me_ref[0] ^ bit) * block, block), block)
        copies.append(
            pltpu.make_async_copy(
                weight_ref.at[rows], held_ref.at[pl.ds(i * block, block)], sem.at[i]
            )
        )
    return copies


def attend(first, parents, queries, keys, values, far, deep, first_head, heads, blocks, bring, after):
    rows = queries.shape[0]
    pairs = heads * rows * (PATH + SEG_LEN + SEG_LEN // 2)
    out_shape = [jax.ShapeDtypeStruct((rows, heads * HEAD_DIM), jnp.bfloat16)]
    in_specs = [SMEM] + [HBM] * 4 + [VMEM, VMEM]
    scratch = [pltpu.VMEM((PATH, 2 * HEAD_DIM), jnp.bfloat16)] * 2 + [
        pltpu.SMEM(parents.shape, parents.dtype),
        pltpu.VMEM((rows, heads * HEAD_DIM), queries.dtype),
        pltpu.VMEM(keys.shape, keys.dtype),
        pltpu.VMEM(values.shape, values.dtype),
        pltpu.SemaphoreType.DMA((4,)),
    ]
    if blocks:
        me, weight = bring
        bring = [me, in_hbm(weight)]
        in_specs += [SMEM, HBM]
        shape = (len(blocks) * weight.shape[0] // 4, weight.shape[1])
        out_shape.append(pltpu.VMEM(shape, weight.dtype))
        scratch.append(pltpu.SemaphoreType.DMA((len(blocks),)))
    else:
        bring = []
    return pl.pallas_call(
        functools.partial(attend_kernel, first_head, blocks),
        out_shape=out_shape,
        in_specs=in_specs + [ANY] * len(after),
        out_specs=[VMEM] * len(out_shape),
        scratch_shapes=scratch,
        compiler_params=pltpu.CompilerParams(vmem_limit_bytes=ATTEND_VMEM),
        cost_estimate=pl.CostEstimate(
            flops=pairs * HEAD_DIM * 10,
            bytes_accessed=heads * rows * HEAD_DIM * 4 + 8 * PATH * HEAD_DIM,
            transcendentals=pairs,
        ),
        name="attend",
    )(
        first,
        in_hbm(parents),
        in_hbm(queries),
        in_hbm(keys),
        in_hbm(values),
        far,
        deep,
        *bring,
        *after,
    )


def project_kernel(counts, spans, has_base, near_ref, far_ref, *refs):
    parts = refs[: sum(counts)]
    out_ref, held_ref = refs[-2:]
    at, ends = 0, [0]
    for count in counts:
        for part in parts[:count]:
            held_ref[:, at : at + part.shape[1]] = part[...]
            at += part.shape[1]
        parts = parts[count:]
        ends.append(at)
    for column in range(0, out_ref.shape[1], TILE):
        columns = slice(column, column + TILE)
        total = refs[sum(counts)][:, columns] if has_base else None
        for (half, start), begin, end in zip(spans, ends, ends[1:]):
            product = jnp.dot(
                held_ref[:, begin:end],
                (near_ref, far_ref)[half][start : start + end - begin, columns],
                preferred_element_type=jnp.float32,
            )
            total = product if total is None else total + product
        out_ref[:, columns] = total.astype(out_ref.dtype)


def project(groups, spans, weights, base, dtype):
    parts = [part for group in groups for part in group]
    rows = parts[0].shape[0]
    depth = sum(part.shape[1] for part in parts)
    width = weights[0].shape[1]
    bases = [] if base is None else [base]
    return pl.pallas_call(
        functools.partial(project_kernel, [len(g) for g in groups], spans, base is not None),
        out_shape=jax.ShapeDtypeStruct((rows, width), dtype),
        in_specs=[VMEM] * (2 + len(parts) + len(bases)),
        out_specs=VMEM,
        scratch_shapes=[pltpu.VMEM((rows, depth), parts[0].dtype)],
        compiler_params=pltpu.CompilerParams(vmem_limit_bytes=PROJECT_VMEM),
        cost_estimate=pl.CostEstimate(
            flops=rows * width,
            bytes_accessed=rows * width,
            transcendentals=0,
        ),
        name="project",
    )(*[in_vmem(weight) for weight in weights], *parts, *bases)


def swap(part, bit):
    size = lax.axis_size("tensor")
    return lax.ppermute(part, "tensor", [(i, i ^ bit) for i in range(size)])


def trade(pieces):
    devices = lax.axis_size("dp")
    rows = [[at + place for place in LISTED] for at in range(0, devices, ROW)]
    return lax.all_to_all(pieces, "dp", 0, 0, tiled=True, axis_index_groups=rows)


def onward(piece, step):
    devices = lax.axis_size("dp")
    return lax.ppermute(piece, "dp", [(i, (i + step) % devices) for i in range(devices)])


def per_device(queries, key_proj, value_proj, out_weight, parents):
    me = lax.axis_index("tensor")
    first = (lax.axis_index("dp") * 2).astype(jnp.int32).reshape(1)
    pieces = trade(pack(key_proj, value_proj)).reshape(ROW_SEGS, 2 * PIECE, HEAD_DIM)
    to_next, to_second = carry_out(first, parents, pieces)
    *inside, deep = pick(first, parents, key_proj, value_proj, pieces)
    deep = onward(deep, 1)
    far = trade(merge(*inside, onward(to_next, ROW), onward(to_second, 2 * ROW)))

    width = queries.shape[1]
    bring = (me.astype(jnp.int32).reshape(1), out_weight)
    own, across, weights, head = [], [], [], 0
    for c, (size, blocks) in enumerate([(2, ()), (3, (0, 1)), (3, (2, 3))]):
        after = [across[c - 2]] if c >= 2 else []
        part, *brought = attend(
            first, parents, queries, key_proj, value_proj, far, deep, head, size, blocks, bring, after
        )
        weights += brought
        own.append(part)
        across.append(swap(part, 2))
        head += size
    beside = [swap(part, 1) for part in own]
    corner = [swap(part, 1) for part in across[:-1]]
    near = project(
        [own + beside, across[:-1], corner[:-1]], [(0, 0), (1, 0), (1, width)], weights, None, jnp.float32
    )
    last, near = lax.optimization_barrier((across[-1], near))
    corner.append(swap(last, 1))
    done = width - last.shape[1]
    turned = sum(part.shape[1] for part in corner[:-2])
    return project(
        [[last], corner[-2:]], [(1, done), (1, width + turned)], weights, near, jnp.bfloat16
    )


def solution(mesh):
    placed = (P("dp", "tensor"), P("dp", "tensor"), P("dp", "tensor"), P(None, "tensor"), P())
    return jax.shard_map(
        per_device, mesh=mesh, in_specs=placed, out_specs=P("dp", "tensor"), check_vma=False
    )
```

```python
import functools
import math

import jax
import jax.numpy as jnp
from jax import lax
from jax.experimental import pallas as pl
from jax.experimental.pallas import tpu as pltpu
from jax.sharding import PartitionSpec as P

HEAD_DIM = 128
SEG_LEN = 256
LEVELS = 4
ROW = 8
ROW_SEGS = 2 * ROW
LISTED = (7, 3, 6, 2, 5, 1, 4, 0)
PIECE = SEG_LEN // ROW
PATH = LEVELS * SEG_LEN
STACK = LEVELS * PIECE
MASKED = -1e30
EXP2_SCALE = math.log2(math.e) * HEAD_DIM ** (-0.5)
SMALL_VMEM = 6 * 1024 * 1024
ATTEND_VMEM = 18 * 1024 * 1024
PROJECT_VMEM = 14 * 1024 * 1024
TILE = 256
SHARED = (3, 3, 2)

VMEM = pl.BlockSpec(memory_space=pltpu.VMEM)
SMEM = pl.BlockSpec(memory_space=pltpu.SMEM)
ANY = pl.BlockSpec(memory_space=pl.ANY)
HBM = pl.BlockSpec(memory_space=pltpu.HBM)
FLAG_ROWS = 16


def in_hbm(array):
    return pltpu.with_memory_space_constraint(array, pltpu.HBM)


def in_vmem(array):
    return pltpu.with_memory_space_constraint(array, pltpu.VMEM)


def path_of(parents_ref, seg):
    path = [parents_ref[seg]]
    for _ in range(LEVELS - 1):
        up = parents_ref[jnp.maximum(path[-1], 0)]
        path.append(jnp.where(path[-1] >= 0, up, -1))
    depth = sum((p >= 0).astype(jnp.int32) for p in path)
    return path, depth


def level_of(path, depth, level):
    found = jnp.int32(0)
    for up in range(LEVELS):
        found = jnp.where(depth - 1 - up == level, path[up], found)
    return found


def pack_kernel(key_ref, value_ref, piece_ref, held_ref, sem):
    copies = [
        pltpu.make_async_copy(source, held_ref.at[i], sem.at[i])
        for i, source in enumerate([key_ref, value_ref])
    ]
    for copy in copies:
        copy.start()
    for i, copy in enumerate(copies):
        copy.wait()
        for piece in range(ROW):
            for seg in range(2):
                rows = pl.ds(seg * SEG_LEN + piece * PIECE, PIECE)
                piece_ref[piece, seg, i * PIECE : (i + 1) * PIECE] = held_ref[i, rows]


def pack(keys, values):
    return pl.pallas_call(
        pack_kernel,
        out_shape=jax.ShapeDtypeStruct((ROW, 2, 2 * PIECE, HEAD_DIM), keys.dtype),
        in_specs=[HBM, HBM],
        out_specs=VMEM,
        scratch_shapes=[pltpu.VMEM((2,) + keys.shape, keys.dtype), pltpu.SemaphoreType.DMA((2,))],
        compiler_params=pltpu.CompilerParams(vmem_limit_bytes=SMALL_VMEM),
        cost_estimate=pl.CostEstimate(flops=0, bytes_accessed=1 << 19, transcendentals=0),
        name="pack",
    )(in_hbm(keys), in_hbm(values))


def row_start(first_ref):
    return (first_ref[0] // ROW_SEGS) * ROW_SEGS


def slot_of(seg):
    place = seg // 2
    member = 2 * (ROW // 2 - 1 - place % (ROW // 2)) + 1 - place // (ROW // 2)
    return 2 * member + seg % 2


def bring_parents(source_ref, parents_ref, sem):
    copy = pltpu.make_async_copy(source_ref, parents_ref, sem)
    copy.start()
    copy.wait()


def carry_kernel(first_ref, source_ref, pieces_ref, next_ref, second_ref, parents_ref, sem):
    bring_parents(source_ref, parents_ref, sem)
    base = row_start(first_ref)
    last = parents_ref.shape[0] - 1

    def held(path, depth, level):
        return pieces_ref[slot_of(jnp.clip(level_of(path, depth, level) - base, 0, ROW_SEGS - 1))]

    path, depth = path_of(parents_ref, jnp.minimum(base + ROW_SEGS, last))
    for level in range(LEVELS):
        next_ref[level] = held(path, depth, level)
    path, depth = path_of(parents_ref, jnp.minimum(base + 2 * ROW_SEGS, last))
    second_ref[0] = held(path, depth, 0)


def carry_out(first, parents, pieces):
    shape = lambda n: jax.ShapeDtypeStruct((n,) + pieces.shape[1:], pieces.dtype)
    return pl.pallas_call(
        carry_kernel,
        out_shape=(shape(LEVELS), shape(1)),
        in_specs=[SMEM, HBM, VMEM],
        out_specs=(VMEM, VMEM),
        scratch_shapes=[pltpu.SMEM(parents.shape, parents.dtype), pltpu.SemaphoreType.DMA],
        compiler_params=pltpu.CompilerParams(vmem_limit_bytes=SMALL_VMEM),
        cost_estimate=pl.CostEstimate(flops=0, bytes_accessed=1 << 18, transcendentals=0),
        name="carry_out",
    )(first, in_hbm(parents), pieces)


def pick_kernel(
    first_ref, source_ref, pieces_ref, inside_ref, next_ref, second_ref, parents_ref, sem
):
    bring_parents(source_ref, parents_ref, sem)
    base = row_start(first_ref)
    ones = lambda on: jnp.full((FLAG_ROWS, HEAD_DIM), on, jnp.float32).astype(jnp.bfloat16)
    for target, place in enumerate(LISTED):
        path, depth = path_of(parents_ref, base + 2 * place)
        for level in range(LEVELS):
            seg = level_of(path, depth, level)
            within = seg >= base
            piece = pieces_ref[slot_of(jnp.maximum(seg - base, 0))]
            inside_ref[target, level] = jnp.where(within, piece, jnp.zeros_like(piece))
            before = jnp.logical_and(seg < base, seg >= base - ROW_SEGS)
            next_ref[target, level] = ones(jnp.where(before, 1.0, 0.0))
            if level == 0:
                second_ref[target] = ones(jnp.where(seg < base - ROW_SEGS, 1.0, 0.0))


def pick(first, parents, pieces):
    shape = lambda *dims: jax.ShapeDtypeStruct(dims, pieces.dtype)
    return pl.pallas_call(
        pick_kernel,
        out_shape=(
            shape(ROW, LEVELS, *pieces.shape[1:]),
            shape(ROW, LEVELS, FLAG_ROWS, HEAD_DIM),
            shape(ROW, FLAG_ROWS, HEAD_DIM),
        ),
        in_specs=[SMEM, HBM, VMEM],
        out_specs=(VMEM, VMEM, VMEM),
        scratch_shapes=[pltpu.SMEM(parents.shape, parents.dtype), pltpu.SemaphoreType.DMA],
        compiler_params=pltpu.CompilerParams(vmem_limit_bytes=SMALL_VMEM),
        cost_estimate=pl.CostEstimate(flops=0, bytes_accessed=1 << 20, transcendentals=0),
        name="pick",
    )(first, in_hbm(parents), pieces)


def merge_kernel(inside_ref, on_next_ref, on_second_ref, next_ref, second_ref, picked_ref):
    for level in range(LEVELS):
        for at in range(0, 2 * PIECE, FLAG_ROWS):
            rows = pl.ds(at, FLAG_ROWS)
            carried = next_ref[level, rows]
            older = second_ref[0, rows]
            for target in range(ROW):
                total = inside_ref[target, level, rows] + carried * on_next_ref[target, level]
                if level == 0:
                    total = total + older * on_second_ref[target]
                picked_ref[target, level, rows] = total


def merge(inside, on_next, on_second, carried, second):
    return pl.pallas_call(
        merge_kernel,
        out_shape=jax.ShapeDtypeStruct(inside.shape, inside.dtype),
        in_specs=[VMEM] * 5,
        out_specs=VMEM,
        compiler_params=pltpu.CompilerParams(vmem_limit_bytes=SMALL_VMEM),
        cost_estimate=pl.CostEstimate(flops=0, bytes_accessed=1 << 20, transcendentals=0),
        name="merge",
    )(inside, on_next, on_second, carried, second)


def attend_kernel(first_head, blocks, earlier, first_ref, *refs):
    sources, (far_ref, *refs) = refs[:4], refs[4:]
    if blocks:
        me_ref, weight_ref = refs[:2]
        weight_sem = refs.pop()
        held_ref = refs.pop(-8)
    earlier = refs[2 : 2 + earlier]
    shared = [refs.pop(-7 - n) for n in range(len(SHARED), 0, -1)] if earlier else []
    out_ref, path_key_ref, path_value_ref, parents_ref, query_ref, key_ref, value_ref, sem = refs[-8:]
    heads = query_ref.shape[1] // HEAD_DIM
    columns = pl.ds(first_head * HEAD_DIM, query_ref.shape[1])
    views = [sources[0], sources[1].at[:, columns], sources[2], sources[3]]
    fetches = [
        pltpu.make_async_copy(view, target, sem.at[i])
        for i, (view, target) in enumerate(zip(views, [parents_ref, query_ref, key_ref, value_ref]))
    ]
    copies = weight_copies(blocks, me_ref, weight_ref, held_ref, weight_sem) if blocks else []
    for copy in fetches + copies:
        copy.start()

    def scores_of(query, keys):
        return lax.dot_general(
            query, keys, (((1,), (1,)), ((), ())), preferred_element_type=jnp.float32
        )

    def with_ones(values):
        return jnp.concatenate([values, jnp.ones_like(values)], axis=1)

    for piece in range(ROW):
        for level in range(LEVELS):
            rows = pl.ds(piece * STACK + level * PIECE, PIECE)
            path_key_ref[rows, :HEAD_DIM] = far_ref[piece, level, :PIECE]
            path_value_ref[rows, :HEAD_DIM] = far_ref[piece, level, PIECE:]
    path_value_ref[:, HEAD_DIM:] = jnp.ones((PATH, HEAD_DIM), jnp.bfloat16)
    for copy in fetches:
        copy.wait()
    first = first_ref[0]
    _, depth0 = path_of(parents_ref, first)
    _, depth1 = path_of(parents_ref, first + 1)
    follows = jnp.where(parents_ref[first + 1] == first, 0.0, MASKED)
    row = lax.broadcasted_iota(jnp.int32, (PATH, HEAD_DIM), 0)
    lane = lax.broadcasted_iota(jnp.int32, (PATH, HEAD_DIM), 1)
    level = lax.rem(row // PIECE, LEVELS)
    limit = jnp.where(lane == 0, depth0, jnp.where(lane == 1, jnp.minimum(depth0, depth1), LEVELS))
    path_key_ref[:, HEAD_DIM:] = jnp.where(level < limit, 0.0, MASKED).astype(jnp.bfloat16)
    path_keys, path_values = path_key_ref[...], path_value_ref[...]

    rows = lax.broadcasted_iota(jnp.int32, (2 * SEG_LEN, HEAD_DIM), 0)
    lanes = lax.broadcasted_iota(jnp.int32, (2 * SEG_LEN, HEAD_DIM), 1)
    marks = (lanes == rows // SEG_LEN).astype(jnp.float32).astype(jnp.bfloat16)
    causal = lax.broadcasted_iota(jnp.int32, (SEG_LEN, SEG_LEN), 1) <= lax.broadcasted_iota(
        jnp.int32, (SEG_LEN, SEG_LEN), 0
    )
    halves = [slice(0, SEG_LEN), slice(SEG_LEN, 2 * SEG_LEN)]
    own_values = [with_ones(value_ref[half]) for half in halves]

    def share(head, mixture):
        for size, ref in zip(SHARED, shared):
            if 0 <= head < size:
                ref[:, head * HEAD_DIM : (head + 1) * HEAD_DIM] = mixture
            head -= size

    head = 0
    for part in earlier:
        for at in range(0, part.shape[1], HEAD_DIM):
            share(head, part[:, at : at + HEAD_DIM])
            head += 1
    for head in range(heads):
        query = query_ref[:, head * HEAD_DIM : (head + 1) * HEAD_DIM]
        path_scores = scores_of(jnp.concatenate([query, marks], axis=1), path_keys)
        own = [
            [(jnp.where(causal, scores_of(query[half], key_ref[half]), MASKED), values)]
            for half, values in zip(halves, own_values)
        ]
        own[1].append((scores_of(query[halves[1]], key_ref[halves[0]]) + follows, own_values[0]))
        path_weights, own_parts = [], []
        for half, blocks in zip(halves, own):
            row_max = functools.reduce(
                jnp.maximum,
                [jnp.max(s, axis=1, keepdims=True) for s, _ in blocks]
                + [jnp.max(path_scores[half], axis=1, keepdims=True)],
            )
            weigh = lambda s: jnp.exp2((s - row_max) * EXP2_SCALE).astype(jnp.bfloat16)
            path_weights.append(weigh(path_scores[half]))
            own_parts.append(
                sum(
                    jnp.dot(weigh(s), values, preferred_element_type=jnp.float32)
                    for s, values in blocks
                )
            )
        total = jnp.dot(
            jnp.concatenate(path_weights, axis=0), path_values, preferred_element_type=jnp.float32
        ) + jnp.concatenate(own_parts, axis=0)
        mixture = total[:, :HEAD_DIM] / total[:, HEAD_DIM:]
        mixture = mixture.astype(out_ref.dtype)
        out_ref[:, head * HEAD_DIM : (head + 1) * HEAD_DIM] = mixture
        share(first_head + head, mixture)
    for copy in copies:
        copy.wait()


def weight_copies(blocks, me_ref, weight_ref, held_ref, sem):
    block = weight_ref.shape[0] // 4
    copies = []
    for i, bit in enumerate(blocks):
        rows = pl.ds(pl.multiple_of((me_ref[0] ^ bit) * block, block), block)
        copies.append(
            pltpu.make_async_copy(
                weight_ref.at[rows], held_ref.at[pl.ds(i * block, block)], sem.at[i]
            )
        )
    return copies


def attend(first, parents, queries, keys, values, far, first_head, heads, blocks, bring, after, earlier):
    rows = queries.shape[0]
    pairs = heads * rows * (PATH + SEG_LEN + SEG_LEN // 2)
    out_shape = [jax.ShapeDtypeStruct((rows, heads * HEAD_DIM), jnp.bfloat16)]
    in_specs = [SMEM] + [HBM] * 4 + [VMEM]
    if earlier:
        out_shape += [jax.ShapeDtypeStruct((rows, n * HEAD_DIM), jnp.bfloat16) for n in SHARED]
    scratch = [pltpu.VMEM((PATH, 2 * HEAD_DIM), jnp.bfloat16)] * 2 + [
        pltpu.SMEM(parents.shape, parents.dtype),
        pltpu.VMEM((rows, heads * HEAD_DIM), queries.dtype),
        pltpu.VMEM(keys.shape, keys.dtype),
        pltpu.VMEM(values.shape, values.dtype),
        pltpu.SemaphoreType.DMA((4,)),
    ]
    if blocks:
        me, weight = bring
        bring = [me, in_hbm(weight)]
        in_specs += [SMEM, HBM]
        shape = (len(blocks) * weight.shape[0] // 4, weight.shape[1])
        out_shape.append(pltpu.VMEM(shape, weight.dtype))
        scratch.append(pltpu.SemaphoreType.DMA((len(blocks),)))
    else:
        bring = []
    return pl.pallas_call(
        functools.partial(attend_kernel, first_head, blocks, len(earlier)),
        out_shape=out_shape,
        in_specs=in_specs + [VMEM] * len(earlier) + [ANY] * len(after),
        out_specs=[VMEM] * len(out_shape),
        scratch_shapes=scratch,
        compiler_params=pltpu.CompilerParams(vmem_limit_bytes=ATTEND_VMEM),
        cost_estimate=pl.CostEstimate(
            flops=pairs * HEAD_DIM * 10,
            bytes_accessed=heads * rows * HEAD_DIM * 4 + 8 * PATH * HEAD_DIM,
            transcendentals=pairs,
        ),
        name="attend",
    )(
        first,
        in_hbm(parents),
        in_hbm(queries),
        in_hbm(keys),
        in_hbm(values),
        far,
        *bring,
        *earlier,
        *after,
    )


def project_kernel(counts, spans, has_base, near_ref, far_ref, *refs):
    parts = refs[: sum(counts)]
    out_ref, held_ref = refs[-2:]
    at, ends = 0, [0]
    for count in counts:
        for part in parts[:count]:
            held_ref[:, at : at + part.shape[1]] = part[...]
            at += part.shape[1]
        parts = parts[count:]
        ends.append(at)
    for column in range(0, out_ref.shape[1], TILE):
        columns = slice(column, column + TILE)
        total = refs[sum(counts)][:, columns] if has_base else None
        for (half, start), begin, end in zip(spans, ends, ends[1:]):
            product = jnp.dot(
                held_ref[:, begin:end],
                (near_ref, far_ref)[half][start : start + end - begin, columns],
                preferred_element_type=jnp.float32,
            )
            total = product if total is None else total + product
        out_ref[:, columns] = total.astype(out_ref.dtype)


def project(groups, spans, weights, base, dtype):
    parts = [part for group in groups for part in group]
    rows = parts[0].shape[0]
    depth = sum(part.shape[1] for part in parts)
    width = weights[0].shape[1]
    bases = [] if base is None else [base]
    return pl.pallas_call(
        functools.partial(project_kernel, [len(g) for g in groups], spans, base is not None),
        out_shape=jax.ShapeDtypeStruct((rows, width), dtype),
        in_specs=[VMEM] * (2 + len(parts) + len(bases)),
        out_specs=VMEM,
        scratch_shapes=[pltpu.VMEM((rows, depth), parts[0].dtype)],
        compiler_params=pltpu.CompilerParams(vmem_limit_bytes=PROJECT_VMEM),
        cost_estimate=pl.CostEstimate(
            flops=rows * width,
            bytes_accessed=rows * width,
            transcendentals=0,
        ),
        name="project",
    )(*[in_vmem(weight) for weight in weights], *parts, *bases)


def swap(part, bit):
    size = lax.axis_size("tensor")
    return lax.ppermute(part, "tensor", [(i, i ^ bit) for i in range(size)])


def trade(pieces):
    devices = lax.axis_size("dp")
    rows = [[at + place for place in LISTED] for at in range(0, devices, ROW)]
    return lax.all_to_all(pieces, "dp", 0, 0, tiled=True, axis_index_groups=rows)


def onward(piece, step):
    devices = lax.axis_size("dp")
    return lax.ppermute(piece, "dp", [(i, (i + step) % devices) for i in range(devices)])


def per_device(queries, key_proj, value_proj, out_weight, parents):
    me = lax.axis_index("tensor")
    first = (lax.axis_index("dp") * 2).astype(jnp.int32).reshape(1)
    pieces = trade(pack(key_proj, value_proj)).reshape(ROW_SEGS, 2 * PIECE, HEAD_DIM)
    to_next, to_second = carry_out(first, parents, pieces)
    inside = pick(first, parents, pieces)
    far = trade(merge(*inside, onward(to_next, ROW), onward(to_second, 2 * ROW)))

    width = queries.shape[1]
    bring = (me.astype(jnp.int32).reshape(1), out_weight)
    own, across, weights, head = [], [], [], 0
    for c, (size, blocks) in enumerate([(2, ()), (2, (0, 1)), (4, (2, 3))]):
        after = [across[c - 2]] if c >= 2 else []
        earlier = own if c == 2 else []
        part, *rest = attend(
            first, parents, queries, key_proj, value_proj, far, head, size, blocks, bring, after, earlier
        )
        weights += rest[len(rest) - len(blocks) // 2 :]
        own = rest[: len(SHARED)] if earlier else own + [part]
        across.append(swap(part, 2))
        head += size
    *own, across[0], across[1] = lax.optimization_barrier(own + across[:2])
    beside = [swap(part, 1) for part in own]
    corner = [swap(part, 1) for part in across[:-1]]
    total = project([own, across[:-1]], [(0, 0), (1, 0)], weights, None, jnp.float32)
    total = project(
        [beside, corner[:-1]], [(0, width), (1, width)], weights, total, jnp.float32
    )
    last, total, corner[-1] = lax.optimization_barrier((across[-1], total, corner[-1]))
    corner.append(swap(last, 1))
    done = width - last.shape[1]
    turned = sum(part.shape[1] for part in corner[:-2])
    return project(
        [[last], corner[-2:]], [(1, done), (1, width + turned)], weights, total, jnp.bfloat16
    )


def solution(mesh):
    placed = (P("dp", "tensor"), P("dp", "tensor"), P("dp", "tensor"), P(None, "tensor"), P())
    return jax.shard_map(
        per_device, mesh=mesh, in_specs=placed, out_specs=P("dp", "tensor"), check_vma=False
    )
```

```python
import functools
import math

import jax
import jax.numpy as jnp
from jax import lax
from jax.experimental import pallas as pl
from jax.experimental.pallas import tpu as pltpu
from jax.sharding import PartitionSpec as P

HEAD_DIM = 128
SEG_LEN = 256
LEVELS = 4
ROW = 8
ROW_SEGS = 2 * ROW
LISTED = (7, 3, 6, 2, 5, 1, 4, 0)
PIECE = SEG_LEN // ROW
PATH = LEVELS * SEG_LEN
STACK = LEVELS * PIECE
MASKED = -1e30
EXP2_SCALE = math.log2(math.e) * HEAD_DIM ** (-0.5)
SMALL_VMEM = 6 * 1024 * 1024
ATTEND_VMEM = 18 * 1024 * 1024
PROJECT_VMEM = 14 * 1024 * 1024
TILE = 256
SHARED = (3, 3, 2)

VMEM = pl.BlockSpec(memory_space=pltpu.VMEM)
SMEM = pl.BlockSpec(memory_space=pltpu.SMEM)
HBM = pl.BlockSpec(memory_space=pltpu.HBM)
FLAG_ROWS = 16


def in_hbm(array):
    return pltpu.with_memory_space_constraint(array, pltpu.HBM)


def in_vmem(array):
    return pltpu.with_memory_space_constraint(array, pltpu.VMEM)


def path_of(parents_ref, seg):
    path = [parents_ref[seg]]
    for _ in range(LEVELS - 1):
        up = parents_ref[jnp.maximum(path[-1], 0)]
        path.append(jnp.where(path[-1] >= 0, up, -1))
    depth = sum((p >= 0).astype(jnp.int32) for p in path)
    return path, depth


def level_of(path, depth, level):
    found = jnp.int32(0)
    for up in range(LEVELS):
        found = jnp.where(depth - 1 - up == level, path[up], found)
    return found


def pack_kernel(key_ref, value_ref, piece_ref, held_ref, sem):
    copies = [
        pltpu.make_async_copy(source, held_ref.at[i], sem.at[i])
        for i, source in enumerate([key_ref, value_ref])
    ]
    for copy in copies:
        copy.start()
    for i, copy in enumerate(copies):
        copy.wait()
        for piece in range(ROW):
            for seg in range(2):
                rows = pl.ds(seg * SEG_LEN + piece * PIECE, PIECE)
                piece_ref[piece, seg, i * PIECE : (i + 1) * PIECE] = held_ref[i, rows]


def pack(keys, values):
    return pl.pallas_call(
        pack_kernel,
        out_shape=jax.ShapeDtypeStruct((ROW, 2, 2 * PIECE, HEAD_DIM), keys.dtype),
        in_specs=[HBM, HBM],
        out_specs=VMEM,
        scratch_shapes=[pltpu.VMEM((2,) + keys.shape, keys.dtype), pltpu.SemaphoreType.DMA((2,))],
        compiler_params=pltpu.CompilerParams(vmem_limit_bytes=SMALL_VMEM),
        cost_estimate=pl.CostEstimate(flops=0, bytes_accessed=1 << 19, transcendentals=0),
        name="pack",
    )(in_hbm(keys), in_hbm(values))


def row_start(first_ref):
    return (first_ref[0] // ROW_SEGS) * ROW_SEGS


def slot_of(seg):
    place = seg // 2
    member = 2 * (ROW // 2 - 1 - place % (ROW // 2)) + 1 - place // (ROW // 2)
    return 2 * member + seg % 2


def bring_parents(source_ref, parents_ref, sem):
    copy = pltpu.make_async_copy(source_ref, parents_ref, sem)
    copy.start()
    copy.wait()


def carry_kernel(first_ref, source_ref, pieces_ref, next_ref, second_ref, parents_ref, sem):
    bring_parents(source_ref, parents_ref, sem)
    base = row_start(first_ref)
    last = parents_ref.shape[0] - 1

    def held(path, depth, level):
        return pieces_ref[slot_of(jnp.clip(level_of(path, depth, level) - base, 0, ROW_SEGS - 1))]

    path, depth = path_of(parents_ref, jnp.minimum(base + ROW_SEGS, last))
    for level in range(LEVELS):
        next_ref[level] = held(path, depth, level)
    path, depth = path_of(parents_ref, jnp.minimum(base + 2 * ROW_SEGS, last))
    second_ref[0] = held(path, depth, 0)


def carry_out(first, parents, pieces):
    shape = lambda n: jax.ShapeDtypeStruct((n,) + pieces.shape[1:], pieces.dtype)
    return pl.pallas_call(
        carry_kernel,
        out_shape=(shape(LEVELS), shape(1)),
        in_specs=[SMEM, HBM, VMEM],
        out_specs=(VMEM, VMEM),
        scratch_shapes=[pltpu.SMEM(parents.shape, parents.dtype), pltpu.SemaphoreType.DMA],
        compiler_params=pltpu.CompilerParams(vmem_limit_bytes=SMALL_VMEM),
        cost_estimate=pl.CostEstimate(flops=0, bytes_accessed=1 << 18, transcendentals=0),
        name="carry_out",
    )(first, in_hbm(parents), pieces)


def pick_kernel(
    first_ref, source_ref, pieces_ref, inside_ref, next_ref, second_ref, parents_ref, sem
):
    bring_parents(source_ref, parents_ref, sem)
    base = row_start(first_ref)
    ones = lambda on: jnp.full((FLAG_ROWS, HEAD_DIM), on, jnp.float32).astype(jnp.bfloat16)
    for target, place in enumerate(LISTED):
        path, depth = path_of(parents_ref, base + 2 * place)
        for level in range(LEVELS):
            seg = level_of(path, depth, level)
            within = seg >= base
            piece = pieces_ref[slot_of(jnp.maximum(seg - base, 0))]
            inside_ref[target, level] = jnp.where(within, piece, jnp.zeros_like(piece))
            before = jnp.logical_and(seg < base, seg >= base - ROW_SEGS)
            next_ref[target, level] = ones(jnp.where(before, 1.0, 0.0))
            if level == 0:
                second_ref[target] = ones(jnp.where(seg < base - ROW_SEGS, 1.0, 0.0))


def pick(first, parents, pieces):
    shape = lambda *dims: jax.ShapeDtypeStruct(dims, pieces.dtype)
    return pl.pallas_call(
        pick_kernel,
        out_shape=(
            shape(ROW, LEVELS, *pieces.shape[1:]),
            shape(ROW, LEVELS, FLAG_ROWS, HEAD_DIM),
            shape(ROW, FLAG_ROWS, HEAD_DIM),
        ),
        in_specs=[SMEM, HBM, VMEM],
        out_specs=(VMEM, VMEM, VMEM),
        scratch_shapes=[pltpu.SMEM(parents.shape, parents.dtype), pltpu.SemaphoreType.DMA],
        compiler_params=pltpu.CompilerParams(vmem_limit_bytes=SMALL_VMEM),
        cost_estimate=pl.CostEstimate(flops=0, bytes_accessed=1 << 20, transcendentals=0),
        name="pick",
    )(first, in_hbm(parents), pieces)


def merge_kernel(inside_ref, on_next_ref, on_second_ref, next_ref, second_ref, picked_ref):
    for level in range(LEVELS):
        for at in range(0, 2 * PIECE, FLAG_ROWS):
            rows = pl.ds(at, FLAG_ROWS)
            carried = next_ref[level, rows]
            older = second_ref[0, rows]
            for target in range(ROW):
                total = inside_ref[target, level, rows] + carried * on_next_ref[target, level]
                if level == 0:
                    total = total + older * on_second_ref[target]
                picked_ref[target, level, rows] = total


def merge(inside, on_next, on_second, carried, second):
    return pl.pallas_call(
        merge_kernel,
        out_shape=jax.ShapeDtypeStruct(inside.shape, inside.dtype),
        in_specs=[VMEM] * 5,
        out_specs=VMEM,
        compiler_params=pltpu.CompilerParams(vmem_limit_bytes=SMALL_VMEM),
        cost_estimate=pl.CostEstimate(flops=0, bytes_accessed=1 << 20, transcendentals=0),
        name="merge",
    )(inside, on_next, on_second, carried, second)


def attend_kernel(first_head, blocks, earlier, first_ref, *refs):
    sources, (far_ref, *refs) = refs[:4], refs[4:]
    if blocks:
        me_ref, weight_ref = refs[:2]
        weight_sem = refs.pop()
        held_ref = refs.pop(-8)
    earlier = refs[2 : 2 + earlier]
    shared = [refs.pop(-7 - n) for n in range(len(SHARED), 0, -1)] if earlier else []
    out_ref, path_key_ref, path_value_ref, parents_ref, query_ref, key_ref, value_ref, sem = refs[-8:]
    heads = query_ref.shape[1] // HEAD_DIM
    columns = pl.ds(first_head * HEAD_DIM, query_ref.shape[1])
    views = [sources[0], sources[1].at[:, columns], sources[2], sources[3]]
    fetches = [
        pltpu.make_async_copy(view, target, sem.at[i])
        for i, (view, target) in enumerate(zip(views, [parents_ref, query_ref, key_ref, value_ref]))
    ]
    copies = weight_copies(blocks, me_ref, weight_ref, held_ref, weight_sem) if blocks else []
    for copy in fetches + copies:
        copy.start()

    def scores_of(query, keys):
        return lax.dot_general(
            query, keys, (((1,), (1,)), ((), ())), preferred_element_type=jnp.float32
        )

    def with_ones(values):
        return jnp.concatenate([values, jnp.ones_like(values)], axis=1)

    for piece in range(ROW):
        for level in range(LEVELS):
            rows = pl.ds(piece * STACK + level * PIECE, PIECE)
            path_key_ref[rows, :HEAD_DIM] = far_ref[piece, level, :PIECE]
            path_value_ref[rows, :HEAD_DIM] = far_ref[piece, level, PIECE:]
    path_value_ref[:, HEAD_DIM:] = jnp.ones((PATH, HEAD_DIM), jnp.bfloat16)
    for copy in fetches:
        copy.wait()
    first = first_ref[0]
    _, depth0 = path_of(parents_ref, first)
    _, depth1 = path_of(parents_ref, first + 1)
    follows = jnp.where(parents_ref[first + 1] == first, 0.0, MASKED)
    row = lax.broadcasted_iota(jnp.int32, (PATH, HEAD_DIM), 0)
    lane = lax.broadcasted_iota(jnp.int32, (PATH, HEAD_DIM), 1)
    level = lax.rem(row // PIECE, LEVELS)
    limit = jnp.where(lane == 0, depth0, jnp.where(lane == 1, jnp.minimum(depth0, depth1), LEVELS))
    path_key_ref[:, HEAD_DIM:] = jnp.where(level < limit, 0.0, MASKED).astype(jnp.bfloat16)
    path_keys, path_values = path_key_ref[...], path_value_ref[...]

    rows = lax.broadcasted_iota(jnp.int32, (2 * SEG_LEN, HEAD_DIM), 0)
    lanes = lax.broadcasted_iota(jnp.int32, (2 * SEG_LEN, HEAD_DIM), 1)
    marks = (lanes == rows // SEG_LEN).astype(jnp.float32).astype(jnp.bfloat16)
    causal = lax.broadcasted_iota(jnp.int32, (SEG_LEN, SEG_LEN), 1) <= lax.broadcasted_iota(
        jnp.int32, (SEG_LEN, SEG_LEN), 0
    )
    halves = [slice(0, SEG_LEN), slice(SEG_LEN, 2 * SEG_LEN)]
    own_values = [with_ones(value_ref[half]) for half in halves]

    def share(head, mixture):
        for size, ref in zip(SHARED, shared):
            if 0 <= head < size:
                ref[:, head * HEAD_DIM : (head + 1) * HEAD_DIM] = mixture
            head -= size

    head = 0
    for part in earlier:
        for at in range(0, part.shape[1], HEAD_DIM):
            share(head, part[:, at : at + HEAD_DIM])
            head += 1
    for head in range(heads):
        query = query_ref[:, head * HEAD_DIM : (head + 1) * HEAD_DIM]
        path_scores = scores_of(jnp.concatenate([query, marks], axis=1), path_keys)
        own = [
            [(jnp.where(causal, scores_of(query[half], key_ref[half]), MASKED), values)]
            for half, values in zip(halves, own_values)
        ]
        own[1].append((scores_of(query[halves[1]], key_ref[halves[0]]) + follows, own_values[0]))
        path_weights, own_parts = [], []
        for half, blocks in zip(halves, own):
            row_max = functools.reduce(
                jnp.maximum,
                [jnp.max(s, axis=1, keepdims=True) for s, _ in blocks]
                + [jnp.max(path_scores[half], axis=1, keepdims=True)],
            )
            weigh = lambda s: jnp.exp2((s - row_max) * EXP2_SCALE).astype(jnp.bfloat16)
            path_weights.append(weigh(path_scores[half]))
            own_parts.append(
                sum(
                    jnp.dot(weigh(s), values, preferred_element_type=jnp.float32)
                    for s, values in blocks
                )
            )
        total = jnp.dot(
            jnp.concatenate(path_weights, axis=0), path_values, preferred_element_type=jnp.float32
        ) + jnp.concatenate(own_parts, axis=0)
        mixture = total[:, :HEAD_DIM] / total[:, HEAD_DIM:]
        mixture = mixture.astype(out_ref.dtype)
        out_ref[:, head * HEAD_DIM : (head + 1) * HEAD_DIM] = mixture
        share(first_head + head, mixture)
    for copy in copies:
        copy.wait()


def weight_copies(blocks, me_ref, weight_ref, held_ref, sem):
    block = weight_ref.shape[0] // 4
    copies = []
    for i, bit in enumerate(blocks):
        rows = pl.ds(pl.multiple_of((me_ref[0] ^ bit) * block, block), block)
        copies.append(
            pltpu.make_async_copy(
                weight_ref.at[rows], held_ref.at[pl.ds(i * block, block)], sem.at[i]
            )
        )
    return copies


def attend(first, parents, queries, keys, values, far, first_head, heads, blocks, bring, earlier):
    rows = queries.shape[0]
    pairs = heads * rows * (PATH + SEG_LEN + SEG_LEN // 2)
    out_shape = [jax.ShapeDtypeStruct((rows, heads * HEAD_DIM), jnp.bfloat16)]
    in_specs = [SMEM] + [HBM] * 4 + [VMEM]
    if earlier:
        out_shape += [jax.ShapeDtypeStruct((rows, n * HEAD_DIM), jnp.bfloat16) for n in SHARED]
    scratch = [pltpu.VMEM((PATH, 2 * HEAD_DIM), jnp.bfloat16)] * 2 + [
        pltpu.SMEM(parents.shape, parents.dtype),
        pltpu.VMEM((rows, heads * HEAD_DIM), queries.dtype),
        pltpu.VMEM(keys.shape, keys.dtype),
        pltpu.VMEM(values.shape, values.dtype),
        pltpu.SemaphoreType.DMA((4,)),
    ]
    if blocks:
        me, weight = bring
        bring = [me, in_hbm(weight)]
        in_specs += [SMEM, HBM]
        shape = (len(blocks) * weight.shape[0] // 4, weight.shape[1])
        out_shape.append(pltpu.VMEM(shape, weight.dtype))
        scratch.append(pltpu.SemaphoreType.DMA((len(blocks),)))
    else:
        bring = []
    return pl.pallas_call(
        functools.partial(attend_kernel, first_head, blocks, len(earlier)),
        out_shape=out_shape,
        in_specs=in_specs + [VMEM] * len(earlier),
        out_specs=[VMEM] * len(out_shape),
        scratch_shapes=scratch,
        compiler_params=pltpu.CompilerParams(vmem_limit_bytes=ATTEND_VMEM),
        cost_estimate=pl.CostEstimate(
            flops=pairs * HEAD_DIM * 10,
            bytes_accessed=heads * rows * HEAD_DIM * 4 + 8 * PATH * HEAD_DIM,
            transcendentals=pairs,
        ),
        name="attend",
    )(
        first,
        in_hbm(parents),
        in_hbm(queries),
        in_hbm(keys),
        in_hbm(values),
        far,
        *bring,
        *earlier,
    )


def project_kernel(counts, spans, has_base, near_ref, far_ref, *refs):
    parts = refs[: sum(counts)]
    out_ref, held_ref = refs[-2:]
    at, ends = 0, [0]
    for count in counts:
        for part in parts[:count]:
            held_ref[:, at : at + part.shape[1]] = part[...]
            at += part.shape[1]
        parts = parts[count:]
        ends.append(at)
    for column in range(0, out_ref.shape[1], TILE):
        columns = slice(column, column + TILE)
        total = refs[sum(counts)][:, columns] if has_base else None
        for (half, start), begin, end in zip(spans, ends, ends[1:]):
            product = jnp.dot(
                held_ref[:, begin:end],
                (near_ref, far_ref)[half][start : start + end - begin, columns],
                preferred_element_type=jnp.float32,
            )
            total = product if total is None else total + product
        out_ref[:, columns] = total.astype(out_ref.dtype)


def project(groups, spans, weights, base, dtype):
    parts = [part for group in groups for part in group]
    rows = parts[0].shape[0]
    depth = sum(part.shape[1] for part in parts)
    width = weights[0].shape[1]
    bases = [] if base is None else [base]
    return pl.pallas_call(
        functools.partial(project_kernel, [len(g) for g in groups], spans, base is not None),
        out_shape=jax.ShapeDtypeStruct((rows, width), dtype),
        in_specs=[VMEM] * (2 + len(parts) + len(bases)),
        out_specs=VMEM,
        scratch_shapes=[pltpu.VMEM((rows, depth), parts[0].dtype)],
        compiler_params=pltpu.CompilerParams(vmem_limit_bytes=PROJECT_VMEM),
        cost_estimate=pl.CostEstimate(
            flops=rows * width,
            bytes_accessed=rows * width,
            transcendentals=0,
        ),
        name="project",
    )(*[in_vmem(weight) for weight in weights], *parts, *bases)


def swap(part, bit):
    size = lax.axis_size("tensor")
    return lax.ppermute(part, "tensor", [(i, i ^ bit) for i in range(size)])


def trade(pieces):
    devices = lax.axis_size("dp")
    rows = [[at + place for place in LISTED] for at in range(0, devices, ROW)]
    return lax.all_to_all(pieces, "dp", 0, 0, tiled=True, axis_index_groups=rows)


def onward(piece, step):
    devices = lax.axis_size("dp")
    return lax.ppermute(piece, "dp", [(i, (i + step) % devices) for i in range(devices)])


def per_device(queries, key_proj, value_proj, out_weight, parents):
    me = lax.axis_index("tensor")
    first = (lax.axis_index("dp") * 2).astype(jnp.int32).reshape(1)
    pieces = trade(pack(key_proj, value_proj)).reshape(ROW_SEGS, 2 * PIECE, HEAD_DIM)
    to_next, to_second = carry_out(first, parents, pieces)
    inside = pick(first, parents, pieces)
    far = trade(merge(*inside, onward(to_next, ROW), onward(to_second, 2 * ROW)))

    width = queries.shape[1]
    bring = (me.astype(jnp.int32).reshape(1), out_weight)
    own, across, weights, head = [], [], [], 0
    for c, (size, blocks) in enumerate([(2, ()), (2, (0, 1)), (4, (2, 3))]):
        earlier = own if c == 2 else []
        part, *rest = attend(
            first, parents, queries, key_proj, value_proj, far, head, size, blocks, bring, earlier
        )
        weights += rest[len(rest) - len(blocks) // 2 :]
        own = rest[: len(SHARED)] if earlier else own + [part]
        across.append(swap(part, 2))
        head += size
    *own, across[0], across[1] = lax.optimization_barrier(own + across[:2])
    beside = [swap(part, 1) for part in own]
    corner = [swap(part, 1) for part in across[:-1]]
    total = project([own, across[:-1]], [(0, 0), (1, 0)], weights, None, jnp.float32)
    total = project(
        [beside, corner[:-1]], [(0, width), (1, width)], weights, total, jnp.float32
    )
    last, total = lax.optimization_barrier((across[-1], total))
    corner.append(swap(last, 1))
    done = width - last.shape[1]
    turned = sum(part.shape[1] for part in corner[:-2])
    return project(
        [[last], corner[-2:]], [(1, done), (1, width + turned)], weights, total, jnp.bfloat16
    )


def solution(mesh):
    placed = (P("dp", "tensor"), P("dp", "tensor"), P("dp", "tensor"), P(None, "tensor"), P())
    return jax.shard_map(
        per_device, mesh=mesh, in_specs=placed, out_specs=P("dp", "tensor"), check_vma=False
    )
```

```python
import functools
import math

import jax
import jax.numpy as jnp
from jax import lax
from jax.experimental import pallas as pl
from jax.experimental.pallas import tpu as pltpu
from jax.sharding import PartitionSpec as P

HEAD_DIM = 128
SEG_LEN = 256
LEVELS = 4
ROW = 8
ROW_SEGS = 2 * ROW
LISTED = (7, 3, 6, 2, 5, 1, 4, 0)
PIECE = SEG_LEN // ROW
PATH = LEVELS * SEG_LEN
STACK = LEVELS * PIECE
MASKED = -1e30
EXP2_SCALE = math.log2(math.e) * HEAD_DIM ** (-0.5)
SMALL_VMEM = 6 * 1024 * 1024
ATTEND_VMEM = 18 * 1024 * 1024
PROJECT_VMEM = 14 * 1024 * 1024
TILE = 256
SHARED = (3, 3, 2)

VMEM = pl.BlockSpec(memory_space=pltpu.VMEM)
SMEM = pl.BlockSpec(memory_space=pltpu.SMEM)
ANY = pl.BlockSpec(memory_space=pl.ANY)
HBM = pl.BlockSpec(memory_space=pltpu.HBM)
FLAG_ROWS = 16


def in_hbm(array):
    return pltpu.with_memory_space_constraint(array, pltpu.HBM)


def in_vmem(array):
    return pltpu.with_memory_space_constraint(array, pltpu.VMEM)


def path_of(parents_ref, seg):
    path = [parents_ref[seg]]
    for _ in range(LEVELS - 1):
        up = parents_ref[jnp.maximum(path[-1], 0)]
        path.append(jnp.where(path[-1] >= 0, up, -1))
    depth = sum((p >= 0).astype(jnp.int32) for p in path)
    return path, depth


def level_of(path, depth, level):
    found = jnp.int32(0)
    for up in range(LEVELS):
        found = jnp.where(depth - 1 - up == level, path[up], found)
    return found


def pack_kernel(key_ref, value_ref, piece_ref, sem):
    copies = []
    for piece in range(ROW):
        for seg in range(2):
            rows = pl.ds(seg * SEG_LEN + piece * PIECE, PIECE)
            for i, source in enumerate([key_ref, value_ref]):
                copies.append(
                    pltpu.make_async_copy(
                        source.at[rows],
                        piece_ref.at[piece, seg, pl.ds(i * PIECE, PIECE)],
                        sem.at[len(copies)],
                    )
                )
    for copy in copies:
        copy.start()
    for copy in copies:
        copy.wait()


def pack(keys, values):
    return pl.pallas_call(
        pack_kernel,
        out_shape=jax.ShapeDtypeStruct((ROW, 2, 2 * PIECE, HEAD_DIM), keys.dtype),
        in_specs=[HBM, HBM],
        out_specs=VMEM,
        scratch_shapes=[pltpu.SemaphoreType.DMA((4 * ROW,))],
        compiler_params=pltpu.CompilerParams(vmem_limit_bytes=SMALL_VMEM),
        cost_estimate=pl.CostEstimate(flops=0, bytes_accessed=1 << 19, transcendentals=0),
        name="pack",
    )(in_hbm(keys), in_hbm(values))


def row_start(first_ref):
    return (first_ref[0] // ROW_SEGS) * ROW_SEGS


def slot_of(seg):
    place = seg // 2
    member = 2 * (ROW // 2 - 1 - place % (ROW // 2)) + 1 - place // (ROW // 2)
    return 2 * member + seg % 2


def bring_parents(source_ref, parents_ref, sem):
    copy = pltpu.make_async_copy(source_ref, parents_ref, sem)
    copy.start()
    copy.wait()


def carry_kernel(first_ref, source_ref, pieces_ref, next_ref, second_ref, parents_ref, sem):
    bring_parents(source_ref, parents_ref, sem)
    base = row_start(first_ref)
    last = parents_ref.shape[0] - 1

    def held(path, depth, level):
        return pieces_ref[slot_of(jnp.clip(level_of(path, depth, level) - base, 0, ROW_SEGS - 1))]

    path, depth = path_of(parents_ref, jnp.minimum(base + ROW_SEGS, last))
    for level in range(LEVELS):
        next_ref[level] = held(path, depth, level)
    path, depth = path_of(parents_ref, jnp.minimum(base + 2 * ROW_SEGS, last))
    second_ref[0] = held(path, depth, 0)


def carry_out(first, parents, pieces):
    shape = lambda n: jax.ShapeDtypeStruct((n,) + pieces.shape[1:], pieces.dtype)
    return pl.pallas_call(
        carry_kernel,
        out_shape=(shape(LEVELS), shape(1)),
        in_specs=[SMEM, HBM, VMEM],
        out_specs=(VMEM, VMEM),
        scratch_shapes=[pltpu.SMEM(parents.shape, parents.dtype), pltpu.SemaphoreType.DMA],
        compiler_params=pltpu.CompilerParams(vmem_limit_bytes=SMALL_VMEM),
        cost_estimate=pl.CostEstimate(flops=0, bytes_accessed=1 << 18, transcendentals=0),
        name="carry_out",
    )(first, in_hbm(parents), pieces)


def pick_kernel(
    first_ref, source_ref, pieces_ref, inside_ref, next_ref, second_ref, parents_ref, sem
):
    bring_parents(source_ref, parents_ref, sem)
    base = row_start(first_ref)
    ones = lambda on: jnp.full((FLAG_ROWS, HEAD_DIM), on, jnp.float32).astype(jnp.bfloat16)
    for target, place in enumerate(LISTED):
        path, depth = path_of(parents_ref, base + 2 * place)
        for level in range(LEVELS):
            seg = level_of(path, depth, level)
            within = seg >= base
            piece = pieces_ref[slot_of(jnp.maximum(seg - base, 0))]
            inside_ref[target, level] = jnp.where(within, piece, jnp.zeros_like(piece))
            before = jnp.logical_and(seg < base, seg >= base - ROW_SEGS)
            next_ref[target, level] = ones(jnp.where(before, 1.0, 0.0))
            if level == 0:
                second_ref[target] = ones(jnp.where(seg < base - ROW_SEGS, 1.0, 0.0))


def pick(first, parents, pieces):
    shape = lambda *dims: jax.ShapeDtypeStruct(dims, pieces.dtype)
    return pl.pallas_call(
        pick_kernel,
        out_shape=(
            shape(ROW, LEVELS, *pieces.shape[1:]),
            shape(ROW, LEVELS, FLAG_ROWS, HEAD_DIM),
            shape(ROW, FLAG_ROWS, HEAD_DIM),
        ),
        in_specs=[SMEM, HBM, VMEM],
        out_specs=(VMEM, VMEM, VMEM),
        scratch_shapes=[pltpu.SMEM(parents.shape, parents.dtype), pltpu.SemaphoreType.DMA],
        compiler_params=pltpu.CompilerParams(vmem_limit_bytes=SMALL_VMEM),
        cost_estimate=pl.CostEstimate(flops=0, bytes_accessed=1 << 20, transcendentals=0),
        name="pick",
    )(first, in_hbm(parents), pieces)


def merge_kernel(inside_ref, on_next_ref, on_second_ref, next_ref, second_ref, picked_ref):
    for level in range(LEVELS):
        for at in range(0, 2 * PIECE, FLAG_ROWS):
            rows = pl.ds(at, FLAG_ROWS)
            carried = next_ref[level, rows]
            older = second_ref[0, rows]
            for target in range(ROW):
                total = inside_ref[target, level, rows] + carried * on_next_ref[target, level]
                if level == 0:
                    total = total + older * on_second_ref[target]
                picked_ref[target, level, rows] = total


def merge(inside, on_next, on_second, carried, second):
    return pl.pallas_call(
        merge_kernel,
        out_shape=jax.ShapeDtypeStruct(inside.shape, inside.dtype),
        in_specs=[VMEM] * 5,
        out_specs=VMEM,
        compiler_params=pltpu.CompilerParams(vmem_limit_bytes=SMALL_VMEM),
        cost_estimate=pl.CostEstimate(flops=0, bytes_accessed=1 << 20, transcendentals=0),
        name="merge",
    )(inside, on_next, on_second, carried, second)


def attend_kernel(first_head, earlier, first_ref, *refs):
    sources, (far_ref, *refs) = refs[:4], refs[4:]
    earlier = refs[:earlier]
    shared = [refs.pop(-7 - n) for n in range(len(SHARED), 0, -1)] if earlier else []
    out_ref, path_key_ref, path_value_ref, parents_ref, query_ref, key_ref, value_ref, sem = refs[-8:]
    heads = query_ref.shape[1] // HEAD_DIM
    columns = pl.ds(first_head * HEAD_DIM, query_ref.shape[1])
    views = [sources[0], sources[1].at[:, columns], sources[2], sources[3]]
    fetches = [
        pltpu.make_async_copy(view, target, sem.at[i])
        for i, (view, target) in enumerate(zip(views, [parents_ref, query_ref, key_ref, value_ref]))
    ]
    for copy in fetches:
        copy.start()

    def scores_of(query, keys):
        return lax.dot_general(
            query, keys, (((1,), (1,)), ((), ())), preferred_element_type=jnp.float32
        )

    def with_ones(values):
        return jnp.concatenate([values, jnp.ones_like(values)], axis=1)

    for piece in range(ROW):
        for level in range(LEVELS):
            rows = pl.ds(piece * STACK + level * PIECE, PIECE)
            path_key_ref[rows, :HEAD_DIM] = far_ref[piece, level, :PIECE]
            path_value_ref[rows, :HEAD_DIM] = far_ref[piece, level, PIECE:]
    path_value_ref[:, HEAD_DIM:] = jnp.ones((PATH, HEAD_DIM), jnp.bfloat16)
    for copy in fetches:
        copy.wait()
    first = first_ref[0]
    _, depth0 = path_of(parents_ref, first)
    _, depth1 = path_of(parents_ref, first + 1)
    follows = jnp.where(parents_ref[first + 1] == first, 0.0, MASKED)
    row = lax.broadcasted_iota(jnp.int32, (PATH, HEAD_DIM), 0)
    lane = lax.broadcasted_iota(jnp.int32, (PATH, HEAD_DIM), 1)
    level = lax.rem(row // PIECE, LEVELS)
    limit = jnp.where(lane == 0, depth0, jnp.where(lane == 1, jnp.minimum(depth0, depth1), LEVELS))
    path_key_ref[:, HEAD_DIM:] = jnp.where(level < limit, 0.0, MASKED).astype(jnp.bfloat16)
    path_keys, path_values = path_key_ref[...], path_value_ref[...]

    rows = lax.broadcasted_iota(jnp.int32, (2 * SEG_LEN, HEAD_DIM), 0)
    lanes = lax.broadcasted_iota(jnp.int32, (2 * SEG_LEN, HEAD_DIM), 1)
    marks = (lanes == rows // SEG_LEN).astype(jnp.float32).astype(jnp.bfloat16)
    causal = lax.broadcasted_iota(jnp.int32, (SEG_LEN, SEG_LEN), 1) <= lax.broadcasted_iota(
        jnp.int32, (SEG_LEN, SEG_LEN), 0
    )
    halves = [slice(0, SEG_LEN), slice(SEG_LEN, 2 * SEG_LEN)]
    own_values = [with_ones(value_ref[half]) for half in halves]

    def share(head, mixture):
        for size, ref in zip(SHARED, shared):
            if 0 <= head < size:
                ref[:, head * HEAD_DIM : (head + 1) * HEAD_DIM] = mixture
            head -= size

    head = 0
    for part in earlier:
        for at in range(0, part.shape[1], HEAD_DIM):
            share(head, part[:, at : at + HEAD_DIM])
            head += 1
    for head in range(heads):
        query = query_ref[:, head * HEAD_DIM : (head + 1) * HEAD_DIM]
        path_scores = scores_of(jnp.concatenate([query, marks], axis=1), path_keys)
        own = [
            [(jnp.where(causal, scores_of(query[half], key_ref[half]), MASKED), values)]
            for half, values in zip(halves, own_values)
        ]
        own[1].append((scores_of(query[halves[1]], key_ref[halves[0]]) + follows, own_values[0]))
        path_weights, own_parts = [], []
        for half, blocks in zip(halves, own):
            row_max = functools.reduce(
                jnp.maximum,
                [jnp.max(s, axis=1, keepdims=True) for s, _ in blocks]
                + [jnp.max(path_scores[half], axis=1, keepdims=True)],
            )
            weigh = lambda s: jnp.exp2((s - row_max) * EXP2_SCALE).astype(jnp.bfloat16)
            path_weights.append(weigh(path_scores[half]))
            own_parts.append(
                sum(
                    jnp.dot(weigh(s), values, preferred_element_type=jnp.float32)
                    for s, values in blocks
                )
            )
        total = jnp.dot(
            jnp.concatenate(path_weights, axis=0), path_values, preferred_element_type=jnp.float32
        ) + jnp.concatenate(own_parts, axis=0)
        mixture = total[:, :HEAD_DIM] / total[:, HEAD_DIM:]
        mixture = mixture.astype(out_ref.dtype)
        out_ref[:, head * HEAD_DIM : (head + 1) * HEAD_DIM] = mixture
        share(first_head + head, mixture)


def attend(first, parents, queries, keys, values, far, first_head, heads, earlier, after):
    rows = queries.shape[0]
    pairs = heads * rows * (PATH + SEG_LEN + SEG_LEN // 2)
    out_shape = [jax.ShapeDtypeStruct((rows, heads * HEAD_DIM), jnp.bfloat16)]
    in_specs = [SMEM] + [HBM] * 4 + [VMEM]
    if earlier:
        out_shape += [jax.ShapeDtypeStruct((rows, n * HEAD_DIM), jnp.bfloat16) for n in SHARED]
    scratch = [pltpu.VMEM((PATH, 2 * HEAD_DIM), jnp.bfloat16)] * 2 + [
        pltpu.SMEM(parents.shape, parents.dtype),
        pltpu.VMEM((rows, heads * HEAD_DIM), queries.dtype),
        pltpu.VMEM(keys.shape, keys.dtype),
        pltpu.VMEM(values.shape, values.dtype),
        pltpu.SemaphoreType.DMA((4,)),
    ]
    return pl.pallas_call(
        functools.partial(attend_kernel, first_head, len(earlier)),
        out_shape=out_shape,
        in_specs=in_specs + [VMEM] * len(earlier) + [ANY] * len(after),
        out_specs=[VMEM] * len(out_shape),
        scratch_shapes=scratch,
        compiler_params=pltpu.CompilerParams(vmem_limit_bytes=ATTEND_VMEM),
        cost_estimate=pl.CostEstimate(
            flops=pairs * HEAD_DIM * 10,
            bytes_accessed=heads * rows * HEAD_DIM * 4 + 8 * PATH * HEAD_DIM,
            transcendentals=pairs,
        ),
        name="attend",
    )(
        first,
        in_hbm(parents),
        in_hbm(queries),
        in_hbm(keys),
        in_hbm(values),
        far,
        *earlier,
        *after,
    )


def gather_parts(parts, held_ref):
    at = 0
    for part in parts:
        held_ref[:, at : at + part.shape[1]] = part[...]
        at += part.shape[1]


def first_kernel(counts, me_ref, weight_ref, *refs):
    parts = refs[: sum(counts)]
    out_ref, kept_ref, own_ref, held_ref, sem = refs[sum(counts) :]
    block = own_ref.shape[0]
    copies = []
    for bit in range(4):
        rows = pl.ds(pl.multiple_of((me_ref[0] ^ bit) * block, block), block)
        target = kept_ref.at[pl.ds((bit - 1) * block, block)] if bit else own_ref
        copies.append(pltpu.make_async_copy(weight_ref.at[rows], target, sem.at[bit]))
    for bit in (0, 2, 1, 3):
        copies[bit].start()
    gather_parts(parts, held_ref)
    tiles = [slice(at, at + TILE) for at in range(0, out_ref.shape[1], TILE)]
    copies[0].wait()
    for columns in tiles:
        out_ref[:, columns] = jnp.dot(
            held_ref[:, :block], own_ref[:, columns], preferred_element_type=jnp.float32
        )
    copies[2].wait()
    depth = held_ref.shape[1] - block
    for columns in tiles:
        out_ref[:, columns] += jnp.dot(
            held_ref[:, block:],
            kept_ref[block : block + depth, columns],
            preferred_element_type=jnp.float32,
        )
    copies[1].wait()
    copies[3].wait()


def first_project(me, weight, own, across):
    parts = own + across
    rows = parts[0].shape[0]
    depth = sum(part.shape[1] for part in parts)
    full, width = weight.shape
    return pl.pallas_call(
        functools.partial(first_kernel, [len(own), len(across)]),
        out_shape=(
            jax.ShapeDtypeStruct((rows, width), jnp.float32),
            pltpu.VMEM((3 * full // 4, width), weight.dtype),
        ),
        in_specs=[SMEM, HBM] + [VMEM] * len(parts),
        out_specs=(VMEM, VMEM),
        scratch_shapes=[
            pltpu.VMEM((full // 4, width), weight.dtype),
            pltpu.VMEM((rows, depth), parts[0].dtype),
            pltpu.SemaphoreType.DMA((4,)),
        ],
        compiler_params=pltpu.CompilerParams(vmem_limit_bytes=PROJECT_VMEM),
        cost_estimate=pl.CostEstimate(
            flops=rows * width, bytes_accessed=rows * width, transcendentals=0
        ),
        name="first_project",
    )(me, in_hbm(weight), *parts)


def project_kernel(counts, spans, weight_ref, *refs):
    parts = refs[: sum(counts)]
    base_ref, out_ref, held_ref = refs[-3:]
    gather_parts(parts, held_ref)
    ends = [0]
    for count in counts:
        ends.append(ends[-1] + sum(part.shape[1] for part in parts[:count]))
        parts = parts[count:]
    for column in range(0, out_ref.shape[1], TILE):
        columns = slice(column, column + TILE)
        total = base_ref[:, columns]
        for start, begin, end in zip(spans, ends, ends[1:]):
            total = total + jnp.dot(
                held_ref[:, begin:end],
                weight_ref[start : start + end - begin, columns],
                preferred_element_type=jnp.float32,
            )
        out_ref[:, columns] = total.astype(out_ref.dtype)


def project(groups, spans, weight, base, dtype):
    parts = [part for group in groups for part in group]
    rows = parts[0].shape[0]
    depth = sum(part.shape[1] for part in parts)
    width = weight.shape[1]
    return pl.pallas_call(
        functools.partial(project_kernel, [len(g) for g in groups], spans),
        out_shape=jax.ShapeDtypeStruct((rows, width), dtype),
        in_specs=[VMEM] * (2 + len(parts)),
        out_specs=VMEM,
        scratch_shapes=[pltpu.VMEM((rows, depth), parts[0].dtype)],
        compiler_params=pltpu.CompilerParams(vmem_limit_bytes=PROJECT_VMEM),
        cost_estimate=pl.CostEstimate(
            flops=rows * width, bytes_accessed=rows * width, transcendentals=0
        ),
        name="project",
    )(in_vmem(weight), *parts, base)


def swap(part, bit):
    size = lax.axis_size("tensor")
    return lax.ppermute(part, "tensor", [(i, i ^ bit) for i in range(size)])


def trade(pieces):
    devices = lax.axis_size("dp")
    rows = [[at + place for place in LISTED] for at in range(0, devices, ROW)]
    return lax.all_to_all(pieces, "dp", 0, 0, tiled=True, axis_index_groups=rows)


def onward(piece, step):
    devices = lax.axis_size("dp")
    return lax.ppermute(piece, "dp", [(i, (i + step) % devices) for i in range(devices)])


def per_device(queries, key_proj, value_proj, out_weight, parents):
    me = lax.axis_index("tensor")
    first = (lax.axis_index("dp") * 2).astype(jnp.int32).reshape(1)
    pieces = trade(pack(key_proj, value_proj)).reshape(ROW_SEGS, 2 * PIECE, HEAD_DIM)
    to_next, to_second = carry_out(first, parents, pieces)
    inside = pick(first, parents, pieces)
    far = trade(merge(*inside, onward(to_next, ROW), onward(to_second, 2 * ROW)))

    width = queries.shape[1]
    own, across, head = [], [], 0
    for c, size in enumerate((2, 2, 4)):
        earlier = own if c == 2 else []
        part, *rest = attend(
            first, parents, queries, key_proj, value_proj, far, head, size, earlier, across[: c - 1]
        )
        own = rest if earlier else own + [part]
        across.append(swap(part, 2))
        head += size
    *own, across[0], across[1] = lax.optimization_barrier(own + across[:2])
    beside = [swap(part, 1) for part in own]
    corner = [swap(part, 1) for part in across[:-1]]
    total, weight = first_project(me.astype(jnp.int32).reshape(1), out_weight, own, across[:-1])
    total = project([beside, corner[:-1]], [0, 2 * width], weight, total, jnp.float32)
    last, total = lax.optimization_barrier((across[-1], total))
    corner.append(swap(last, 1))
    done = width - last.shape[1]
    turned = sum(part.shape[1] for part in corner[:-2])
    return project(
        [[last], corner[-2:]], [width + done, 2 * width + turned], weight, total, jnp.bfloat16
    )


def solution(mesh):
    placed = (P("dp", "tensor"), P("dp", "tensor"), P("dp", "tensor"), P(None, "tensor"), P())
    return jax.shard_map(
        per_device, mesh=mesh, in_specs=placed, out_specs=P("dp", "tensor"), check_vma=False
    )
```

```python
import functools
import math

import jax
import jax.numpy as jnp
from jax import lax
from jax.experimental import pallas as pl
from jax.experimental.pallas import tpu as pltpu
from jax.sharding import PartitionSpec as P

HEAD_DIM = 128
SEG_LEN = 256
LEVELS = 4
ROW = 8
ROW_SEGS = 2 * ROW
LISTED = (7, 3, 6, 2, 5, 1, 4, 0)
PIECE = SEG_LEN // ROW
PATH = LEVELS * SEG_LEN
STACK = LEVELS * PIECE
MASKED = -1e30
EXP2_SCALE = math.log2(math.e) * HEAD_DIM ** (-0.5)
SMALL_VMEM = 6 * 1024 * 1024
ATTEND_VMEM = 18 * 1024 * 1024
PROJECT_VMEM = 14 * 1024 * 1024
TILE = 256

VMEM = pl.BlockSpec(memory_space=pltpu.VMEM)
SMEM = pl.BlockSpec(memory_space=pltpu.SMEM)
ANY = pl.BlockSpec(memory_space=pl.ANY)
HBM = pl.BlockSpec(memory_space=pltpu.HBM)
FLAG_ROWS = 16


def in_hbm(array):
    return pltpu.with_memory_space_constraint(array, pltpu.HBM)


def in_vmem(array):
    return pltpu.with_memory_space_constraint(array, pltpu.VMEM)


def path_of(parents_ref, seg):
    path = [parents_ref[seg]]
    for _ in range(LEVELS - 1):
        up = parents_ref[jnp.maximum(path[-1], 0)]
        path.append(jnp.where(path[-1] >= 0, up, -1))
    depth = sum((p >= 0).astype(jnp.int32) for p in path)
    return path, depth


def level_of(path, depth, level):
    found = jnp.int32(0)
    for up in range(LEVELS):
        found = jnp.where(depth - 1 - up == level, path[up], found)
    return found


def pack_kernel(key_ref, value_ref, piece_ref, held_ref, sem):
    copies = [
        pltpu.make_async_copy(source, held_ref.at[i], sem.at[i])
        for i, source in enumerate([key_ref, value_ref])
    ]
    for copy in copies:
        copy.start()
    for i, copy in enumerate(copies):
        copy.wait()
        for piece in range(ROW):
            for seg in range(2):
                rows = pl.ds(seg * SEG_LEN + piece * PIECE, PIECE)
                piece_ref[piece, seg, i * PIECE : (i + 1) * PIECE] = held_ref[i, rows]


def pack(keys, values):
    return pl.pallas_call(
        pack_kernel,
        out_shape=jax.ShapeDtypeStruct((ROW, 2, 2 * PIECE, HEAD_DIM), keys.dtype),
        in_specs=[HBM, HBM],
        out_specs=VMEM,
        scratch_shapes=[pltpu.VMEM((2,) + keys.shape, keys.dtype), pltpu.SemaphoreType.DMA((2,))],
        compiler_params=pltpu.CompilerParams(vmem_limit_bytes=SMALL_VMEM),
        cost_estimate=pl.CostEstimate(flops=0, bytes_accessed=1 << 19, transcendentals=0),
        name="pack",
    )(in_hbm(keys), in_hbm(values))


def row_start(first_ref):
    return (first_ref[0] // ROW_SEGS) * ROW_SEGS


def slot_of(seg):
    place = seg // 2
    member = 2 * (ROW // 2 - 1 - place % (ROW // 2)) + 1 - place // (ROW // 2)
    return 2 * member + seg % 2


def bring_parents(source_ref, parents_ref, sem):
    copy = pltpu.make_async_copy(source_ref, parents_ref, sem)
    copy.start()
    copy.wait()


def carry_kernel(first_ref, source_ref, pieces_ref, next_ref, second_ref, parents_ref, sem):
    bring_parents(source_ref, parents_ref, sem)
    base = row_start(first_ref)
    last = parents_ref.shape[0] - 1

    def held(path, depth, level):
        return pieces_ref[slot_of(jnp.clip(level_of(path, depth, level) - base, 0, ROW_SEGS - 1))]

    path, depth = path_of(parents_ref, jnp.minimum(base + ROW_SEGS, last))
    for level in range(LEVELS):
        next_ref[level] = held(path, depth, level)
    path, depth = path_of(parents_ref, jnp.minimum(base + 2 * ROW_SEGS, last))
    second_ref[0] = held(path, depth, 0)


def carry_out(first, parents, pieces):
    shape = lambda n: jax.ShapeDtypeStruct((n,) + pieces.shape[1:], pieces.dtype)
    return pl.pallas_call(
        carry_kernel,
        out_shape=(shape(LEVELS), shape(1)),
        in_specs=[SMEM, HBM, VMEM],
        out_specs=(VMEM, VMEM),
        scratch_shapes=[pltpu.SMEM(parents.shape, parents.dtype), pltpu.SemaphoreType.DMA],
        compiler_params=pltpu.CompilerParams(vmem_limit_bytes=SMALL_VMEM),
        cost_estimate=pl.CostEstimate(flops=0, bytes_accessed=1 << 18, transcendentals=0),
        name="carry_out",
    )(first, in_hbm(parents), pieces)


def pick_kernel(
    first_ref, source_ref, pieces_ref, inside_ref, next_ref, second_ref, parents_ref, sem
):
    bring_parents(source_ref, parents_ref, sem)
    base = row_start(first_ref)
    ones = lambda on: jnp.full((FLAG_ROWS, HEAD_DIM), on, jnp.float32).astype(jnp.bfloat16)
    for target, place in enumerate(LISTED):
        path, depth = path_of(parents_ref, base + 2 * place)
        for level in range(LEVELS):
            seg = level_of(path, depth, level)
            within = seg >= base
            piece = pieces_ref[slot_of(jnp.maximum(seg - base, 0))]
            inside_ref[target, level] = jnp.where(within, piece, jnp.zeros_like(piece))
            before = jnp.logical_and(seg < base, seg >= base - ROW_SEGS)
            next_ref[target, level] = ones(jnp.where(before, 1.0, 0.0))
            if level == 0:
                second_ref[target] = ones(jnp.where(seg < base - ROW_SEGS, 1.0, 0.0))


def pick(first, parents, pieces):
    shape = lambda *dims: jax.ShapeDtypeStruct(dims, pieces.dtype)
    return pl.pallas_call(
        pick_kernel,
        out_shape=(
            shape(ROW, LEVELS, *pieces.shape[1:]),
            shape(ROW, LEVELS, FLAG_ROWS, HEAD_DIM),
            shape(ROW, FLAG_ROWS, HEAD_DIM),
        ),
        in_specs=[SMEM, HBM, VMEM],
        out_specs=(VMEM, VMEM, VMEM),
        scratch_shapes=[pltpu.SMEM(parents.shape, parents.dtype), pltpu.SemaphoreType.DMA],
        compiler_params=pltpu.CompilerParams(vmem_limit_bytes=SMALL_VMEM),
        cost_estimate=pl.CostEstimate(flops=0, bytes_accessed=1 << 20, transcendentals=0),
        name="pick",
    )(first, in_hbm(parents), pieces)


def merge_kernel(inside_ref, on_next_ref, on_second_ref, next_ref, second_ref, picked_ref):
    for level in range(LEVELS):
        for at in range(0, 2 * PIECE, FLAG_ROWS):
            rows = pl.ds(at, FLAG_ROWS)
            carried = next_ref[level, rows]
            older = second_ref[0, rows]
            for target in range(ROW):
                total = inside_ref[target, level, rows] + carried * on_next_ref[target, level]
                if level == 0:
                    total = total + older * on_second_ref[target]
                picked_ref[target, level, rows] = total


def merge(inside, on_next, on_second, carried, second):
    return pl.pallas_call(
        merge_kernel,
        out_shape=jax.ShapeDtypeStruct(inside.shape, inside.dtype),
        in_specs=[VMEM] * 5,
        out_specs=VMEM,
        compiler_params=pltpu.CompilerParams(vmem_limit_bytes=SMALL_VMEM),
        cost_estimate=pl.CostEstimate(flops=0, bytes_accessed=1 << 20, transcendentals=0),
        name="merge",
    )(inside, on_next, on_second, carried, second)


def attend_kernel(first_head, blocks, first_ref, *refs):
    sources, (far_ref, *refs) = refs[:4], refs[4:]
    if blocks:
        me_ref, weight_ref = refs[:2]
        weight_sem = refs.pop()
        held_ref = refs.pop(-8)
    out_ref, path_key_ref, path_value_ref, parents_ref, query_ref, key_ref, value_ref, sem = refs[-8:]
    heads = query_ref.shape[1] // HEAD_DIM
    columns = pl.ds(first_head * HEAD_DIM, query_ref.shape[1])
    views = [sources[0], sources[1].at[:, columns], sources[2], sources[3]]
    fetches = [
        pltpu.make_async_copy(view, target, sem.at[i])
        for i, (view, target) in enumerate(zip(views, [parents_ref, query_ref, key_ref, value_ref]))
    ]
    copies = weight_copies(blocks, me_ref, weight_ref, held_ref, weight_sem) if blocks else []
    for copy in fetches + copies:
        copy.start()

    def scores_of(query, keys):
        return lax.dot_general(
            query, keys, (((1,), (1,)), ((), ())), preferred_element_type=jnp.float32
        )

    def with_ones(values):
        return jnp.concatenate([values, jnp.ones_like(values)], axis=1)

    for piece in range(ROW):
        for level in range(LEVELS):
            rows = pl.ds(piece * STACK + level * PIECE, PIECE)
            path_key_ref[rows, :HEAD_DIM] = far_ref[piece, level, :PIECE]
            path_value_ref[rows, :HEAD_DIM] = far_ref[piece, level, PIECE:]
    path_value_ref[:, HEAD_DIM:] = jnp.ones((PATH, HEAD_DIM), jnp.bfloat16)
    for copy in fetches:
        copy.wait()
    first = first_ref[0]
    _, depth0 = path_of(parents_ref, first)
    _, depth1 = path_of(parents_ref, first + 1)
    follows = jnp.where(parents_ref[first + 1] == first, 0.0, MASKED)
    row = lax.broadcasted_iota(jnp.int32, (PATH, HEAD_DIM), 0)
    lane = lax.broadcasted_iota(jnp.int32, (PATH, HEAD_DIM), 1)
    level = lax.rem(row // PIECE, LEVELS)
    limit = jnp.where(lane == 0, depth0, jnp.where(lane == 1, jnp.minimum(depth0, depth1), LEVELS))
    path_key_ref[:, HEAD_DIM:] = jnp.where(level < limit, 0.0, MASKED).astype(jnp.bfloat16)
    path_keys, path_values = path_key_ref[...], path_value_ref[...]

    rows = lax.broadcasted_iota(jnp.int32, (2 * SEG_LEN, HEAD_DIM), 0)
    lanes = lax.broadcasted_iota(jnp.int32, (2 * SEG_LEN, HEAD_DIM), 1)
    marks = (lanes == rows // SEG_LEN).astype(jnp.float32).astype(jnp.bfloat16)
    causal = lax.broadcasted_iota(jnp.int32, (SEG_LEN, SEG_LEN), 1) <= lax.broadcasted_iota(
        jnp.int32, (SEG_LEN, SEG_LEN), 0
    )
    halves = [slice(0, SEG_LEN), slice(SEG_LEN, 2 * SEG_LEN)]
    own_values = [with_ones(value_ref[half]) for half in halves]
    for head in range(heads):
        query = query_ref[:, head * HEAD_DIM : (head + 1) * HEAD_DIM]
        path_scores = scores_of(jnp.concatenate([query, marks], axis=1), path_keys)
        own = [
            [(jnp.where(causal, scores_of(query[half], key_ref[half]), MASKED), values)]
            for half, values in zip(halves, own_values)
        ]
        own[1].append((scores_of(query[halves[1]], key_ref[halves[0]]) + follows, own_values[0]))
        path_weights, own_parts = [], []
        for half, blocks in zip(halves, own):
            row_max = functools.reduce(
                jnp.maximum,
                [jnp.max(s, axis=1, keepdims=True) for s, _ in blocks]
                + [jnp.max(path_scores[half], axis=1, keepdims=True)],
            )
            weigh = lambda s: jnp.exp2((s - row_max) * EXP2_SCALE).astype(jnp.bfloat16)
            path_weights.append(weigh(path_scores[half]))
            own_parts.append(
                sum(
                    jnp.dot(weigh(s), values, preferred_element_type=jnp.float32)
                    for s, values in blocks
                )
            )
        total = jnp.dot(
            jnp.concatenate(path_weights, axis=0), path_values, preferred_element_type=jnp.float32
        ) + jnp.concatenate(own_parts, axis=0)
        mixture = total[:, :HEAD_DIM] / total[:, HEAD_DIM:]
        out_ref[:, head * HEAD_DIM : (head + 1) * HEAD_DIM] = mixture.astype(out_ref.dtype)
    for copy in copies:
        copy.wait()


def weight_copies(blocks, me_ref, weight_ref, held_ref, sem):
    block = weight_ref.shape[0] // 4
    copies = []
    for i, bit in enumerate(blocks):
        rows = pl.ds(pl.multiple_of((me_ref[0] ^ bit) * block, block), block)
        copies.append(
            pltpu.make_async_copy(
                weight_ref.at[rows], held_ref.at[pl.ds(i * block, block)], sem.at[i]
            )
        )
    return copies


def attend(first, parents, queries, keys, values, far, first_head, heads, blocks, bring, after):
    rows = queries.shape[0]
    pairs = heads * rows * (PATH + SEG_LEN + SEG_LEN // 2)
    out_shape = [jax.ShapeDtypeStruct((rows, heads * HEAD_DIM), jnp.bfloat16)]
    in_specs = [SMEM] + [HBM] * 4 + [VMEM]
    scratch = [pltpu.VMEM((PATH, 2 * HEAD_DIM), jnp.bfloat16)] * 2 + [
        pltpu.SMEM(parents.shape, parents.dtype),
        pltpu.VMEM((rows, heads * HEAD_DIM), queries.dtype),
        pltpu.VMEM(keys.shape, keys.dtype),
        pltpu.VMEM(values.shape, values.dtype),
        pltpu.SemaphoreType.DMA((4,)),
    ]
    if blocks:
        me, weight = bring
        bring = [me, in_hbm(weight)]
        in_specs += [SMEM, HBM]
        shape = (len(blocks) * weight.shape[0] // 4, weight.shape[1])
        out_shape.append(pltpu.VMEM(shape, weight.dtype))
        scratch.append(pltpu.SemaphoreType.DMA((len(blocks),)))
    else:
        bring = []
    return pl.pallas_call(
        functools.partial(attend_kernel, first_head, blocks),
        out_shape=out_shape,
        in_specs=in_specs + [ANY] * len(after),
        out_specs=[VMEM] * len(out_shape),
        scratch_shapes=scratch,
        compiler_params=pltpu.CompilerParams(vmem_limit_bytes=ATTEND_VMEM),
        cost_estimate=pl.CostEstimate(
            flops=pairs * HEAD_DIM * 10,
            bytes_accessed=heads * rows * HEAD_DIM * 4 + 8 * PATH * HEAD_DIM,
            transcendentals=pairs,
        ),
        name="attend",
    )(
        first,
        in_hbm(parents),
        in_hbm(queries),
        in_hbm(keys),
        in_hbm(values),
        far,
        *bring,
        *after,
    )


def project_kernel(counts, spans, has_base, near_ref, far_ref, *refs):
    parts = refs[: sum(counts)]
    out_ref, held_ref = refs[-2:]
    at, ends = 0, [0]
    for count in counts:
        for part in parts[:count]:
            held_ref[:, at : at + part.shape[1]] = part[...]
            at += part.shape[1]
        parts = parts[count:]
        ends.append(at)
    for column in range(0, out_ref.shape[1], TILE):
        columns = slice(column, column + TILE)
        total = refs[sum(counts)][:, columns] if has_base else None
        for (half, start), begin, end in zip(spans, ends, ends[1:]):
            product = jnp.dot(
                held_ref[:, begin:end],
                (near_ref, far_ref)[half][start : start + end - begin, columns],
                preferred_element_type=jnp.float32,
            )
            total = product if total is None else total + product
        out_ref[:, columns] = total.astype(out_ref.dtype)


def project(groups, spans, weights, base, dtype):
    parts = [part for group in groups for part in group]
    rows = parts[0].shape[0]
    depth = sum(part.shape[1] for part in parts)
    width = weights[0].shape[1]
    bases = [] if base is None else [base]
    return pl.pallas_call(
        functools.partial(project_kernel, [len(g) for g in groups], spans, base is not None),
        out_shape=jax.ShapeDtypeStruct((rows, width), dtype),
        in_specs=[VMEM] * (2 + len(parts) + len(bases)),
        out_specs=VMEM,
        scratch_shapes=[pltpu.VMEM((rows, depth), parts[0].dtype)],
        compiler_params=pltpu.CompilerParams(vmem_limit_bytes=PROJECT_VMEM),
        cost_estimate=pl.CostEstimate(
            flops=rows * width,
            bytes_accessed=rows * width,
            transcendentals=0,
        ),
        name="project",
    )(*[in_vmem(weight) for weight in weights], *parts, *bases)


def swap(part, bit):
    size = lax.axis_size("tensor")
    return lax.ppermute(part, "tensor", [(i, i ^ bit) for i in range(size)])


def trade(pieces):
    devices = lax.axis_size("dp")
    rows = [[at + place for place in LISTED] for at in range(0, devices, ROW)]
    return lax.all_to_all(pieces, "dp", 0, 0, tiled=True, axis_index_groups=rows)


def onward(piece, step):
    devices = lax.axis_size("dp")
    return lax.ppermute(piece, "dp", [(i, (i + step) % devices) for i in range(devices)])


def per_device(queries, key_proj, value_proj, out_weight, parents):
    me = lax.axis_index("tensor")
    first = (lax.axis_index("dp") * 2).astype(jnp.int32).reshape(1)
    pieces = trade(pack(key_proj, value_proj)).reshape(ROW_SEGS, 2 * PIECE, HEAD_DIM)
    to_next, to_second = carry_out(first, parents, pieces)
    inside = pick(first, parents, pieces)
    far = trade(merge(*inside, onward(to_next, ROW), onward(to_second, 2 * ROW)))

    width = queries.shape[1]
    bring = (me.astype(jnp.int32).reshape(1), out_weight)
    own, across, weights, head = [], [], [], 0
    for c, (size, blocks) in enumerate([(3, ()), (3, (0, 1)), (2, (2, 3))]):
        after = [across[c - 2]] if c >= 2 else []
        part, *brought = attend(
            first, parents, queries, key_proj, value_proj, far, head, size, blocks, bring, after
        )
        weights += brought
        own.append(part)
        across.append(swap(part, 2))
        head += size
    beside = [swap(part, 1) for part in own]
    corner = [swap(part, 1) for part in across[:-1]]
    near = project(
        [own + beside, across[:-1], corner[:-1]], [(0, 0), (1, 0), (1, width)], weights, None, jnp.float32
    )
    last, near = lax.optimization_barrier((across[-1], near))
    corner.append(swap(last, 1))
    done = width - last.shape[1]
    turned = sum(part.shape[1] for part in corner[:-2])
    return project(
        [[last], corner[-2:]], [(1, done), (1, width + turned)], weights, near, jnp.bfloat16
    )


def solution(mesh):
    placed = (P("dp", "tensor"), P("dp", "tensor"), P("dp", "tensor"), P(None, "tensor"), P())
    return jax.shard_map(
        per_device, mesh=mesh, in_specs=placed, out_specs=P("dp", "tensor"), check_vma=False
    )
```

```python
import functools
import math

import jax
import jax.numpy as jnp
from jax import lax
from jax.experimental import pallas as pl
from jax.experimental.pallas import tpu as pltpu
from jax.sharding import PartitionSpec as P

HEAD_DIM = 128
SEG_LEN = 256
LEVELS = 4
ROW = 8
ROW_SEGS = 2 * ROW
LISTED = (7, 3, 6, 2, 5, 1, 4, 0)
PIECE = SEG_LEN // ROW
PATH = LEVELS * SEG_LEN
STACK = LEVELS * PIECE
MASKED = -1e30
EXP2_SCALE = math.log2(math.e) * HEAD_DIM ** (-0.5)
SMALL_VMEM = 6 * 1024 * 1024
ATTEND_VMEM = 18 * 1024 * 1024
PROJECT_VMEM = 14 * 1024 * 1024
TILE = 256

VMEM = pl.BlockSpec(memory_space=pltpu.VMEM)
SMEM = pl.BlockSpec(memory_space=pltpu.SMEM)
ANY = pl.BlockSpec(memory_space=pl.ANY)
HBM = pl.BlockSpec(memory_space=pltpu.HBM)
FLAG_ROWS = 16


def in_hbm(array):
    return pltpu.with_memory_space_constraint(array, pltpu.HBM)


def in_vmem(array):
    return pltpu.with_memory_space_constraint(array, pltpu.VMEM)


def path_of(parents_ref, seg):
    path = [parents_ref[seg]]
    for _ in range(LEVELS - 1):
        up = parents_ref[jnp.maximum(path[-1], 0)]
        path.append(jnp.where(path[-1] >= 0, up, -1))
    depth = sum((p >= 0).astype(jnp.int32) for p in path)
    return path, depth


def level_of(path, depth, level):
    found = jnp.int32(0)
    for up in range(LEVELS):
        found = jnp.where(depth - 1 - up == level, path[up], found)
    return found


def pack_kernel(key_ref, value_ref, piece_ref, held_ref, sem):
    copies = [
        pltpu.make_async_copy(source, held_ref.at[i], sem.at[i])
        for i, source in enumerate([key_ref, value_ref])
    ]
    for copy in copies:
        copy.start()
    for i, copy in enumerate(copies):
        copy.wait()
        for piece in range(ROW):
            for seg in range(2):
                rows = pl.ds(seg * SEG_LEN + piece * PIECE, PIECE)
                piece_ref[piece, seg, i * PIECE : (i + 1) * PIECE] = held_ref[i, rows]


def pack(keys, values):
    return pl.pallas_call(
        pack_kernel,
        out_shape=jax.ShapeDtypeStruct((ROW, 2, 2 * PIECE, HEAD_DIM), keys.dtype),
        in_specs=[HBM, HBM],
        out_specs=VMEM,
        scratch_shapes=[pltpu.VMEM((2,) + keys.shape, keys.dtype), pltpu.SemaphoreType.DMA((2,))],
        compiler_params=pltpu.CompilerParams(vmem_limit_bytes=SMALL_VMEM),
        cost_estimate=pl.CostEstimate(flops=0, bytes_accessed=1 << 19, transcendentals=0),
        name="pack",
    )(in_hbm(keys), in_hbm(values))


def row_start(first_ref):
    return (first_ref[0] // ROW_SEGS) * ROW_SEGS


def slot_of(seg):
    place = seg // 2
    member = 2 * (ROW // 2 - 1 - place % (ROW // 2)) + 1 - place // (ROW // 2)
    return 2 * member + seg % 2


def bring_parents(source_ref, parents_ref, sem):
    copy = pltpu.make_async_copy(source_ref, parents_ref, sem)
    copy.start()
    copy.wait()


def carry_kernel(first_ref, source_ref, pieces_ref, next_ref, second_ref, parents_ref, sem):
    bring_parents(source_ref, parents_ref, sem)
    base = row_start(first_ref)
    last = parents_ref.shape[0] - 1

    def held(path, depth, level):
        return pieces_ref[slot_of(jnp.clip(level_of(path, depth, level) - base, 0, ROW_SEGS - 1))]

    path, depth = path_of(parents_ref, jnp.minimum(base + ROW_SEGS, last))
    for level in range(LEVELS):
        next_ref[level] = held(path, depth, level)
    path, depth = path_of(parents_ref, jnp.minimum(base + 2 * ROW_SEGS, last))
    second_ref[0] = held(path, depth, 0)


def carry_out(first, parents, pieces):
    shape = lambda n: jax.ShapeDtypeStruct((n,) + pieces.shape[1:], pieces.dtype)
    return pl.pallas_call(
        carry_kernel,
        out_shape=(shape(LEVELS), shape(1)),
        in_specs=[SMEM, HBM, VMEM],
        out_specs=(VMEM, VMEM),
        scratch_shapes=[pltpu.SMEM(parents.shape, parents.dtype), pltpu.SemaphoreType.DMA],
        compiler_params=pltpu.CompilerParams(vmem_limit_bytes=SMALL_VMEM),
        cost_estimate=pl.CostEstimate(flops=0, bytes_accessed=1 << 18, transcendentals=0),
        name="carry_out",
    )(first, in_hbm(parents), pieces)


def pick_kernel(
    first_ref, source_ref, pieces_ref, inside_ref, next_ref, second_ref, parents_ref, sem
):
    bring_parents(source_ref, parents_ref, sem)
    base = row_start(first_ref)
    ones = lambda on: jnp.full((FLAG_ROWS, HEAD_DIM), on, jnp.float32).astype(jnp.bfloat16)
    for target, place in enumerate(LISTED):
        path, depth = path_of(parents_ref, base + 2 * place)
        for level in range(LEVELS):
            seg = level_of(path, depth, level)
            within = seg >= base
            piece = pieces_ref[slot_of(jnp.maximum(seg - base, 0))]
            inside_ref[target, level] = jnp.where(within, piece, jnp.zeros_like(piece))
            before = jnp.logical_and(seg < base, seg >= base - ROW_SEGS)
            next_ref[target, level] = ones(jnp.where(before, 1.0, 0.0))
            if level == 0:
                second_ref[target] = ones(jnp.where(seg < base - ROW_SEGS, 1.0, 0.0))


def pick(first, parents, pieces):
    shape = lambda *dims: jax.ShapeDtypeStruct(dims, pieces.dtype)
    return pl.pallas_call(
        pick_kernel,
        out_shape=(
            shape(ROW, LEVELS, *pieces.shape[1:]),
            shape(ROW, LEVELS, FLAG_ROWS, HEAD_DIM),
            shape(ROW, FLAG_ROWS, HEAD_DIM),
        ),
        in_specs=[SMEM, HBM, VMEM],
        out_specs=(VMEM, VMEM, VMEM),
        scratch_shapes=[pltpu.SMEM(parents.shape, parents.dtype), pltpu.SemaphoreType.DMA],
        compiler_params=pltpu.CompilerParams(vmem_limit_bytes=SMALL_VMEM),
        cost_estimate=pl.CostEstimate(flops=0, bytes_accessed=1 << 20, transcendentals=0),
        name="pick",
    )(first, in_hbm(parents), pieces)


def merge_kernel(inside_ref, on_next_ref, on_second_ref, next_ref, second_ref, picked_ref):
    for level in range(LEVELS):
        for at in range(0, 2 * PIECE, FLAG_ROWS):
            rows = pl.ds(at, FLAG_ROWS)
            carried = next_ref[level, rows]
            older = second_ref[0, rows]
            for target in range(ROW):
                total = inside_ref[target, level, rows] + carried * on_next_ref[target, level]
                if level == 0:
                    total = total + older * on_second_ref[target]
                picked_ref[target, level, rows] = total


def merge(inside, on_next, on_second, carried, second):
    return pl.pallas_call(
        merge_kernel,
        out_shape=jax.ShapeDtypeStruct(inside.shape, inside.dtype),
        in_specs=[VMEM] * 5,
        out_specs=VMEM,
        compiler_params=pltpu.CompilerParams(vmem_limit_bytes=SMALL_VMEM),
        cost_estimate=pl.CostEstimate(flops=0, bytes_accessed=1 << 20, transcendentals=0),
        name="merge",
    )(inside, on_next, on_second, carried, second)


def attend_kernel(first_head, blocks, first_ref, *refs):
    sources, (far_ref, *refs) = refs[:4], refs[4:]
    if blocks:
        me_ref, weight_ref = refs[:2]
        weight_sem = refs.pop()
        held_ref = refs.pop(-8)
    out_ref, path_key_ref, path_value_ref, parents_ref, query_ref, key_ref, value_ref, sem = refs[-8:]
    heads = query_ref.shape[1] // HEAD_DIM
    columns = pl.ds(first_head * HEAD_DIM, query_ref.shape[1])
    views = [sources[0], sources[1].at[:, columns], sources[2], sources[3]]
    fetches = [
        pltpu.make_async_copy(view, target, sem.at[i])
        for i, (view, target) in enumerate(zip(views, [parents_ref, query_ref, key_ref, value_ref]))
    ]
    copies = weight_copies(blocks, me_ref, weight_ref, held_ref, weight_sem) if blocks else []
    for copy in fetches + copies:
        copy.start()

    def scores_of(query, keys):
        return lax.dot_general(
            query, keys, (((1,), (1,)), ((), ())), preferred_element_type=jnp.float32
        )

    def with_ones(values):
        return jnp.concatenate([values, jnp.ones_like(values)], axis=1)

    for piece in range(ROW):
        for level in range(LEVELS):
            rows = pl.ds(piece * STACK + level * PIECE, PIECE)
            path_key_ref[rows, :HEAD_DIM] = far_ref[piece, level, :PIECE]
            path_value_ref[rows, :HEAD_DIM] = far_ref[piece, level, PIECE:]
    path_value_ref[:, HEAD_DIM:] = jnp.ones((PATH, HEAD_DIM), jnp.bfloat16)
    for copy in fetches:
        copy.wait()
    first = first_ref[0]
    _, depth0 = path_of(parents_ref, first)
    _, depth1 = path_of(parents_ref, first + 1)
    follows = jnp.where(parents_ref[first + 1] == first, 0.0, MASKED)
    row = lax.broadcasted_iota(jnp.int32, (PATH, HEAD_DIM), 0)
    lane = lax.broadcasted_iota(jnp.int32, (PATH, HEAD_DIM), 1)
    level = lax.rem(row // PIECE, LEVELS)
    limit = jnp.where(lane == 0, depth0, jnp.where(lane == 1, jnp.minimum(depth0, depth1), LEVELS))
    path_key_ref[:, HEAD_DIM:] = jnp.where(level < limit, 0.0, MASKED).astype(jnp.bfloat16)
    path_keys, path_values = path_key_ref[...], path_value_ref[...]

    rows = lax.broadcasted_iota(jnp.int32, (2 * SEG_LEN, HEAD_DIM), 0)
    lanes = lax.broadcasted_iota(jnp.int32, (2 * SEG_LEN, HEAD_DIM), 1)
    marks = (lanes == rows // SEG_LEN).astype(jnp.float32).astype(jnp.bfloat16)
    causal = lax.broadcasted_iota(jnp.int32, (SEG_LEN, SEG_LEN), 1) <= lax.broadcasted_iota(
        jnp.int32, (SEG_LEN, SEG_LEN), 0
    )
    halves = [slice(0, SEG_LEN), slice(SEG_LEN, 2 * SEG_LEN)]
    own_values = [with_ones(value_ref[half]) for half in halves]
    for head in range(heads):
        query = query_ref[:, head * HEAD_DIM : (head + 1) * HEAD_DIM]
        path_scores = scores_of(jnp.concatenate([query, marks], axis=1), path_keys)
        own = [
            [(jnp.where(causal, scores_of(query[half], key_ref[half]), MASKED), values)]
            for half, values in zip(halves, own_values)
        ]
        own[1].append((scores_of(query[halves[1]], key_ref[halves[0]]) + follows, own_values[0]))
        path_weights, own_parts = [], []
        for half, blocks in zip(halves, own):
            row_max = functools.reduce(
                jnp.maximum,
                [jnp.max(s, axis=1, keepdims=True) for s, _ in blocks]
                + [jnp.max(path_scores[half], axis=1, keepdims=True)],
            )
            weigh = lambda s: jnp.exp2((s - row_max) * EXP2_SCALE).astype(jnp.bfloat16)
            path_weights.append(weigh(path_scores[half]))
            own_parts.append(
                sum(
                    jnp.dot(weigh(s), values, preferred_element_type=jnp.float32)
                    for s, values in blocks
                )
            )
        total = jnp.dot(
            jnp.concatenate(path_weights, axis=0), path_values, preferred_element_type=jnp.float32
        ) + jnp.concatenate(own_parts, axis=0)
        mixture = total[:, :HEAD_DIM] / total[:, HEAD_DIM:]
        out_ref[:, head * HEAD_DIM : (head + 1) * HEAD_DIM] = mixture.astype(out_ref.dtype)
    for copy in copies:
        copy.wait()


def weight_copies(blocks, me_ref, weight_ref, held_ref, sem):
    block = weight_ref.shape[0] // 4
    copies = []
    for i, bit in enumerate(blocks):
        rows = pl.ds(pl.multiple_of((me_ref[0] ^ bit) * block, block), block)
        copies.append(
            pltpu.make_async_copy(
                weight_ref.at[rows], held_ref.at[pl.ds(i * block, block)], sem.at[i]
            )
        )
    return copies


def attend(first, parents, queries, keys, values, far, first_head, heads, blocks, bring, after):
    rows = queries.shape[0]
    pairs = heads * rows * (PATH + SEG_LEN + SEG_LEN // 2)
    out_shape = [jax.ShapeDtypeStruct((rows, heads * HEAD_DIM), jnp.bfloat16)]
    in_specs = [SMEM] + [HBM] * 4 + [VMEM]
    scratch = [pltpu.VMEM((PATH, 2 * HEAD_DIM), jnp.bfloat16)] * 2 + [
        pltpu.SMEM(parents.shape, parents.dtype),
        pltpu.VMEM((rows, heads * HEAD_DIM), queries.dtype),
        pltpu.VMEM(keys.shape, keys.dtype),
        pltpu.VMEM(values.shape, values.dtype),
        pltpu.SemaphoreType.DMA((4,)),
    ]
    if blocks:
        me, weight = bring
        bring = [me, in_hbm(weight)]
        in_specs += [SMEM, HBM]
        shape = (len(blocks) * weight.shape[0] // 4, weight.shape[1])
        out_shape.append(pltpu.VMEM(shape, weight.dtype))
        scratch.append(pltpu.SemaphoreType.DMA((len(blocks),)))
    else:
        bring = []
    return pl.pallas_call(
        functools.partial(attend_kernel, first_head, blocks),
        out_shape=out_shape,
        in_specs=in_specs + [ANY] * len(after),
        out_specs=[VMEM] * len(out_shape),
        scratch_shapes=scratch,
        compiler_params=pltpu.CompilerParams(vmem_limit_bytes=ATTEND_VMEM),
        cost_estimate=pl.CostEstimate(
            flops=pairs * HEAD_DIM * 10,
            bytes_accessed=heads * rows * HEAD_DIM * 4 + 8 * PATH * HEAD_DIM,
            transcendentals=pairs,
        ),
        name="attend",
    )(
        first,
        in_hbm(parents),
        in_hbm(queries),
        in_hbm(keys),
        in_hbm(values),
        far,
        *bring,
        *after,
    )


def project_kernel(counts, spans, has_base, near_ref, far_ref, *refs):
    parts = refs[: sum(counts)]
    out_ref, held_ref = refs[-2:]
    at, ends = 0, [0]
    for count in counts:
        for part in parts[:count]:
            held_ref[:, at : at + part.shape[1]] = part[...]
            at += part.shape[1]
        parts = parts[count:]
        ends.append(at)
    for column in range(0, out_ref.shape[1], TILE):
        columns = slice(column, column + TILE)
        total = refs[sum(counts)][:, columns] if has_base else None
        for (half, start), begin, end in zip(spans, ends, ends[1:]):
            product = jnp.dot(
                held_ref[:, begin:end],
                (near_ref, far_ref)[half][start : start + end - begin, columns],
                preferred_element_type=jnp.float32,
            )
            total = product if total is None else total + product
        out_ref[:, columns] = total.astype(out_ref.dtype)


def project(groups, spans, weights, base, dtype):
    parts = [part for group in groups for part in group]
    rows = parts[0].shape[0]
    depth = sum(part.shape[1] for part in parts)
    width = weights[0].shape[1]
    bases = [] if base is None else [base]
    return pl.pallas_call(
        functools.partial(project_kernel, [len(g) for g in groups], spans, base is not None),
        out_shape=jax.ShapeDtypeStruct((rows, width), dtype),
        in_specs=[VMEM] * (2 + len(parts) + len(bases)),
        out_specs=VMEM,
        scratch_shapes=[pltpu.VMEM((rows, depth), parts[0].dtype)],
        compiler_params=pltpu.CompilerParams(vmem_limit_bytes=PROJECT_VMEM),
        cost_estimate=pl.CostEstimate(
            flops=rows * width,
            bytes_accessed=rows * width,
            transcendentals=0,
        ),
        name="project",
    )(*[in_vmem(weight) for weight in weights], *parts, *bases)


def swap(part, bit):
    size = lax.axis_size("tensor")
    return lax.ppermute(part, "tensor", [(i, i ^ bit) for i in range(size)])


def trade(pieces):
    devices = lax.axis_size("dp")
    rows = [[at + place for place in LISTED] for at in range(0, devices, ROW)]
    return lax.all_to_all(pieces, "dp", 0, 0, tiled=True, axis_index_groups=rows)


def onward(piece, step):
    devices = lax.axis_size("dp")
    return lax.ppermute(piece, "dp", [(i, (i + step) % devices) for i in range(devices)])


def per_device(queries, key_proj, value_proj, out_weight, parents):
    me = lax.axis_index("tensor")
    first = (lax.axis_index("dp") * 2).astype(jnp.int32).reshape(1)
    pieces = trade(pack(key_proj, value_proj)).reshape(ROW_SEGS, 2 * PIECE, HEAD_DIM)
    to_next, to_second = carry_out(first, parents, pieces)
    inside = pick(first, parents, pieces)
    far = trade(merge(*inside, onward(to_next, ROW), onward(to_second, 2 * ROW)))

    width = queries.shape[1]
    bring = (me.astype(jnp.int32).reshape(1), out_weight)
    own, across, weights, head = [], [], [], 0
    for c, (size, blocks) in enumerate([(3, ()), (3, (0, 1)), (2, (2, 3))]):
        after = [across[c - 2]] if c >= 2 else []
        part, *brought = attend(
            first, parents, queries, key_proj, value_proj, far, head, size, blocks, bring, after
        )
        weights += brought
        own.append(part)
        across.append(swap(part, 2))
        head += size
    beside = [swap(part, 1) for part in own]
    corner = [swap(across[0], 1)]
    near = project(
        [own + beside, across[:1], corner], [(0, 0), (1, 0), (1, width)], weights, None, jnp.float32
    )
    across[1], near = lax.optimization_barrier((across[1], near))
    corner.append(swap(across[1], 1))
    across[2], near = lax.optimization_barrier((across[2], near))
    corner.append(swap(across[2], 1))
    done = across[0].shape[1]
    return project(
        [across[1:], corner[1:]], [(1, done), (1, width + done)], weights, near, jnp.bfloat16
    )


def solution(mesh):
    placed = (P("dp", "tensor"), P("dp", "tensor"), P("dp", "tensor"), P(None, "tensor"), P())
    return jax.shard_map(
        per_device, mesh=mesh, in_specs=placed, out_specs=P("dp", "tensor"), check_vma=False
    )
```

```python
import functools
import math

import jax
import jax.numpy as jnp
from jax import lax
from jax.experimental import pallas as pl
from jax.experimental.pallas import tpu as pltpu
from jax.sharding import PartitionSpec as P

HEAD_DIM = 128
SEG_LEN = 256
LEVELS = 4
ROW = 8
ROW_SEGS = 2 * ROW
LISTED = (7, 3, 6, 2, 5, 1, 4, 0)
PIECE = SEG_LEN // ROW
PATH = LEVELS * SEG_LEN
STACK = LEVELS * PIECE
MASKED = -1e30
EXP2_SCALE = math.log2(math.e) * HEAD_DIM ** (-0.5)
SMALL_VMEM = 6 * 1024 * 1024
ATTEND_VMEM = 18 * 1024 * 1024
PROJECT_VMEM = 14 * 1024 * 1024
TILE = 256

VMEM = pl.BlockSpec(memory_space=pltpu.VMEM)
SMEM = pl.BlockSpec(memory_space=pltpu.SMEM)
ANY = pl.BlockSpec(memory_space=pl.ANY)
HBM = pl.BlockSpec(memory_space=pltpu.HBM)
FLAG_ROWS = 16


def in_hbm(array):
    return pltpu.with_memory_space_constraint(array, pltpu.HBM)


def in_vmem(array):
    return pltpu.with_memory_space_constraint(array, pltpu.VMEM)


def path_of(parents_ref, seg):
    path = [parents_ref[seg]]
    for _ in range(LEVELS - 1):
        up = parents_ref[jnp.maximum(path[-1], 0)]
        path.append(jnp.where(path[-1] >= 0, up, -1))
    depth = sum((p >= 0).astype(jnp.int32) for p in path)
    return path, depth


def level_of(path, depth, level):
    found = jnp.int32(0)
    for up in range(LEVELS):
        found = jnp.where(depth - 1 - up == level, path[up], found)
    return found


def pack_kernel(key_ref, value_ref, piece_ref, held_ref, sem):
    copies = [
        pltpu.make_async_copy(source, held_ref.at[i], sem.at[i])
        for i, source in enumerate([key_ref, value_ref])
    ]
    for copy in copies:
        copy.start()
    for i, copy in enumerate(copies):
        copy.wait()
        for piece in range(ROW):
            for seg in range(2):
                rows = pl.ds(seg * SEG_LEN + piece * PIECE, PIECE)
                piece_ref[piece, seg, i * PIECE : (i + 1) * PIECE] = held_ref[i, rows]


def pack(keys, values):
    return pl.pallas_call(
        pack_kernel,
        out_shape=jax.ShapeDtypeStruct((ROW, 2, 2 * PIECE, HEAD_DIM), keys.dtype),
        in_specs=[HBM, HBM],
        out_specs=VMEM,
        scratch_shapes=[pltpu.VMEM((2,) + keys.shape, keys.dtype), pltpu.SemaphoreType.DMA((2,))],
        compiler_params=pltpu.CompilerParams(vmem_limit_bytes=SMALL_VMEM),
        cost_estimate=pl.CostEstimate(flops=0, bytes_accessed=1 << 19, transcendentals=0),
        name="pack",
    )(in_hbm(keys), in_hbm(values))


def row_start(first_ref):
    return (first_ref[0] // ROW_SEGS) * ROW_SEGS


def slot_of(seg):
    place = seg // 2
    member = 2 * (ROW // 2 - 1 - place % (ROW // 2)) + 1 - place // (ROW // 2)
    return 2 * member + seg % 2


def bring_parents(source_ref, parents_ref, sem):
    copy = pltpu.make_async_copy(source_ref, parents_ref, sem)
    copy.start()
    copy.wait()


def carry_kernel(first_ref, source_ref, pieces_ref, next_ref, second_ref, parents_ref, sem):
    bring_parents(source_ref, parents_ref, sem)
    base = row_start(first_ref)
    last = parents_ref.shape[0] - 1

    def held(path, depth, level):
        return pieces_ref[slot_of(jnp.clip(level_of(path, depth, level) - base, 0, ROW_SEGS - 1))]

    path, depth = path_of(parents_ref, jnp.minimum(base + ROW_SEGS, last))
    for level in range(LEVELS):
        next_ref[level] = held(path, depth, level)
    path, depth = path_of(parents_ref, jnp.minimum(base + 2 * ROW_SEGS, last))
    second_ref[0] = held(path, depth, 0)


def carry_out(first, parents, pieces):
    shape = lambda n: jax.ShapeDtypeStruct((n,) + pieces.shape[1:], pieces.dtype)
    return pl.pallas_call(
        carry_kernel,
        out_shape=(shape(LEVELS), shape(1)),
        in_specs=[SMEM, HBM, VMEM],
        out_specs=(VMEM, VMEM),
        scratch_shapes=[pltpu.SMEM(parents.shape, parents.dtype), pltpu.SemaphoreType.DMA],
        compiler_params=pltpu.CompilerParams(vmem_limit_bytes=SMALL_VMEM),
        cost_estimate=pl.CostEstimate(flops=0, bytes_accessed=1 << 18, transcendentals=0),
        name="carry_out",
    )(first, in_hbm(parents), pieces)


def pick_kernel(
    first_ref, source_ref, pieces_ref, inside_ref, next_ref, second_ref, parents_ref, sem
):
    bring_parents(source_ref, parents_ref, sem)
    base = row_start(first_ref)
    ones = lambda on: jnp.full((FLAG_ROWS, HEAD_DIM), on, jnp.float32).astype(jnp.bfloat16)
    for target, place in enumerate(LISTED):
        path, depth = path_of(parents_ref, base + 2 * place)
        for level in range(LEVELS):
            seg = level_of(path, depth, level)
            within = seg >= base
            piece = pieces_ref[slot_of(jnp.maximum(seg - base, 0))]
            inside_ref[target, level] = jnp.where(within, piece, jnp.zeros_like(piece))
            before = jnp.logical_and(seg < base, seg >= base - ROW_SEGS)
            next_ref[target, level] = ones(jnp.where(before, 1.0, 0.0))
            if level == 0:
                second_ref[target] = ones(jnp.where(seg < base - ROW_SEGS, 1.0, 0.0))


def pick(first, parents, pieces):
    shape = lambda *dims: jax.ShapeDtypeStruct(dims, pieces.dtype)
    return pl.pallas_call(
        pick_kernel,
        out_shape=(
            shape(ROW, LEVELS, *pieces.shape[1:]),
            shape(ROW, LEVELS, FLAG_ROWS, HEAD_DIM),
            shape(ROW, FLAG_ROWS, HEAD_DIM),
        ),
        in_specs=[SMEM, HBM, VMEM],
        out_specs=(VMEM, VMEM, VMEM),
        scratch_shapes=[pltpu.SMEM(parents.shape, parents.dtype), pltpu.SemaphoreType.DMA],
        compiler_params=pltpu.CompilerParams(vmem_limit_bytes=SMALL_VMEM),
        cost_estimate=pl.CostEstimate(flops=0, bytes_accessed=1 << 20, transcendentals=0),
        name="pick",
    )(first, in_hbm(parents), pieces)


def merge_kernel(inside_ref, on_next_ref, on_second_ref, next_ref, second_ref, picked_ref):
    for level in range(LEVELS):
        for at in range(0, 2 * PIECE, FLAG_ROWS):
            rows = pl.ds(at, FLAG_ROWS)
            carried = next_ref[level, rows]
            older = second_ref[0, rows]
            for target in range(ROW):
                total = inside_ref[target, level, rows] + carried * on_next_ref[target, level]
                if level == 0:
                    total = total + older * on_second_ref[target]
                picked_ref[target, level, rows] = total


def merge(inside, on_next, on_second, carried, second):
    return pl.pallas_call(
        merge_kernel,
        out_shape=jax.ShapeDtypeStruct(inside.shape, inside.dtype),
        in_specs=[VMEM] * 5,
        out_specs=VMEM,
        compiler_params=pltpu.CompilerParams(vmem_limit_bytes=SMALL_VMEM),
        cost_estimate=pl.CostEstimate(flops=0, bytes_accessed=1 << 20, transcendentals=0),
        name="merge",
    )(inside, on_next, on_second, carried, second)


def attend_kernel(first_head, blocks, first_ref, *refs):
    sources, (far_ref, *refs) = refs[:4], refs[4:]
    if blocks:
        me_ref, weight_ref = refs[:2]
        weight_sem = refs.pop()
        held_ref = refs.pop(-8)
    out_ref, path_key_ref, path_value_ref, parents_ref, query_ref, key_ref, value_ref, sem = refs[-8:]
    heads = query_ref.shape[1] // HEAD_DIM
    columns = pl.ds(first_head * HEAD_DIM, query_ref.shape[1])
    views = [sources[0], sources[1].at[:, columns], sources[2], sources[3]]
    fetches = [
        pltpu.make_async_copy(view, target, sem.at[i])
        for i, (view, target) in enumerate(zip(views, [parents_ref, query_ref, key_ref, value_ref]))
    ]
    copies = weight_copies(blocks, me_ref, weight_ref, held_ref, weight_sem) if blocks else []
    for copy in fetches + copies:
        copy.start()

    def scores_of(query, keys):
        return lax.dot_general(
            query, keys, (((1,), (1,)), ((), ())), preferred_element_type=jnp.float32
        )

    def with_ones(values):
        return jnp.concatenate([values, jnp.ones_like(values)], axis=1)

    for piece in range(ROW):
        for level in range(LEVELS):
            rows = pl.ds(piece * STACK + level * PIECE, PIECE)
            path_key_ref[rows, :HEAD_DIM] = far_ref[piece, level, :PIECE]
            path_value_ref[rows, :HEAD_DIM] = far_ref[piece, level, PIECE:]
    path_value_ref[:, HEAD_DIM:] = jnp.ones((PATH, HEAD_DIM), jnp.bfloat16)
    for copy in fetches:
        copy.wait()
    first = first_ref[0]
    _, depth0 = path_of(parents_ref, first)
    _, depth1 = path_of(parents_ref, first + 1)
    follows = jnp.where(parents_ref[first + 1] == first, 0.0, MASKED)
    row = lax.broadcasted_iota(jnp.int32, (PATH, HEAD_DIM), 0)
    lane = lax.broadcasted_iota(jnp.int32, (PATH, HEAD_DIM), 1)
    level = lax.rem(row // PIECE, LEVELS)
    limit = jnp.where(lane == 0, depth0, jnp.where(lane == 1, jnp.minimum(depth0, depth1), LEVELS))
    path_key_ref[:, HEAD_DIM:] = jnp.where(level < limit, 0.0, MASKED).astype(jnp.bfloat16)
    path_keys, path_values = path_key_ref[...], path_value_ref[...]

    rows = lax.broadcasted_iota(jnp.int32, (2 * SEG_LEN, HEAD_DIM), 0)
    lanes = lax.broadcasted_iota(jnp.int32, (2 * SEG_LEN, HEAD_DIM), 1)
    marks = (lanes == rows // SEG_LEN).astype(jnp.float32).astype(jnp.bfloat16)
    causal = lax.broadcasted_iota(jnp.int32, (SEG_LEN, SEG_LEN), 1) <= lax.broadcasted_iota(
        jnp.int32, (SEG_LEN, SEG_LEN), 0
    )
    halves = [slice(0, SEG_LEN), slice(SEG_LEN, 2 * SEG_LEN)]
    own_values = [with_ones(value_ref[half]) for half in halves]
    for head in range(heads):
        query = query_ref[:, head * HEAD_DIM : (head + 1) * HEAD_DIM]
        path_scores = scores_of(jnp.concatenate([query, marks], axis=1), path_keys)
        own = [
            [(jnp.where(causal, scores_of(query[half], key_ref[half]), MASKED), values)]
            for half, values in zip(halves, own_values)
        ]
        own[1].append((scores_of(query[halves[1]], key_ref[halves[0]]) + follows, own_values[0]))
        path_weights, own_parts = [], []
        for half, blocks in zip(halves, own):
            row_max = functools.reduce(
                jnp.maximum,
                [jnp.max(s, axis=1, keepdims=True) for s, _ in blocks]
                + [jnp.max(path_scores[half], axis=1, keepdims=True)],
            )
            weigh = lambda s: jnp.exp2((s - row_max) * EXP2_SCALE).astype(jnp.bfloat16)
            path_weights.append(weigh(path_scores[half]))
            own_parts.append(
                sum(
                    jnp.dot(weigh(s), values, preferred_element_type=jnp.float32)
                    for s, values in blocks
                )
            )
        total = jnp.dot(
            jnp.concatenate(path_weights, axis=0), path_values, preferred_element_type=jnp.float32
        ) + jnp.concatenate(own_parts, axis=0)
        mixture = total[:, :HEAD_DIM] / total[:, HEAD_DIM:]
        out_ref[:, head * HEAD_DIM : (head + 1) * HEAD_DIM] = mixture.astype(out_ref.dtype)
    for copy in copies:
        copy.wait()


def weight_copies(blocks, me_ref, weight_ref, held_ref, sem):
    block = weight_ref.shape[0] // 4
    copies = []
    for i, bit in enumerate(blocks):
        rows = pl.ds(pl.multiple_of((me_ref[0] ^ bit) * block, block), block)
        copies.append(
            pltpu.make_async_copy(
                weight_ref.at[rows], held_ref.at[pl.ds(i * block, block)], sem.at[i]
            )
        )
    return copies


def attend(first, parents, queries, keys, values, far, first_head, heads, blocks, bring, after):
    rows = queries.shape[0]
    pairs = heads * rows * (PATH + SEG_LEN + SEG_LEN // 2)
    out_shape = [jax.ShapeDtypeStruct((rows, heads * HEAD_DIM), jnp.bfloat16)]
    in_specs = [SMEM] + [HBM] * 4 + [VMEM]
    scratch = [pltpu.VMEM((PATH, 2 * HEAD_DIM), jnp.bfloat16)] * 2 + [
        pltpu.SMEM(parents.shape, parents.dtype),
        pltpu.VMEM((rows, heads * HEAD_DIM), queries.dtype),
        pltpu.VMEM(keys.shape, keys.dtype),
        pltpu.VMEM(values.shape, values.dtype),
        pltpu.SemaphoreType.DMA((4,)),
    ]
    if blocks:
        me, weight = bring
        bring = [me, in_hbm(weight)]
        in_specs += [SMEM, HBM]
        shape = (len(blocks) * weight.shape[0] // 4, weight.shape[1])
        out_shape.append(pltpu.VMEM(shape, weight.dtype))
        scratch.append(pltpu.SemaphoreType.DMA((len(blocks),)))
    else:
        bring = []
    return pl.pallas_call(
        functools.partial(attend_kernel, first_head, blocks),
        out_shape=out_shape,
        in_specs=in_specs + [ANY] * len(after),
        out_specs=[VMEM] * len(out_shape),
        scratch_shapes=scratch,
        compiler_params=pltpu.CompilerParams(vmem_limit_bytes=ATTEND_VMEM),
        cost_estimate=pl.CostEstimate(
            flops=pairs * HEAD_DIM * 10,
            bytes_accessed=heads * rows * HEAD_DIM * 4 + 8 * PATH * HEAD_DIM,
            transcendentals=pairs,
        ),
        name="attend",
    )(
        first,
        in_hbm(parents),
        in_hbm(queries),
        in_hbm(keys),
        in_hbm(values),
        far,
        *bring,
        *after,
    )


def project_kernel(counts, spans, has_base, near_ref, far_ref, *refs):
    parts = refs[: sum(counts)]
    out_ref, held_ref = refs[-2:]
    at, ends = 0, [0]
    for count in counts:
        for part in parts[:count]:
            held_ref[:, at : at + part.shape[1]] = part[...]
            at += part.shape[1]
        parts = parts[count:]
        ends.append(at)
    for column in range(0, out_ref.shape[1], TILE):
        columns = slice(column, column + TILE)
        total = refs[sum(counts)][:, columns] if has_base else None
        for (half, start), begin, end in zip(spans, ends, ends[1:]):
            product = jnp.dot(
                held_ref[:, begin:end],
                (near_ref, far_ref)[half][start : start + end - begin, columns],
                preferred_element_type=jnp.float32,
            )
            total = product if total is None else total + product
        out_ref[:, columns] = total.astype(out_ref.dtype)


def project(groups, spans, weights, base, dtype):
    parts = [part for group in groups for part in group]
    rows = parts[0].shape[0]
    depth = sum(part.shape[1] for part in parts)
    width = weights[0].shape[1]
    bases = [] if base is None else [base]
    return pl.pallas_call(
        functools.partial(project_kernel, [len(g) for g in groups], spans, base is not None),
        out_shape=jax.ShapeDtypeStruct((rows, width), dtype),
        in_specs=[VMEM] * (2 + len(parts) + len(bases)),
        out_specs=VMEM,
        scratch_shapes=[pltpu.VMEM((rows, depth), parts[0].dtype)],
        compiler_params=pltpu.CompilerParams(vmem_limit_bytes=PROJECT_VMEM),
        cost_estimate=pl.CostEstimate(
            flops=rows * width,
            bytes_accessed=rows * width,
            transcendentals=0,
        ),
        name="project",
    )(*[in_vmem(weight) for weight in weights], *parts, *bases)


def swap(part, bit):
    size = lax.axis_size("tensor")
    return lax.ppermute(part, "tensor", [(i, i ^ bit) for i in range(size)])


def trade(pieces):
    devices = lax.axis_size("dp")
    rows = [[at + place for place in LISTED] for at in range(0, devices, ROW)]
    return lax.all_to_all(pieces, "dp", 0, 0, tiled=True, axis_index_groups=rows)


def onward(piece, step):
    devices = lax.axis_size("dp")
    return lax.ppermute(piece, "dp", [(i, (i + step) % devices) for i in range(devices)])


def per_device(queries, key_proj, value_proj, out_weight, parents):
    me = lax.axis_index("tensor")
    first = (lax.axis_index("dp") * 2).astype(jnp.int32).reshape(1)
    pieces = trade(pack(key_proj, value_proj)).reshape(ROW_SEGS, 2 * PIECE, HEAD_DIM)
    to_next, to_second = carry_out(first, parents, pieces)
    inside = pick(first, parents, pieces)
    far = trade(merge(*inside, onward(to_next, ROW), onward(to_second, 2 * ROW)))

    width = queries.shape[1]
    bring = (me.astype(jnp.int32).reshape(1), out_weight)
    own, across, weights, head = [], [], [], 0
    for c, (size, blocks) in enumerate([(2, ()), (3, (0, 1)), (3, (2, 3))]):
        after = [across[c - 2]] if c >= 2 else []
        part, *brought = attend(
            first, parents, queries, key_proj, value_proj, far, head, size, blocks, bring, after
        )
        weights += brought
        own.append(part)
        across.append(swap(part, 2))
        head += size
    own = lax.optimization_barrier(own)
    beside = [swap(part, 1) for part in own]
    corner = [swap(part, 1) for part in across[:-1]]
    near = project(
        [own + beside, across[:-1], corner[:-1]], [(0, 0), (1, 0), (1, width)], weights, None, jnp.float32
    )
    last, near = lax.optimization_barrier((across[-1], near))
    corner.append(swap(last, 1))
    done = width - last.shape[1]
    turned = sum(part.shape[1] for part in corner[:-2])
    return project(
        [[last], corner[-2:]], [(1, done), (1, width + turned)], weights, near, jnp.bfloat16
    )


def solution(mesh):
    placed = (P("dp", "tensor"), P("dp", "tensor"), P("dp", "tensor"), P(None, "tensor"), P())
    return jax.shard_map(
        per_device, mesh=mesh, in_specs=placed, out_specs=P("dp", "tensor"), check_vma=False
    )
```

```python
import functools
import math

import jax
import jax.numpy as jnp
from jax import lax
from jax.experimental import pallas as pl
from jax.experimental.pallas import tpu as pltpu
from jax.sharding import PartitionSpec as P

HEAD_DIM = 128
SEG_LEN = 256
LEVELS = 4
ROW = 8
ROW_SEGS = 2 * ROW
LISTED = (5, 4, 3, 2, 1, 0, 7, 6)
PIECE = SEG_LEN // ROW
PATH = LEVELS * SEG_LEN
STACK = LEVELS * PIECE
MASKED = -1e30
EXP2_SCALE = math.log2(math.e) * HEAD_DIM ** (-0.5)
SMALL_VMEM = 6 * 1024 * 1024
ATTEND_VMEM = 18 * 1024 * 1024
PROJECT_VMEM = 14 * 1024 * 1024
TILE = 256

VMEM = pl.BlockSpec(memory_space=pltpu.VMEM)
SMEM = pl.BlockSpec(memory_space=pltpu.SMEM)
ANY = pl.BlockSpec(memory_space=pl.ANY)
HBM = pl.BlockSpec(memory_space=pltpu.HBM)
FLAG_ROWS = 16


def in_hbm(array):
    return pltpu.with_memory_space_constraint(array, pltpu.HBM)


def in_vmem(array):
    return pltpu.with_memory_space_constraint(array, pltpu.VMEM)


def path_of(parents_ref, seg):
    path = [parents_ref[seg]]
    for _ in range(LEVELS - 1):
        up = parents_ref[jnp.maximum(path[-1], 0)]
        path.append(jnp.where(path[-1] >= 0, up, -1))
    depth = sum((p >= 0).astype(jnp.int32) for p in path)
    return path, depth


def level_of(path, depth, level):
    found = jnp.int32(0)
    for up in range(LEVELS):
        found = jnp.where(depth - 1 - up == level, path[up], found)
    return found


def pack_kernel(key_ref, value_ref, piece_ref, held_ref, sem):
    copies = [
        pltpu.make_async_copy(source, held_ref.at[i], sem.at[i])
        for i, source in enumerate([key_ref, value_ref])
    ]
    for copy in copies:
        copy.start()
    for i, copy in enumerate(copies):
        copy.wait()
        for piece in range(ROW):
            for seg in range(2):
                rows = pl.ds(seg * SEG_LEN + piece * PIECE, PIECE)
                piece_ref[piece, seg, i * PIECE : (i + 1) * PIECE] = held_ref[i, rows]


def pack(keys, values):
    return pl.pallas_call(
        pack_kernel,
        out_shape=jax.ShapeDtypeStruct((ROW, 2, 2 * PIECE, HEAD_DIM), keys.dtype),
        in_specs=[HBM, HBM],
        out_specs=VMEM,
        scratch_shapes=[pltpu.VMEM((2,) + keys.shape, keys.dtype), pltpu.SemaphoreType.DMA((2,))],
        compiler_params=pltpu.CompilerParams(vmem_limit_bytes=SMALL_VMEM),
        cost_estimate=pl.CostEstimate(flops=0, bytes_accessed=1 << 19, transcendentals=0),
        name="pack",
    )(in_hbm(keys), in_hbm(values))


def row_start(first_ref):
    return (first_ref[0] // ROW_SEGS) * ROW_SEGS


def slot_of(seg):
    member = (LISTED[0] + ROW - seg // 2) % ROW
    return 2 * member + seg % 2


def bring_parents(source_ref, parents_ref, sem):
    copy = pltpu.make_async_copy(source_ref, parents_ref, sem)
    copy.start()
    copy.wait()


def carry_kernel(first_ref, source_ref, pieces_ref, next_ref, second_ref, parents_ref, sem):
    bring_parents(source_ref, parents_ref, sem)
    base = row_start(first_ref)
    last = parents_ref.shape[0] - 1

    def held(path, depth, level):
        return pieces_ref[slot_of(jnp.clip(level_of(path, depth, level) - base, 0, ROW_SEGS - 1))]

    path, depth = path_of(parents_ref, jnp.minimum(base + ROW_SEGS, last))
    for level in range(LEVELS):
        next_ref[level] = held(path, depth, level)
    path, depth = path_of(parents_ref, jnp.minimum(base + 2 * ROW_SEGS, last))
    second_ref[0] = held(path, depth, 0)


def carry_out(first, parents, pieces):
    shape = lambda n: jax.ShapeDtypeStruct((n,) + pieces.shape[1:], pieces.dtype)
    return pl.pallas_call(
        carry_kernel,
        out_shape=(shape(LEVELS), shape(1)),
        in_specs=[SMEM, HBM, VMEM],
        out_specs=(VMEM, VMEM),
        scratch_shapes=[pltpu.SMEM(parents.shape, parents.dtype), pltpu.SemaphoreType.DMA],
        compiler_params=pltpu.CompilerParams(vmem_limit_bytes=SMALL_VMEM),
        cost_estimate=pl.CostEstimate(flops=0, bytes_accessed=1 << 18, transcendentals=0),
        name="carry_out",
    )(first, in_hbm(parents), pieces)


def pick_kernel(
    first_ref, source_ref, pieces_ref, inside_ref, next_ref, second_ref, parents_ref, sem
):
    bring_parents(source_ref, parents_ref, sem)
    base = row_start(first_ref)
    ones = lambda on: jnp.full((FLAG_ROWS, HEAD_DIM), on, jnp.float32).astype(jnp.bfloat16)
    for target, place in enumerate(LISTED):
        path, depth = path_of(parents_ref, base + 2 * place)
        for level in range(LEVELS):
            seg = level_of(path, depth, level)
            within = seg >= base
            piece = pieces_ref[slot_of(jnp.maximum(seg - base, 0))]
            inside_ref[target, level] = jnp.where(within, piece, jnp.zeros_like(piece))
            before = jnp.logical_and(seg < base, seg >= base - ROW_SEGS)
            next_ref[target, level] = ones(jnp.where(before, 1.0, 0.0))
            if level == 0:
                second_ref[target] = ones(jnp.where(seg < base - ROW_SEGS, 1.0, 0.0))


def pick(first, parents, pieces):
    shape = lambda *dims: jax.ShapeDtypeStruct(dims, pieces.dtype)
    return pl.pallas_call(
        pick_kernel,
        out_shape=(
            shape(ROW, LEVELS, *pieces.shape[1:]),
            shape(ROW, LEVELS, FLAG_ROWS, HEAD_DIM),
            shape(ROW, FLAG_ROWS, HEAD_DIM),
        ),
        in_specs=[SMEM, HBM, VMEM],
        out_specs=(VMEM, VMEM, VMEM),
        scratch_shapes=[pltpu.SMEM(parents.shape, parents.dtype), pltpu.SemaphoreType.DMA],
        compiler_params=pltpu.CompilerParams(vmem_limit_bytes=SMALL_VMEM),
        cost_estimate=pl.CostEstimate(flops=0, bytes_accessed=1 << 20, transcendentals=0),
        name="pick",
    )(first, in_hbm(parents), pieces)


def merge_kernel(inside_ref, on_next_ref, on_second_ref, next_ref, second_ref, picked_ref):
    for level in range(LEVELS):
        for at in range(0, 2 * PIECE, FLAG_ROWS):
            rows = pl.ds(at, FLAG_ROWS)
            carried = next_ref[level, rows]
            older = second_ref[0, rows]
            for target in range(ROW):
                total = inside_ref[target, level, rows] + carried * on_next_ref[target, level]
                if level == 0:
                    total = total + older * on_second_ref[target]
                picked_ref[target, level, rows] = total


def merge(inside, on_next, on_second, carried, second):
    return pl.pallas_call(
        merge_kernel,
        out_shape=jax.ShapeDtypeStruct(inside.shape, inside.dtype),
        in_specs=[VMEM] * 5,
        out_specs=VMEM,
        compiler_params=pltpu.CompilerParams(vmem_limit_bytes=SMALL_VMEM),
        cost_estimate=pl.CostEstimate(flops=0, bytes_accessed=1 << 20, transcendentals=0),
        name="merge",
    )(inside, on_next, on_second, carried, second)


def attend_kernel(first_head, blocks, first_ref, *refs):
    sources, (far_ref, *refs) = refs[:4], refs[4:]
    if blocks:
        me_ref, weight_ref = refs[:2]
        weight_sem = refs.pop()
        held_ref = refs.pop(-8)
    out_ref, path_key_ref, path_value_ref, parents_ref, query_ref, key_ref, value_ref, sem = refs[-8:]
    heads = query_ref.shape[1] // HEAD_DIM
    columns = pl.ds(first_head * HEAD_DIM, query_ref.shape[1])
    views = [sources[0], sources[1].at[:, columns], sources[2], sources[3]]
    fetches = [
        pltpu.make_async_copy(view, target, sem.at[i])
        for i, (view, target) in enumerate(zip(views, [parents_ref, query_ref, key_ref, value_ref]))
    ]
    copies = weight_copies(blocks, me_ref, weight_ref, held_ref, weight_sem) if blocks else []
    for copy in fetches + copies:
        copy.start()

    def scores_of(query, keys):
        return lax.dot_general(
            query, keys, (((1,), (1,)), ((), ())), preferred_element_type=jnp.float32
        )

    def with_ones(values):
        return jnp.concatenate([values, jnp.ones_like(values)], axis=1)

    for piece in range(ROW):
        for level in range(LEVELS):
            rows = pl.ds(piece * STACK + level * PIECE, PIECE)
            path_key_ref[rows, :HEAD_DIM] = far_ref[piece, level, :PIECE]
            path_value_ref[rows, :HEAD_DIM] = far_ref[piece, level, PIECE:]
    path_value_ref[:, HEAD_DIM:] = jnp.ones((PATH, HEAD_DIM), jnp.bfloat16)
    for copy in fetches:
        copy.wait()
    first = first_ref[0]
    _, depth0 = path_of(parents_ref, first)
    _, depth1 = path_of(parents_ref, first + 1)
    follows = jnp.where(parents_ref[first + 1] == first, 0.0, MASKED)
    row = lax.broadcasted_iota(jnp.int32, (PATH, HEAD_DIM), 0)
    lane = lax.broadcasted_iota(jnp.int32, (PATH, HEAD_DIM), 1)
    level = lax.rem(row // PIECE, LEVELS)
    limit = jnp.where(lane == 0, depth0, jnp.where(lane == 1, jnp.minimum(depth0, depth1), LEVELS))
    path_key_ref[:, HEAD_DIM:] = jnp.where(level < limit, 0.0, MASKED).astype(jnp.bfloat16)
    path_keys, path_values = path_key_ref[...], path_value_ref[...]

    rows = lax.broadcasted_iota(jnp.int32, (2 * SEG_LEN, HEAD_DIM), 0)
    lanes = lax.broadcasted_iota(jnp.int32, (2 * SEG_LEN, HEAD_DIM), 1)
    marks = (lanes == rows // SEG_LEN).astype(jnp.float32).astype(jnp.bfloat16)
    causal = lax.broadcasted_iota(jnp.int32, (SEG_LEN, SEG_LEN), 1) <= lax.broadcasted_iota(
        jnp.int32, (SEG_LEN, SEG_LEN), 0
    )
    halves = [slice(0, SEG_LEN), slice(SEG_LEN, 2 * SEG_LEN)]
    own_values = [with_ones(value_ref[half]) for half in halves]
    for head in range(heads):
        query = query_ref[:, head * HEAD_DIM : (head + 1) * HEAD_DIM]
        path_scores = scores_of(jnp.concatenate([query, marks], axis=1), path_keys)
        own = [
            [(jnp.where(causal, scores_of(query[half], key_ref[half]), MASKED), values)]
            for half, values in zip(halves, own_values)
        ]
        own[1].append((scores_of(query[halves[1]], key_ref[halves[0]]) + follows, own_values[0]))
        path_weights, own_parts = [], []
        for half, blocks in zip(halves, own):
            row_max = functools.reduce(
                jnp.maximum,
                [jnp.max(s, axis=1, keepdims=True) for s, _ in blocks]
                + [jnp.max(path_scores[half], axis=1, keepdims=True)],
            )
            weigh = lambda s: jnp.exp2((s - row_max) * EXP2_SCALE).astype(jnp.bfloat16)
            path_weights.append(weigh(path_scores[half]))
            own_parts.append(
                sum(
                    jnp.dot(weigh(s), values, preferred_element_type=jnp.float32)
                    for s, values in blocks
                )
            )
        total = jnp.dot(
            jnp.concatenate(path_weights, axis=0), path_values, preferred_element_type=jnp.float32
        ) + jnp.concatenate(own_parts, axis=0)
        mixture = total[:, :HEAD_DIM] / total[:, HEAD_DIM:]
        out_ref[:, head * HEAD_DIM : (head + 1) * HEAD_DIM] = mixture.astype(out_ref.dtype)
    for copy in copies:
        copy.wait()


def weight_copies(blocks, me_ref, weight_ref, held_ref, sem):
    block = weight_ref.shape[0] // 4
    copies = []
    for i, bit in enumerate(blocks):
        rows = pl.ds(pl.multiple_of((me_ref[0] ^ bit) * block, block), block)
        copies.append(
            pltpu.make_async_copy(
                weight_ref.at[rows], held_ref.at[pl.ds(i * block, block)], sem.at[i]
            )
        )
    return copies


def attend(first, parents, queries, keys, values, far, first_head, heads, blocks, bring, after):
    rows = queries.shape[0]
    pairs = heads * rows * (PATH + SEG_LEN + SEG_LEN // 2)
    out_shape = [jax.ShapeDtypeStruct((rows, heads * HEAD_DIM), jnp.bfloat16)]
    in_specs = [SMEM] + [HBM] * 4 + [VMEM]
    scratch = [pltpu.VMEM((PATH, 2 * HEAD_DIM), jnp.bfloat16)] * 2 + [
        pltpu.SMEM(parents.shape, parents.dtype),
        pltpu.VMEM((rows, heads * HEAD_DIM), queries.dtype),
        pltpu.VMEM(keys.shape, keys.dtype),
        pltpu.VMEM(values.shape, values.dtype),
        pltpu.SemaphoreType.DMA((4,)),
    ]
    if blocks:
        me, weight = bring
        bring = [me, in_hbm(weight)]
        in_specs += [SMEM, HBM]
        shape = (len(blocks) * weight.shape[0] // 4, weight.shape[1])
        out_shape.append(pltpu.VMEM(shape, weight.dtype))
        scratch.append(pltpu.SemaphoreType.DMA((len(blocks),)))
    else:
        bring = []
    return pl.pallas_call(
        functools.partial(attend_kernel, first_head, blocks),
        out_shape=out_shape,
        in_specs=in_specs + [ANY] * len(after),
        out_specs=[VMEM] * len(out_shape),
        scratch_shapes=scratch,
        compiler_params=pltpu.CompilerParams(vmem_limit_bytes=ATTEND_VMEM),
        cost_estimate=pl.CostEstimate(
            flops=pairs * HEAD_DIM * 10,
            bytes_accessed=heads * rows * HEAD_DIM * 4 + 8 * PATH * HEAD_DIM,
            transcendentals=pairs,
        ),
        name="attend",
    )(
        first,
        in_hbm(parents),
        in_hbm(queries),
        in_hbm(keys),
        in_hbm(values),
        far,
        *bring,
        *after,
    )


def project_kernel(counts, spans, has_base, near_ref, far_ref, *refs):
    parts = refs[: sum(counts)]
    out_ref, held_ref = refs[-2:]
    at, ends = 0, [0]
    for count in counts:
        for part in parts[:count]:
            held_ref[:, at : at + part.shape[1]] = part[...]
            at += part.shape[1]
        parts = parts[count:]
        ends.append(at)
    for column in range(0, out_ref.shape[1], TILE):
        columns = slice(column, column + TILE)
        total = refs[sum(counts)][:, columns] if has_base else None
        for (half, start), begin, end in zip(spans, ends, ends[1:]):
            product = jnp.dot(
                held_ref[:, begin:end],
                (near_ref, far_ref)[half][start : start + end - begin, columns],
                preferred_element_type=jnp.float32,
            )
            total = product if total is None else total + product
        out_ref[:, columns] = total.astype(out_ref.dtype)


def project(groups, spans, weights, base, dtype):
    parts = [part for group in groups for part in group]
    rows = parts[0].shape[0]
    depth = sum(part.shape[1] for part in parts)
    width = weights[0].shape[1]
    bases = [] if base is None else [base]
    return pl.pallas_call(
        functools.partial(project_kernel, [len(g) for g in groups], spans, base is not None),
        out_shape=jax.ShapeDtypeStruct((rows, width), dtype),
        in_specs=[VMEM] * (2 + len(parts) + len(bases)),
        out_specs=VMEM,
        scratch_shapes=[pltpu.VMEM((rows, depth), parts[0].dtype)],
        compiler_params=pltpu.CompilerParams(vmem_limit_bytes=PROJECT_VMEM),
        cost_estimate=pl.CostEstimate(
            flops=rows * width,
            bytes_accessed=rows * width,
            transcendentals=0,
        ),
        name="project",
    )(*[in_vmem(weight) for weight in weights], *parts, *bases)


def swap(part, bit):
    size = lax.axis_size("tensor")
    return lax.ppermute(part, "tensor", [(i, i ^ bit) for i in range(size)])


def trade(pieces):
    devices = lax.axis_size("dp")
    rows = [[at + place for place in LISTED] for at in range(0, devices, ROW)]
    return lax.all_to_all(pieces, "dp", 0, 0, tiled=True, axis_index_groups=rows)


def onward(piece, step):
    devices = lax.axis_size("dp")
    return lax.ppermute(piece, "dp", [(i, (i + step) % devices) for i in range(devices)])


def per_device(queries, key_proj, value_proj, out_weight, parents):
    me = lax.axis_index("tensor")
    first = (lax.axis_index("dp") * 2).astype(jnp.int32).reshape(1)
    pieces = trade(pack(key_proj, value_proj)).reshape(ROW_SEGS, 2 * PIECE, HEAD_DIM)
    to_next, to_second = carry_out(first, parents, pieces)
    inside = pick(first, parents, pieces)
    far = trade(merge(*inside, onward(to_next, ROW), onward(to_second, 2 * ROW)))

    width = queries.shape[1]
    bring = (me.astype(jnp.int32).reshape(1), out_weight)
    own, across, weights, head = [], [], [], 0
    for c, (size, blocks) in enumerate([(3, ()), (3, (0, 1)), (2, (2, 3))]):
        after = [across[c - 2]] if c >= 2 else []
        part, *brought = attend(
            first, parents, queries, key_proj, value_proj, far, head, size, blocks, bring, after
        )
        weights += brought
        own.append(part)
        across.append(swap(part, 2))
        head += size
    beside = [swap(part, 1) for part in own]
    corner = [swap(part, 1) for part in across[:-1]]
    near = project(
        [own + beside, across[:-1], corner[:-1]], [(0, 0), (1, 0), (1, width)], weights, None, jnp.float32
    )
    last, near = lax.optimization_barrier((across[-1], near))
    corner.append(swap(last, 1))
    done = width - last.shape[1]
    turned = sum(part.shape[1] for part in corner[:-2])
    return project(
        [[last], corner[-2:]], [(1, done), (1, width + turned)], weights, near, jnp.bfloat16
    )


def solution(mesh):
    placed = (P("dp", "tensor"), P("dp", "tensor"), P("dp", "tensor"), P(None, "tensor"), P())
    return jax.shard_map(
        per_device, mesh=mesh, in_specs=placed, out_specs=P("dp", "tensor"), check_vma=False
    )
```

```python
import functools
import math

import jax
import jax.numpy as jnp
from jax import lax
from jax.experimental import pallas as pl
from jax.experimental.pallas import tpu as pltpu
from jax.sharding import PartitionSpec as P

HEAD_DIM = 128
SEG_LEN = 256
LEVELS = 4
ROW = 8
ROW_SEGS = 2 * ROW
LISTED = (7, 3, 6, 2, 5, 1, 4, 0)
PIECE = SEG_LEN // ROW
PATH = LEVELS * SEG_LEN
STACK = LEVELS * PIECE
MASKED = -1e30
EXP2_SCALE = math.log2(math.e) * HEAD_DIM ** (-0.5)
SMALL_VMEM = 6 * 1024 * 1024
ATTEND_VMEM = 18 * 1024 * 1024
PROJECT_VMEM = 14 * 1024 * 1024
TILE = 256

VMEM = pl.BlockSpec(memory_space=pltpu.VMEM)
SMEM = pl.BlockSpec(memory_space=pltpu.SMEM)
ANY = pl.BlockSpec(memory_space=pl.ANY)
HBM = pl.BlockSpec(memory_space=pltpu.HBM)
FLAG_ROWS = 16


def in_hbm(array):
    return pltpu.with_memory_space_constraint(array, pltpu.HBM)


def in_vmem(array):
    return pltpu.with_memory_space_constraint(array, pltpu.VMEM)


def path_of(parents_ref, seg):
    path = [parents_ref[seg]]
    for _ in range(LEVELS - 1):
        up = parents_ref[jnp.maximum(path[-1], 0)]
        path.append(jnp.where(path[-1] >= 0, up, -1))
    depth = sum((p >= 0).astype(jnp.int32) for p in path)
    return path, depth


def level_of(path, depth, level):
    found = jnp.int32(0)
    for up in range(LEVELS):
        found = jnp.where(depth - 1 - up == level, path[up], found)
    return found


def pack_kernel(key_ref, value_ref, piece_ref, held_ref, sem):
    copies = [
        pltpu.make_async_copy(source, held_ref.at[i], sem.at[i])
        for i, source in enumerate([key_ref, value_ref])
    ]
    for copy in copies:
        copy.start()
    for i, copy in enumerate(copies):
        copy.wait()
        for piece in range(ROW):
            for seg in range(2):
                rows = pl.ds(seg * SEG_LEN + piece * PIECE, PIECE)
                piece_ref[piece, seg, i * PIECE : (i + 1) * PIECE] = held_ref[i, rows]


def pack(keys, values):
    return pl.pallas_call(
        pack_kernel,
        out_shape=jax.ShapeDtypeStruct((ROW, 2, 2 * PIECE, HEAD_DIM), keys.dtype),
        in_specs=[HBM, HBM],
        out_specs=VMEM,
        scratch_shapes=[pltpu.VMEM((2,) + keys.shape, keys.dtype), pltpu.SemaphoreType.DMA((2,))],
        compiler_params=pltpu.CompilerParams(vmem_limit_bytes=SMALL_VMEM),
        cost_estimate=pl.CostEstimate(flops=0, bytes_accessed=1 << 19, transcendentals=0),
        name="pack",
    )(in_hbm(keys), in_hbm(values))


def row_start(first_ref):
    return (first_ref[0] // ROW_SEGS) * ROW_SEGS


def slot_of(seg):
    place = seg // 2
    member = 2 * (ROW // 2 - 1 - place % (ROW // 2)) + 1 - place // (ROW // 2)
    return 2 * member + seg % 2


def bring_parents(source_ref, parents_ref, sem):
    copy = pltpu.make_async_copy(source_ref, parents_ref, sem)
    copy.start()
    copy.wait()


def carry_kernel(first_ref, source_ref, pieces_ref, next_ref, second_ref, parents_ref, sem):
    bring_parents(source_ref, parents_ref, sem)
    base = row_start(first_ref)
    last = parents_ref.shape[0] - 1

    def held(path, depth, level):
        return pieces_ref[slot_of(jnp.clip(level_of(path, depth, level) - base, 0, ROW_SEGS - 1))]

    path, depth = path_of(parents_ref, jnp.minimum(base + ROW_SEGS, last))
    for level in range(LEVELS):
        next_ref[level] = held(path, depth, level)
    path, depth = path_of(parents_ref, jnp.minimum(base + 2 * ROW_SEGS, last))
    second_ref[0] = held(path, depth, 0)


def carry_out(first, parents, pieces):
    shape = lambda n: jax.ShapeDtypeStruct((n,) + pieces.shape[1:], pieces.dtype)
    return pl.pallas_call(
        carry_kernel,
        out_shape=(shape(LEVELS), shape(1)),
        in_specs=[SMEM, HBM, VMEM],
        out_specs=(VMEM, VMEM),
        scratch_shapes=[pltpu.SMEM(parents.shape, parents.dtype), pltpu.SemaphoreType.DMA],
        compiler_params=pltpu.CompilerParams(vmem_limit_bytes=SMALL_VMEM),
        cost_estimate=pl.CostEstimate(flops=0, bytes_accessed=1 << 18, transcendentals=0),
        name="carry_out",
    )(first, in_hbm(parents), pieces)


def pick_kernel(
    first_ref, source_ref, pieces_ref, inside_ref, next_ref, second_ref, parents_ref, sem
):
    bring_parents(source_ref, parents_ref, sem)
    base = row_start(first_ref)
    ones = lambda on: jnp.full((FLAG_ROWS, HEAD_DIM), on, jnp.float32).astype(jnp.bfloat16)
    for target, place in enumerate(LISTED):
        path, depth = path_of(parents_ref, base + 2 * place)
        for level in range(LEVELS):
            seg = level_of(path, depth, level)
            within = seg >= base
            piece = pieces_ref[slot_of(jnp.maximum(seg - base, 0))]
            inside_ref[target, level] = jnp.where(within, piece, jnp.zeros_like(piece))
            before = jnp.logical_and(seg < base, seg >= base - ROW_SEGS)
            next_ref[target, level] = ones(jnp.where(before, 1.0, 0.0))
            if level == 0:
                second_ref[target] = ones(jnp.where(seg < base - ROW_SEGS, 1.0, 0.0))


def pick(first, parents, pieces):
    shape = lambda *dims: jax.ShapeDtypeStruct(dims, pieces.dtype)
    return pl.pallas_call(
        pick_kernel,
        out_shape=(
            shape(ROW, LEVELS, *pieces.shape[1:]),
            shape(ROW, LEVELS, FLAG_ROWS, HEAD_DIM),
            shape(ROW, FLAG_ROWS, HEAD_DIM),
        ),
        in_specs=[SMEM, HBM, VMEM],
        out_specs=(VMEM, VMEM, VMEM),
        scratch_shapes=[pltpu.SMEM(parents.shape, parents.dtype), pltpu.SemaphoreType.DMA],
        compiler_params=pltpu.CompilerParams(vmem_limit_bytes=SMALL_VMEM),
        cost_estimate=pl.CostEstimate(flops=0, bytes_accessed=1 << 20, transcendentals=0),
        name="pick",
    )(first, in_hbm(parents), pieces)


def merge_kernel(inside_ref, on_next_ref, on_second_ref, next_ref, second_ref, picked_ref):
    for level in range(LEVELS):
        for at in range(0, 2 * PIECE, FLAG_ROWS):
            rows = pl.ds(at, FLAG_ROWS)
            carried = next_ref[level, rows]
            older = second_ref[0, rows]
            for target in range(ROW):
                total = inside_ref[target, level, rows] + carried * on_next_ref[target, level]
                if level == 0:
                    total = total + older * on_second_ref[target]
                picked_ref[target, level, rows] = total


def merge(inside, on_next, on_second, carried, second):
    return pl.pallas_call(
        merge_kernel,
        out_shape=jax.ShapeDtypeStruct(inside.shape, inside.dtype),
        in_specs=[VMEM] * 5,
        out_specs=VMEM,
        compiler_params=pltpu.CompilerParams(vmem_limit_bytes=SMALL_VMEM),
        cost_estimate=pl.CostEstimate(flops=0, bytes_accessed=1 << 20, transcendentals=0),
        name="merge",
    )(inside, on_next, on_second, carried, second)


def attend_kernel(first_head, blocks, first_ref, *refs):
    sources, (far_ref, *refs) = refs[:4], refs[4:]
    if blocks:
        me_ref, weight_ref = refs[:2]
        weight_sem = refs.pop()
        held_ref = refs.pop(-8)
    out_ref, path_key_ref, path_value_ref, parents_ref, query_ref, key_ref, value_ref, sem = refs[-8:]
    heads = query_ref.shape[1] // HEAD_DIM
    columns = pl.ds(first_head * HEAD_DIM, query_ref.shape[1])
    views = [sources[0], sources[1].at[:, columns], sources[2], sources[3]]
    fetches = [
        pltpu.make_async_copy(view, target, sem.at[i])
        for i, (view, target) in enumerate(zip(views, [parents_ref, query_ref, key_ref, value_ref]))
    ]
    copies = weight_copies(blocks, me_ref, weight_ref, held_ref, weight_sem) if blocks else []
    for copy in fetches + copies:
        copy.start()

    def scores_of(query, keys):
        return lax.dot_general(
            query, keys, (((1,), (1,)), ((), ())), preferred_element_type=jnp.float32
        )

    def with_ones(values):
        return jnp.concatenate([values, jnp.ones_like(values)], axis=1)

    for piece in range(ROW):
        for level in range(LEVELS):
            rows = pl.ds(piece * STACK + level * PIECE, PIECE)
            path_key_ref[rows, :HEAD_DIM] = far_ref[piece, level, :PIECE]
            path_value_ref[rows, :HEAD_DIM] = far_ref[piece, level, PIECE:]
    path_value_ref[:, HEAD_DIM:] = jnp.ones((PATH, HEAD_DIM), jnp.bfloat16)
    fetches[0].wait()
    first = first_ref[0]
    _, depth0 = path_of(parents_ref, first)
    _, depth1 = path_of(parents_ref, first + 1)
    follows = jnp.where(parents_ref[first + 1] == first, 0.0, MASKED)
    row = lax.broadcasted_iota(jnp.int32, (PATH, HEAD_DIM), 0)
    lane = lax.broadcasted_iota(jnp.int32, (PATH, HEAD_DIM), 1)
    level = lax.rem(row // PIECE, LEVELS)
    limit = jnp.where(lane == 0, depth0, jnp.where(lane == 1, jnp.minimum(depth0, depth1), LEVELS))
    path_key_ref[:, HEAD_DIM:] = jnp.where(level < limit, 0.0, MASKED).astype(jnp.bfloat16)
    for copy in fetches[1:]:
        copy.wait()
    path_keys, path_values = path_key_ref[...], path_value_ref[...]

    rows = lax.broadcasted_iota(jnp.int32, (2 * SEG_LEN, HEAD_DIM), 0)
    lanes = lax.broadcasted_iota(jnp.int32, (2 * SEG_LEN, HEAD_DIM), 1)
    marks = (lanes == rows // SEG_LEN).astype(jnp.float32).astype(jnp.bfloat16)
    causal = lax.broadcasted_iota(jnp.int32, (SEG_LEN, SEG_LEN), 1) <= lax.broadcasted_iota(
        jnp.int32, (SEG_LEN, SEG_LEN), 0
    )
    halves = [slice(0, SEG_LEN), slice(SEG_LEN, 2 * SEG_LEN)]
    own_values = [with_ones(value_ref[half]) for half in halves]
    for head in range(heads):
        query = query_ref[:, head * HEAD_DIM : (head + 1) * HEAD_DIM]
        path_scores = scores_of(jnp.concatenate([query, marks], axis=1), path_keys)
        own = [
            [(jnp.where(causal, scores_of(query[half], key_ref[half]), MASKED), values)]
            for half, values in zip(halves, own_values)
        ]
        own[1].append((scores_of(query[halves[1]], key_ref[halves[0]]) + follows, own_values[0]))
        path_weights, own_parts = [], []
        for half, blocks in zip(halves, own):
            row_max = functools.reduce(
                jnp.maximum,
                [jnp.max(s, axis=1, keepdims=True) for s, _ in blocks]
                + [jnp.max(path_scores[half], axis=1, keepdims=True)],
            )
            weigh = lambda s: jnp.exp2((s - row_max) * EXP2_SCALE).astype(jnp.bfloat16)
            path_weights.append(weigh(path_scores[half]))
            own_parts.append(
                sum(
                    jnp.dot(weigh(s), values, preferred_element_type=jnp.float32)
                    for s, values in blocks
                )
            )
        total = jnp.dot(
            jnp.concatenate(path_weights, axis=0), path_values, preferred_element_type=jnp.float32
        ) + jnp.concatenate(own_parts, axis=0)
        mixture = total[:, :HEAD_DIM] / total[:, HEAD_DIM:]
        out_ref[:, head * HEAD_DIM : (head + 1) * HEAD_DIM] = mixture.astype(out_ref.dtype)
    for copy in copies:
        copy.wait()


def weight_copies(blocks, me_ref, weight_ref, held_ref, sem):
    block = weight_ref.shape[0] // 4
    copies = []
    for i, bit in enumerate(blocks):
        rows = pl.ds(pl.multiple_of((me_ref[0] ^ bit) * block, block), block)
        copies.append(
            pltpu.make_async_copy(
                weight_ref.at[rows], held_ref.at[pl.ds(i * block, block)], sem.at[i]
            )
        )
    return copies


def attend(first, parents, queries, keys, values, far, first_head, heads, blocks, bring, after):
    rows = queries.shape[0]
    pairs = heads * rows * (PATH + SEG_LEN + SEG_LEN // 2)
    out_shape = [jax.ShapeDtypeStruct((rows, heads * HEAD_DIM), jnp.bfloat16)]
    in_specs = [SMEM] + [HBM] * 4 + [VMEM]
    scratch = [pltpu.VMEM((PATH, 2 * HEAD_DIM), jnp.bfloat16)] * 2 + [
        pltpu.SMEM(parents.shape, parents.dtype),
        pltpu.VMEM((rows, heads * HEAD_DIM), queries.dtype),
        pltpu.VMEM(keys.shape, keys.dtype),
        pltpu.VMEM(values.shape, values.dtype),
        pltpu.SemaphoreType.DMA((4,)),
    ]
    if blocks:
        me, weight = bring
        bring = [me, in_hbm(weight)]
        in_specs += [SMEM, HBM]
        shape = (len(blocks) * weight.shape[0] // 4, weight.shape[1])
        out_shape.append(pltpu.VMEM(shape, weight.dtype))
        scratch.append(pltpu.SemaphoreType.DMA((len(blocks),)))
    else:
        bring = []
    return pl.pallas_call(
        functools.partial(attend_kernel, first_head, blocks),
        out_shape=out_shape,
        in_specs=in_specs + [ANY] * len(after),
        out_specs=[VMEM] * len(out_shape),
        scratch_shapes=scratch,
        compiler_params=pltpu.CompilerParams(vmem_limit_bytes=ATTEND_VMEM),
        cost_estimate=pl.CostEstimate(
            flops=pairs * HEAD_DIM * 10,
            bytes_accessed=heads * rows * HEAD_DIM * 4 + 8 * PATH * HEAD_DIM,
            transcendentals=pairs,
        ),
        name="attend",
    )(
        first,
        in_hbm(parents),
        in_hbm(queries),
        in_hbm(keys),
        in_hbm(values),
        far,
        *bring,
        *after,
    )


def project_kernel(counts, spans, has_base, near_ref, far_ref, *refs):
    parts = refs[: sum(counts)]
    out_ref, held_ref = refs[-2:]
    at, ends = 0, [0]
    for count in counts:
        for part in parts[:count]:
            held_ref[:, at : at + part.shape[1]] = part[...]
            at += part.shape[1]
        parts = parts[count:]
        ends.append(at)
    for column in range(0, out_ref.shape[1], TILE):
        columns = slice(column, column + TILE)
        total = refs[sum(counts)][:, columns] if has_base else None
        for (half, start), begin, end in zip(spans, ends, ends[1:]):
            product = jnp.dot(
                held_ref[:, begin:end],
                (near_ref, far_ref)[half][start : start + end - begin, columns],
                preferred_element_type=jnp.float32,
            )
            total = product if total is None else total + product
        out_ref[:, columns] = total.astype(out_ref.dtype)


def project(groups, spans, weights, base, dtype):
    parts = [part for group in groups for part in group]
    rows = parts[0].shape[0]
    depth = sum(part.shape[1] for part in parts)
    width = weights[0].shape[1]
    bases = [] if base is None else [base]
    return pl.pallas_call(
        functools.partial(project_kernel, [len(g) for g in groups], spans, base is not None),
        out_shape=jax.ShapeDtypeStruct((rows, width), dtype),
        in_specs=[VMEM] * (2 + len(parts) + len(bases)),
        out_specs=VMEM,
        scratch_shapes=[pltpu.VMEM((rows, depth), parts[0].dtype)],
        compiler_params=pltpu.CompilerParams(vmem_limit_bytes=PROJECT_VMEM),
        cost_estimate=pl.CostEstimate(
            flops=rows * width,
            bytes_accessed=rows * width,
            transcendentals=0,
        ),
        name="project",
    )(*[in_vmem(weight) for weight in weights], *parts, *bases)


def swap(part, bit):
    size = lax.axis_size("tensor")
    return lax.ppermute(part, "tensor", [(i, i ^ bit) for i in range(size)])


def trade(pieces):
    devices = lax.axis_size("dp")
    rows = [[at + place for place in LISTED] for at in range(0, devices, ROW)]
    return lax.all_to_all(pieces, "dp", 0, 0, tiled=True, axis_index_groups=rows)


def onward(piece, step):
    devices = lax.axis_size("dp")
    return lax.ppermute(piece, "dp", [(i, (i + step) % devices) for i in range(devices)])


def per_device(queries, key_proj, value_proj, out_weight, parents):
    me = lax.axis_index("tensor")
    first = (lax.axis_index("dp") * 2).astype(jnp.int32).reshape(1)
    pieces = trade(pack(key_proj, value_proj)).reshape(ROW_SEGS, 2 * PIECE, HEAD_DIM)
    to_next, to_second = carry_out(first, parents, pieces)
    inside = pick(first, parents, pieces)
    far = trade(merge(*inside, onward(to_next, ROW), onward(to_second, 2 * ROW)))

    width = queries.shape[1]
    bring = (me.astype(jnp.int32).reshape(1), out_weight)
    own, across, weights, head = [], [], [], 0
    for c, (size, blocks) in enumerate([(3, ()), (3, (0, 1)), (2, (2, 3))]):
        after = [across[c - 2]] if c >= 2 else []
        part, *brought = attend(
            first, parents, queries, key_proj, value_proj, far, head, size, blocks, bring, after
        )
        weights += brought
        own.append(part)
        across.append(swap(part, 2))
        head += size
    beside = [swap(part, 1) for part in own]
    corner = [swap(part, 1) for part in across[:-1]]
    near = project(
        [own + beside, across[:-1], corner[:-1]], [(0, 0), (1, 0), (1, width)], weights, None, jnp.float32
    )
    last, near = lax.optimization_barrier((across[-1], near))
    corner.append(swap(last, 1))
    done = width - last.shape[1]
    turned = sum(part.shape[1] for part in corner[:-2])
    return project(
        [[last], corner[-2:]], [(1, done), (1, width + turned)], weights, near, jnp.bfloat16
    )


def solution(mesh):
    placed = (P("dp", "tensor"), P("dp", "tensor"), P("dp", "tensor"), P(None, "tensor"), P())
    return jax.shard_map(
        per_device, mesh=mesh, in_specs=placed, out_specs=P("dp", "tensor"), check_vma=False
    )
```
